32 devices in a mesh: seq: 16 (over z, x, core), grp: 2 (over y).
Axes of the slice: x: 2, y: 2, z: 4, core: 2. Of those that a mesh axis runs over, the one named last changes fastest.
Arguments:
- tokens: bfloat16 [2, 4096, 768], P('grp', 'seq'), may hold values from -6 to 6
- lengths: int32 [2, 6], P('grp'), may hold values from 176 to 3136, as said below
- image_ids: int32 [2, 6], P('grp'), may hold values from 0 to 5, as said below
- ln_gain: float32 [768], replicated, may hold values from 0.5 to 1.5
- w_qkv: bfloat16 [768, 2304], replicated, may hold values from -0.21875 to 0.21875
- q_gain: float32 [64], replicated, may hold values from 0.5 to 1.5
- k_gain: float32 [64], replicated, may hold values from 0.5 to 1.5
- w_attn_out: bfloat16 [768, 768], replicated, may hold values from -6 to 6
- w_in: bfloat16 [768, 3072], replicated, may hold values from -0.21875 to 0.21875
- b_in: float32 [3072], replicated, may hold values from -3 to 3
- w_mlp_out: bfloat16 [3072, 768], replicated, may hold values from -0.109375 to 0.109375
- b_out: float32 [768], replicated, may hold values from -3 to 3
- cotangent: bfloat16 [2, 4096, 768], P('grp', 'seq'), may hold values from -6 to 6
Outputs:
- output: bfloat16 [2, 4096, 768], P('grp', 'seq')
- grad_tokens: float32 [2, 4096, 768], P('grp', 'seq')
- grad_ln_gain: float32 [768], P('grp')
- grad_w_qkv: float32 [768, 2304], P('grp')
- grad_q_gain: float32 [64], P('grp')
- grad_k_gain: float32 [64], P('grp')
- grad_w_attn_out: float32 [768, 768], P('grp')
- grad_w_in: float32 [768, 3072], P('grp')
- grad_b_in: float32 [3072], P('grp')
- grad_w_mlp_out: float32 [3072, 768], P('grp')
- grad_b_out: float32 [768], P('grp')
The draws below stay inside these ranges and needn't reach their ends.
Inputs may be any that keep to these rules, and one draw needn't show every extreme that they name: `lengths`: each row gives the tokens of image ids 0 to 5 and sums to 4096: 1 images of 3136 tokens, 4 of 196 tokens, and one image of the tokens that remain. `image_ids`: each row is an order of the ids 0 to 5, each once.
All inputs are finite; a program needn't handle non-finite values.
Results may differ from the reference program's by a relative error of at most 0.012.
Values may be sent and summed in bfloat16 or wider, within the bound.
No kernel may reach another device: no remote copies, remote signals or barrier semaphores. Data moves between devices by JAX's collectives and lax.ppermute only.
A program may use at most 128 MiB of HBM per device.

```python
import math
import jax
import jax.numpy as jnp
from jax import lax

D = 768
H = 12
HD = 64
FF = 3072
BIG_LEN = 3136
SMALL_LEN = 196
GROUP_TOK = 4096
BIG_IMAGES = 1
SMALL_IMAGES = 4
IMAGES = 6
N_GRP = 2


def pack_plan(key):
    leftover = GROUP_TOK - BIG_IMAGES * BIG_LEN - SMALL_IMAGES * SMALL_LEN
    by_slot = jnp.concatenate([jnp.full((BIG_IMAGES,), BIG_LEN, jnp.int32), jnp.full((SMALL_IMAGES,), SMALL_LEN, jnp.int32), jnp.full((1,), leftover, jnp.int32)]).astype(jnp.int32)

    def one_pack(index):
        sub_key = jax.random.fold_in(key, index)
        order = jax.random.permutation(jax.random.fold_in(sub_key, 12), IMAGES).astype(jnp.int32)
        by_label = by_slot[jnp.argsort(order, stable=True)]
        return (by_label.astype(jnp.int32), order)
    return jax.vmap(one_pack)(jnp.arange(N_GRP, dtype=jnp.int32))


def draw_lengths(key, part):
    by_label, order = pack_plan(key)
    return by_label


def draw_image_ids(key, part):
    by_label, order = pack_plan(key)
    return order


def level_of(own_key, dims, cuts, least, largest):
    level, own = 1.0, jax.random.fold_in(own_key, 6)
    for dim, shards_of in cuts:
        steps = jnp.exp(jax.random.uniform(jax.random.fold_in(own, dim), (shards_of,), jnp.float32, least / len(cuts), largest / len(cuts)))
        level = level * jnp.repeat(steps, dims[dim] // shards_of).reshape([-1 if axis == dim else 1 for axis in range(len(dims))])
    return level


def bell_draw(own_key, extent, scale, limit, cuts=(), kind=jnp.bfloat16):
    values = scale * jax.random.normal(own_key, extent, jnp.float32)
    if cuts:
        values = values * level_of(own_key, extent, cuts, -0.22, 0.18)
    return jnp.clip(values, -limit, limit).astype(kind)


def setup_inputs(seed: int = 0) -> dict:
    streams_of = jax.random.split(jax.random.key(seed), 14)
    tokens = bell_draw(streams_of[0], (N_GRP, GROUP_TOK, D), 1.0, 6.0, ((0, 2), (1, 16)))
    lengths = draw_lengths(jax.random.fold_in(streams_of[13], 71), 0)
    image_ids = draw_image_ids(jax.random.fold_in(streams_of[13], 71), 0)
    ln_gain = jnp.clip(1.0 + 0.1 * jax.random.normal(streams_of[3], (D,), jnp.float32), 0.5, 1.5)
    w_qkv = bell_draw(streams_of[4], (D, 3 * D), D ** -0.5, 0.21875)
    q_gain = jnp.clip(1.0 + 0.1 * jax.random.normal(streams_of[5], (HD,), jnp.float32), 0.5, 1.5)
    k_gain = jnp.clip(1.0 + 0.1 * jax.random.normal(streams_of[6], (HD,), jnp.float32), 0.5, 1.5)
    w_attn_out = bell_draw(streams_of[7], (D, D), ((BIG_LEN * SMALL_LEN) ** 0.25 / (2 * D ** 0.5)), 6.0)
    w_in = bell_draw(streams_of[8], (D, FF), D ** -0.5, 0.21875)
    b_in = bell_draw(streams_of[9], (FF,), 0.5, 3.0, (), jnp.float32)
    w_mlp_out = bell_draw(streams_of[10], (FF, D), FF ** -0.5, 0.109375)
    b_out = bell_draw(streams_of[11], (D,), 0.5, 3.0, (), jnp.float32)
    cotangent = bell_draw(streams_of[12], (N_GRP, GROUP_TOK, D), 1.0, 6.0, ((0, 2), (1, 16)))
    return {"tokens": tokens, "lengths": lengths, "image_ids": image_ids, "ln_gain": ln_gain, "w_qkv": w_qkv, "q_gain": q_gain, "k_gain": k_gain, "w_attn_out": w_attn_out, "w_in": w_in, "b_in": b_in, "w_mlp_out": w_mlp_out, "b_out": b_out, "cotangent": cotangent}


@jax.custom_vjp
def low(v):
    return lax.optimization_barrier(v.astype(jnp.bfloat16)).astype(jnp.float32)

@jax.custom_vjp
def low_back(v):
    return v

def low_keep(v):
    return (low(v), None)

def low_pass(kept, grad):
    return (grad,)

def back_keep(v):
    return (v, None)

def back_low(kept, grad):
    return (low(grad),)
low.defvjp(low_keep, low_pass)
low_back.defvjp(back_keep, back_low)
EPSILON = 1e-06
MASKED = -1e+30

def dense(left_side, right_side):
    return jnp.dot(left_side, right_side, precision=lax.Precision.HIGHEST)

def norm_rows(values, gain_vec):
    row_mean = lax.optimization_barrier(jnp.mean(values, axis=-1, keepdims=True))
    centred = values - row_mean
    spread = lax.optimization_barrier(jnp.mean(centred * centred, axis=-1, keepdims=True))
    return centred * lax.rsqrt(spread + EPSILON) * gain_vec

def image_index(length_row, order_row):
    ordered = jnp.take(length_row, order_row).astype(jnp.int32)
    image_ends = jnp.cumsum(ordered).astype(jnp.int32)
    places = jnp.arange(GROUP_TOK, dtype=jnp.int32)
    return lax.optimization_barrier(jnp.sum((places[:, None] >= image_ends[None, :]).astype(jnp.int32), axis=1)).astype(jnp.int32)

def attend(queries, key_rows, values, images):
    block_rows = math.gcd(GROUP_TOK, 512)
    count = GROUP_TOK // block_rows
    query_parts = queries.reshape(count, block_rows, H, HD)
    image_parts = images.reshape(count, block_rows)

    def attend_block(pieces):
        query_part, image_part = pieces
        scores = jnp.einsum('qhd,khd->hqk', query_part, key_rows, precision=lax.Precision.HIGHEST)
        scores = low_back(scores)
        same_image = image_part[None, :, None] == images[None, None, :]
        scores = jnp.where(same_image, scores, MASKED)
        running_max = lax.optimization_barrier(jnp.max(scores, axis=-1, keepdims=True))
        weights = jnp.exp(scores - running_max)
        weights = weights / lax.optimization_barrier(jnp.sum(weights, axis=-1, keepdims=True))
        return jnp.einsum('hqk,khd->qhd', low(weights), values, precision=lax.Precision.HIGHEST)
    attended = lax.map(jax.checkpoint(attend_block), (query_parts, image_parts))
    return attended.reshape(GROUP_TOK, H * HD)

def layer(inputs, ln_gain, w_qkv, q_gain, k_gain, w_attn_out, w_in, b_in, w_mlp_out, b_out, images_all):
    normed = low(norm_rows(inputs, ln_gain))
    projected = low_back(dense(normed, w_qkv))
    shape = (N_GRP, GROUP_TOK, H, HD)
    query_raw = projected[..., :D].reshape(shape)
    key_raw = projected[..., D:2 * D].reshape(shape)
    value_raw = projected[..., 2 * D:].reshape(shape)
    queries = low(norm_rows(query_raw, q_gain) * HD ** (-0.5))
    key_rows = low(norm_rows(key_raw, k_gain))
    values = low(value_raw)
    attended = jnp.stack([attend(queries[g], key_rows[g], values[g], images_all[g]) for g in range(N_GRP)])
    attended = low_back(low(attended))
    branch_attn = dense(attended, w_attn_out)
    pre_act = low_back(dense(normed, w_in) + b_in)
    hidden = low(jax.nn.gelu(pre_act, approximate=True))
    branch_mlp = dense(hidden, w_mlp_out) + b_out
    return inputs + branch_attn + branch_mlp

def reference(tokens, lengths, image_ids, ln_gain, w_qkv, q_gain, k_gain, w_attn_out, w_in, b_in, w_mlp_out, b_out, cotangent):
    images_all = jnp.stack([image_index(lengths[g], image_ids[g]) for g in range(N_GRP)])
    params = (tokens.astype(jnp.float32), ln_gain.astype(jnp.float32), w_qkv.astype(jnp.float32), q_gain.astype(jnp.float32), k_gain.astype(jnp.float32), w_attn_out.astype(jnp.float32), w_in.astype(jnp.float32), b_in.astype(jnp.float32), w_mlp_out.astype(jnp.float32), b_out.astype(jnp.float32))

    def forward(*pieces):
        return layer(*pieces, images_all)
    output, pull = jax.vjp(forward, *params)
    grads = pull(cotangent.astype(jnp.float32))
    return (output.astype(jnp.bfloat16), grads[0], grads[1], grads[2], grads[3], grads[4], grads[5], grads[6], grads[7], grads[8], grads[9])
```

```python
import functools

import jax
import jax.numpy as jnp
from jax import lax
from jax.experimental import pallas as pl
from jax.experimental.pallas import tpu as pltpu
from jax.sharding import PartitionSpec as P

H = 12
HD = 64
Z_COUNT = 4
PER_Z = H // Z_COUNT
EPSILON = 1e-06
BF = jnp.bfloat16
F32 = jnp.float32
VMEM_BYTES = 58 * 1024 * 1024


def params():
    return pltpu.CompilerParams(vmem_limit_bytes=VMEM_BYTES)


def dot_nn(left, right):
    return lax.dot_general(left, right, (((1,), (0,)), ((), ())), preferred_element_type=F32)


def dot_nt(left, right):
    return lax.dot_general(left, right, (((1,), (1,)), ((), ())), preferred_element_type=F32)


def dot_tn(left, right):
    return lax.dot_general(left, right, (((0,), (0,)), ((), ())), preferred_element_type=F32)


def whole(shape):
    return pl.BlockSpec(shape, lambda *_: (0,) * len(shape))


def normalized(values, axis):
    mean = jnp.mean(values, axis=axis, keepdims=True)
    centred = values - mean
    spread = jnp.mean(centred * centred, axis=axis, keepdims=True)
    scale = lax.rsqrt(spread + EPSILON)
    return centred * scale, scale


def mlp_kernel(
    core_ref, x_ref, dy_ref, gain_ref, w_in_ref, b_in_ref, w_out_ref,
    out_ref, ngrad_ref, gw_in_ref, gw_out_ref, gb_in_ref, gb_out_ref,
    normed_s, normed_t_s, out_s, ngrad_s,
):
    step = pl.program_id(0)

    @pl.when(step == 0)
    def _():
        hat, _unused = normalized(x_ref[...].astype(F32), 1)
        normed = (hat * gain_ref[...]).astype(BF)
        normed_s[...] = normed
        normed_t_s[...] = jnp.transpose(normed)
        out_s[...] = jnp.zeros_like(out_s)
        ngrad_s[...] = jnp.zeros_like(ngrad_s)
        rows = dy_ref.shape[0] // 2
        gb_out_ref[...] = jnp.sum(dy_ref[:rows, :].astype(F32), axis=0, keepdims=True)

    pre = dot_nn(normed_s[...], w_in_ref[...]) + b_in_ref[...]
    cube = 0.7978845608028654 * (pre + 0.044715 * pre * pre * pre)
    tanh = jnp.tanh(cube)
    half = 0.5 * (1.0 + tanh)
    hidden = (pre * half).astype(BF)
    slope = half + 0.5 * pre * (1.0 - tanh * tanh) * (
        0.7978845608028654 * (1.0 + 3.0 * 0.044715 * pre * pre)
    )
    out_s[...] += dot_nn(hidden, w_out_ref[...])
    grad_hidden = dot_nt(dy_ref[...], w_out_ref[...])
    grad_pre = (slope * grad_hidden).astype(BF)
    gb_in_ref[...] = jnp.sum(grad_pre.astype(F32), axis=0, keepdims=True)
    ngrad_s[...] += dot_nt(grad_pre, w_in_ref[...])
    gw_in_ref[...] = dot_nn(normed_t_s[...], grad_pre).astype(BF)
    gw_out_ref[...] = dot_nn(jnp.transpose(hidden), dy_ref[...]).astype(BF)

    @pl.when(step == pl.num_programs(0) - 1)
    def _():
        out_ref[...] = out_s[...].astype(BF)
        ngrad_ref[...] = ngrad_s[...].astype(BF)


def mlp(core, x_pair, dy_pair, ln_gain, w_in, b_in, w_out):
    tokens, width = x_pair.shape
    hidden = w_in.shape[1]
    tile = 256
    part = hidden // 4 // tile

    def place(step, core_ref):
        return (step // part) * 2 * part + core_ref[0] * part + step % part

    grid_spec = pltpu.PrefetchScalarGridSpec(
        num_scalar_prefetch=1,
        grid=(2 * part,),
        in_specs=[
            whole((tokens, width)),
            whole((tokens, width)),
            whole((1, width)),
            pl.BlockSpec((width, tile), lambda s, c: (0, place(s, c))),
            pl.BlockSpec((1, tile), lambda s, c: (0, place(s, c))),
            pl.BlockSpec((tile, width), lambda s, c: (place(s, c), 0)),
        ],
        out_specs=[
            whole((tokens, width)),
            whole((tokens, width)),
            pl.BlockSpec((width, tile), lambda s, c: (0, s)),
            pl.BlockSpec((tile, width), lambda s, c: (s, 0)),
            pl.BlockSpec((1, tile), lambda s, c: (0, s)),
            whole((1, width)),
        ],
        scratch_shapes=[
            pltpu.VMEM((tokens, width), BF),
            pltpu.VMEM((width, tokens), BF),
            pltpu.VMEM((tokens, width), F32),
            pltpu.VMEM((tokens, width), F32),
        ],
    )
    return pl.pallas_call(
        mlp_kernel,
        grid_spec=grid_spec,
        out_shape=[
            jax.ShapeDtypeStruct((tokens, width), BF),
            jax.ShapeDtypeStruct((tokens, width), BF),
            jax.ShapeDtypeStruct((width, hidden // 2), BF),
            jax.ShapeDtypeStruct((hidden // 2, width), BF),
            jax.ShapeDtypeStruct((1, hidden // 2), F32),
            jax.ShapeDtypeStruct((1, width), F32),
        ],
        compiler_params=params(),
        name="mlp",
    )(core, x_pair, dy_pair, ln_gain, w_in, b_in, w_out)


def qkv_kernel(x_ref, gain_ref, w_ref, q_gain_ref, k_gain_ref, normed_ref, q_ref, kv_ref, raw_ref):
    hat, _unused = normalized(x_ref[...].astype(F32), 1)
    normed = (hat * gain_ref[...]).astype(BF)
    normed_ref[...] = normed
    projected = dot_nt(w_ref[0], normed)
    zeros = jnp.zeros((HD, normed.shape[0]), F32)
    for head in range(PER_Z):
        rows = projected[head * 3 * HD : (head + 1) * 3 * HD]
        raw_ref[head] = rows[: 2 * HD]
        q_hat, _unused = normalized(rows[:HD], 0)
        k_hat, _unused = normalized(rows[HD : 2 * HD], 0)
        q = q_hat * q_gain_ref[...] * HD ** (-0.5)
        k = k_hat * k_gain_ref[...]
        q_ref[head] = jnp.transpose(jnp.concatenate([q, zeros], axis=0)).astype(BF)
        kv_ref[head] = jnp.transpose(jnp.concatenate([k, rows[2 * HD :]], axis=0)).astype(BF)


def qkv(z_index, x, ln_gain, w_all, q_gain, k_gain):
    tokens, width = x.shape
    body = lambda z_ref, *refs: qkv_kernel(*refs)
    grid_spec = pltpu.PrefetchScalarGridSpec(
        num_scalar_prefetch=1,
        grid=(1,),
        in_specs=[
            whole((tokens, width)),
            whole((1, width)),
            pl.BlockSpec((1, 3 * PER_Z * HD, width), lambda s, z: (z[0], 0, 0)),
            whole((HD, 1)),
            whole((HD, 1)),
        ],
        out_specs=[
            whole((tokens, width)),
            whole((PER_Z, tokens, 2 * HD)),
            whole((PER_Z, tokens, 2 * HD)),
            whole((PER_Z, 2 * HD, tokens)),
        ],
    )
    return pl.pallas_call(
        body,
        grid_spec=grid_spec,
        out_shape=[
            jax.ShapeDtypeStruct((tokens, width), BF),
            jax.ShapeDtypeStruct((PER_Z, tokens, 2 * HD), BF),
            jax.ShapeDtypeStruct((PER_Z, tokens, 2 * HD), BF),
            jax.ShapeDtypeStruct((PER_Z, 2 * HD, tokens), F32),
        ],
        compiler_params=params(),
        name="qkv",
    )(z_index, x, ln_gain, w_all, q_gain, k_gain)


def attention_kernel(sources, slots, tokens, *refs):
    q_refs, refs = refs[:slots], refs[slots:]
    do_refs, refs = refs[:slots], refs[slots:]
    kv_refs, refs = refs[: sources * slots], refs[sources * slots :]
    qi_ref, ki_ref, out_ref, dq_ref, dkv_ref, q_s, do_s, kv_s, one_v_s, e_s, acc_s = refs
    rows = slots * tokens
    lane = lax.broadcasted_iota(jnp.int32, (tokens, 2 * HD), 1)
    for slot in range(slots):
        span = pl.ds(slot * tokens, tokens)
        q_s[span, :] = q_refs[slot][0]
        grad = do_refs[slot][0].astype(F32)
        do_s[span, :] = jnp.transpose(jnp.concatenate([jnp.zeros_like(grad), grad], axis=0))
        for source in range(sources):
            block = kv_refs[source * slots + slot][0]
            kv_s[source, span, :] = block
            one_v_s[source, span, :] = jnp.where(lane < HD, jnp.ones((), BF), block)
    acc_s[...] = jnp.zeros_like(acc_s)

    def forward(source, carry):
        scores = dot_nt(q_s[...], kv_s[source])
        same = qi_ref[...] == ki_ref[source]
        weights = jnp.where(same, jnp.exp(scores), 0.0).astype(BF)
        e_s[source] = weights
        acc_s[...] += dot_nn(weights, one_v_s[source])
        return carry

    lax.fori_loop(0, sources, forward, 0)
    acc = acc_s[...]
    wide = lax.broadcasted_iota(jnp.int32, (rows, 2 * HD), 1)
    attended = jnp.where(wide >= HD, acc / pltpu.roll(acc, HD, 1), 0.0)
    inverse = 1.0 / acc[:, 0:1]
    do = do_s[...]
    out_dot = jnp.sum(do * attended, axis=1, keepdims=True) * inverse
    coarse = out_dot.astype(BF).astype(F32)
    do = do * inverse
    probe = jnp.where(wide == 0, -coarse, jnp.where(wide == 1, coarse - out_dot, do)).astype(BF)
    do_s[...] = do
    out_ref[...] = jnp.transpose(attended)[HD:].astype(BF)
    q_t = jnp.transpose(q_s[...].astype(F32))[:HD].astype(BF)
    do_t = jnp.transpose(do)[HD:].astype(BF)
    acc_s[...] = jnp.zeros_like(acc_s)

    def backward(source, carry):
        weights = e_s[source]
        grad_weights = dot_nt(probe, one_v_s[source])
        grad_scores = (weights.astype(F32) * grad_weights).astype(BF)
        acc_s[...] += dot_nn(grad_scores, kv_s[source])
        dkv_ref[source, :HD, :] = dot_nn(q_t, grad_scores).astype(BF)
        dkv_ref[source, HD:, :] = dot_nn(do_t, weights).astype(BF)
        return carry

    lax.fori_loop(0, sources, backward, 0)
    dq_ref[...] = jnp.transpose(acc_s[...])[:HD]


def attention(head, q_slots, do_slots, kv_sources, query_images, key_images):
    slots, sources = len(q_slots), len(kv_sources)
    tokens = q_slots[0].shape[1]
    rows = slots * tokens
    part = pl.BlockSpec((1, tokens, 2 * HD), lambda i: (head, 0, 0))
    do_part = pl.BlockSpec((1, HD, tokens), lambda i: (head, 0, 0))
    return pl.pallas_call(
        functools.partial(attention_kernel, sources, slots, tokens),
        grid=(1,),
        in_specs=[part] * slots
        + [do_part] * slots
        + [part] * (sources * slots)
        + [whole((rows, 1)), whole((sources, 1, rows))],
        out_specs=[whole((HD, rows)), whole((HD, rows)), whole((sources, 2 * HD, rows))],
        out_shape=[
            jax.ShapeDtypeStruct((HD, rows), BF),
            jax.ShapeDtypeStruct((HD, rows), F32),
            jax.ShapeDtypeStruct((sources, 2 * HD, rows), BF),
        ],
        scratch_shapes=[
            pltpu.VMEM((rows, 2 * HD), BF),
            pltpu.VMEM((rows, 2 * HD), F32),
            pltpu.VMEM((sources, rows, 2 * HD), BF),
            pltpu.VMEM((sources, rows, 2 * HD), BF),
            pltpu.VMEM((sources, rows, rows), BF),
            pltpu.VMEM((rows, 2 * HD), F32),
        ],
        compiler_params=params(),
        name="attention",
    )(*q_slots, *do_slots, *[kv for source in kv_sources for kv in source], query_images, key_images)


def post_kernel(slots, tokens, *refs):
    dq_ref, own_ref, came_ref = refs[:3]
    raw_refs = refs[3 : 3 + slots]
    normed_refs = refs[3 + slots : 3 + 2 * slots]
    q_gain_ref, k_gain_ref, grad_ref, weight_ref, gain_ref = refs[3 + 2 * slots :]
    total = None
    gains = [0.0, 0.0]
    for slot in range(slots):
        span = slice(slot * tokens, (slot + 1) * tokens)
        dkv = own_ref[:, span].astype(F32) + came_ref[:, span].astype(F32)
        grads = []
        for which, (grad, gain) in enumerate(
            ((dq_ref[:, span], q_gain_ref[...] * HD ** (-0.5)), (dkv[:HD], k_gain_ref[...]))
        ):
            hat, scale = normalized(raw_refs[slot][0, which * HD : (which + 1) * HD, :], 0)
            factor = HD ** (-0.5) if which == 0 else 1.0
            gains[which] += jnp.sum(grad * hat, axis=1, keepdims=True) * factor
            grad = grad * gain
            grad = scale * (
                grad
                - jnp.mean(grad, axis=0, keepdims=True)
                - hat * jnp.mean(grad * hat, axis=0, keepdims=True)
            )
            grads.append(grad)
        grads.append(dkv[HD:])
        projected_grad = jnp.concatenate(grads, axis=0).astype(BF)
        grad_ref[slot] = projected_grad
        term = dot_nn(projected_grad, normed_refs[slot][...])
        total = term if total is None else total + term
    half = total.shape[1] // 2
    weight_ref[0] = total[:, :half].astype(BF)
    weight_ref[1] = total[:, half:].astype(BF)
    gain_ref[0] = jnp.broadcast_to(gains[0], (HD, 128))
    gain_ref[1] = jnp.broadcast_to(gains[1], (HD, 128))


def post(head, dq, dkv_own, dkv_came, raw_slots, normed_slots, q_gain, k_gain):
    slots = len(raw_slots)
    tokens, width = normed_slots[0].shape
    rows = slots * tokens
    return pl.pallas_call(
        functools.partial(post_kernel, slots, tokens),
        grid=(1,),
        in_specs=[whole((HD, rows)), whole((2 * HD, rows)), whole((2 * HD, rows))]
        + [pl.BlockSpec((1, 2 * HD, tokens), lambda i: (head, 0, 0))] * slots
        + [whole((tokens, width))] * slots
        + [whole((HD, 1))] * 2,
        out_specs=[
            whole((slots, 3 * HD, tokens)),
            whole((2, 3 * HD, width // 2)),
            whole((2, HD, 128)),
        ],
        out_shape=[
            jax.ShapeDtypeStruct((slots, 3 * HD, tokens), BF),
            jax.ShapeDtypeStruct((2, 3 * HD, width // 2), BF),
            jax.ShapeDtypeStruct((2, HD, 128), F32),
        ],
        compiler_params=params(),
        name="post",
    )(dq, dkv_own, dkv_came, *raw_slots, *normed_slots, q_gain, k_gain)


def output_kernel(
    z_ref, *refs
):
    (*att_refs, x_ref, dy_ref, own_ref, came_ref, b_ref, w_ref, out_ref, gw_ref, acc_s) = refs
    step = pl.program_id(0)

    @pl.when(step == 0)
    def _():
        acc_s[...] = (
            x_ref[...].astype(F32)
            + own_ref[...].astype(F32)
            + came_ref[...].astype(F32)
            + b_ref[...]
        )

    for slot, att_ref in enumerate(att_refs):

        @pl.when(step == slot)
        def _():
            att = att_ref[...]
            acc_s[...] += dot_tn(att, w_ref[...])
            gw_ref[0] = dot_nn(att, dy_ref[...]).astype(BF)

    @pl.when(step == pl.num_programs(0) - 1)
    def _():
        out_ref[...] = acc_s[...].astype(BF)


def block_output(z_index, att_slots, x, dy, mlp_own, mlp_came, b_out, w_attn_out):
    tokens, width = x.shape
    depth = PER_Z * HD

    def place(step, z_ref):
        return lax.rem(z_ref[0] + step, Z_COUNT)

    grid_spec = pltpu.PrefetchScalarGridSpec(
        num_scalar_prefetch=1,
        grid=(Z_COUNT,),
        in_specs=[whole((depth, tokens))] * Z_COUNT
        + [whole((tokens, width))] * 4
        + [whole((1, width)), pl.BlockSpec((depth, width), lambda s, z: (place(s, z), 0))],
        out_specs=[
            whole((tokens, width)),
            pl.BlockSpec((1, depth, width), lambda s, z: (place(s, z), 0, 0)),
        ],
        scratch_shapes=[pltpu.VMEM((tokens, width), F32)],
    )
    return pl.pallas_call(
        output_kernel,
        grid_spec=grid_spec,
        out_shape=[
            jax.ShapeDtypeStruct((tokens, width), BF),
            jax.ShapeDtypeStruct((Z_COUNT, depth, width), BF),
        ],
        compiler_params=params(),
        name="block_output",
    )(z_index, *att_slots, x, dy, mlp_own, mlp_came, b_out, w_attn_out)


def tokens_kernel(z_ref, *refs):
    (*grad_refs, x_ref, dy_ref, gain_ref, own_ref, came_ref, w_ref, out_ref, gg_ref, acc_s) = refs
    step = pl.program_id(0)

    @pl.when(step == 0)
    def _():
        acc_s[...] = own_ref[...].astype(F32) + came_ref[...].astype(F32)

    for slot in range(Z_COUNT):

        @pl.when(step == slot)
        def _():
            grads = jnp.concatenate(
                [grad_refs[head * Z_COUNT + slot][...] for head in range(PER_Z)], axis=0
            )
            acc_s[...] += dot_tn(grads, w_ref[0])

    @pl.when(step == pl.num_programs(0) - 1)
    def _():
        hat, scale = normalized(x_ref[...].astype(F32), 1)
        normed_grad = acc_s[...]
        gg_ref[...] = jnp.sum(normed_grad * hat, axis=0, keepdims=True)
        grad = normed_grad * gain_ref[...]
        out_ref[...] = dy_ref[...].astype(F32) + scale * (
            grad
            - jnp.mean(grad, axis=1, keepdims=True)
            - hat * jnp.mean(grad * hat, axis=1, keepdims=True)
        )


def token_gradient(z_index, grad_pieces, x, dy, ln_gain, mlp_own, mlp_came, w_all):
    tokens, width = x.shape
    depth = 3 * PER_Z * HD
    grid_spec = pltpu.PrefetchScalarGridSpec(
        num_scalar_prefetch=1,
        grid=(Z_COUNT,),
        in_specs=[whole((3 * HD, tokens))] * (PER_Z * Z_COUNT)
        + [whole((tokens, width))] * 2
        + [whole((1, width))]
        + [whole((tokens, width))] * 2
        + [pl.BlockSpec((1, depth, width), lambda s, z: (lax.rem(z[0] + s, Z_COUNT), 0, 0))],
        out_specs=[whole((tokens, width)), whole((1, width))],
        scratch_shapes=[pltpu.VMEM((tokens, width), F32)],
    )
    return pl.pallas_call(
        tokens_kernel,
        grid_spec=grid_spec,
        out_shape=[
            jax.ShapeDtypeStruct((tokens, width), F32),
            jax.ShapeDtypeStruct((1, width), F32),
        ],
        compiler_params=params(),
        name="token_gradient",
    )(z_index, *grad_pieces, x, dy, ln_gain, mlp_own, mlp_came, w_all)


def exchange_half(rows, bit, send):
    half = rows.shape[0] // 2
    gone = lax.dynamic_slice_in_dim(rows, (1 - bit) * half, half, 0)
    kept = lax.dynamic_slice_in_dim(rows, bit * half, half, 0)
    came = send(gone)
    return (kept.astype(F32) + came.astype(F32)).astype(BF)


def gather_doubling(piece, sends):
    pieces = piece[None]
    for send in sends:
        pieces = jnp.concatenate([pieces, send(pieces)], axis=0)
    return pieces


def place_kernel(index_ref, piece_ref, out_ref):
    out_ref[...] = piece_ref[...].astype(F32)


def place(pieces, index):
    count = pieces.shape[0]
    block = (1,) + pieces.shape[1:]
    rest = (0,) * (pieces.ndim - 1)
    grid_spec = pltpu.PrefetchScalarGridSpec(
        num_scalar_prefetch=1,
        grid=(count,),
        in_specs=[pl.BlockSpec(block, lambda s, i: (jnp.bitwise_xor(s, i[0]),) + rest)],
        out_specs=pl.BlockSpec(block, lambda s, i: (s,) + rest),
    )
    return pl.pallas_call(
        place_kernel,
        grid_spec=grid_spec,
        out_shape=jax.ShapeDtypeStruct(pieces.shape, F32),
        compiler_params=params(),
        name="place",
    )(index.reshape(1), pieces)


def per_device(
    tokens, lengths, image_ids, ln_gain, w_qkv, q_gain, k_gain,
    w_attn_out, w_in, b_in, w_mlp_out, b_out, cotangent,
):
    x, dy = tokens[0], cotangent[0]
    rows, width = x.shape
    hidden = w_in.shape[1]
    seq_count = lax.axis_size("seq")
    rest = seq_count // Z_COUNT
    rest_bits = rest.bit_length() - 1
    me = lax.axis_index("seq")
    z_index, r_index = me // rest, me % rest
    grp = lax.axis_index("grp")
    core = r_index % 2

    def z_shift(block, distance):
        route = [(i, (i + distance * rest) % seq_count) for i in range(seq_count)]
        return lax.ppermute(block, "seq", route)

    def flip(mask):
        route = [(i, i ^ mask) for i in range(seq_count)]
        return lambda block: lax.ppermute(block, "seq", route)

    def swap_packs(block):
        return lax.ppermute(block, "grp", [(0, 1), (1, 0)])

    swap_core = flip(1)

    order = image_ids[0]
    labels = jnp.arange(order.shape[0], dtype=jnp.int32)
    ordered = jnp.sum(jnp.where(order[:, None] == labels[None, :], lengths[0][None, :], 0), axis=1)
    ends = jnp.cumsum(ordered)
    offsets = jnp.arange(rows, dtype=jnp.int32)
    slot_z = (z_index - jnp.arange(Z_COUNT, dtype=jnp.int32)) % Z_COUNT
    source_masks = [0]
    for bit in reversed(range(rest_bits)):
        source_masks = source_masks + [m | (1 << bit) for m in source_masks]
    source_r = r_index ^ jnp.array(source_masks, dtype=jnp.int32)
    starts = (slot_z[None, :] * rest + source_r[:, None]) * rows
    places = (starts[:, :, None] + offsets).reshape(rest, Z_COUNT * rows)
    images = jnp.sum((places[:, :, None] >= ends).astype(jnp.int32), axis=2)
    key_images = images[:, None, :]
    query_images = images[0][:, None]

    ln_row = ln_gain.reshape(1, width)
    z_scalar = z_index.astype(jnp.int32).reshape(1)
    core_scalar = core.astype(jnp.int32).reshape(1)
    q_col, k_col = q_gain.reshape(HD, 1), k_gain.reshape(HD, 1)
    w_all = (
        w_qkv.reshape(width, 3, Z_COUNT, PER_Z, HD)
        .transpose(2, 3, 1, 4, 0)
        .reshape(Z_COUNT, 3 * PER_Z * HD, width)
    )

    x_slots = [x] + [z_shift(x, d) for d in range(1, Z_COUNT)]
    x_came, dy_came = swap_core(x), swap_core(dy)
    do_t = dot_nt(w_attn_out, dy).astype(BF).reshape(Z_COUNT, PER_Z, HD, rows)
    do_slots = [lax.dynamic_index_in_dim(do_t, z_index, 0, keepdims=False)]
    for d in range(1, Z_COUNT):
        gone = lax.dynamic_index_in_dim(do_t, (z_index + d) % Z_COUNT, 0, keepdims=False)
        do_slots.append(z_shift(gone, d))

    x_pair = jnp.concatenate([x, x_came], axis=0)
    dy_pair = jnp.concatenate([dy, dy_came], axis=0)
    mlp_out, mlp_ngrad, gw_in, gw_out, gb_in, gb_out = mlp(
        core_scalar, x_pair, dy_pair, ln_row, w_in, b_in.reshape(1, hidden), w_mlp_out
    )
    out_came = swap_core(mlp_out[rows:])
    ngrad_came = swap_core(mlp_ngrad[rows:])

    normed_slots, q_slots, kv_slots, raw_slots = [], [], [], []
    for slot in range(Z_COUNT):
        normed, q, kv, raw = qkv(z_scalar, x_slots[slot], ln_row, w_all, q_col, k_col)
        normed_slots.append(normed)
        q_slots.append(q)
        raw_slots.append(raw)
        gathered = [kv]
        for bit in reversed(range(rest_bits)):
            gathered = gathered + [flip(1 << bit)(block) for block in gathered]
        kv_slots.append(gathered)
    kv_sources = [[kv_slots[slot][s] for slot in range(Z_COUNT)] for s in range(rest)]

    upper_bits = list(reversed(range(1, rest_bits)))
    share_index = r_index >> 1
    share_index = share_index * Z_COUNT + z_index
    halvings = [((r_index >> bit) & 1, flip(1 << bit)) for bit in upper_bits]
    halvings += [((z_index >> 1) & 1, flip(2 * rest)), (z_index & 1, flip(rest))]
    doublings = [flip(rest), flip(2 * rest)] + [flip(1 << bit) for bit in reversed(upper_bits)]

    def reduce_rows(grad):
        grad = exchange_half(grad, grp, swap_packs)
        for bit, send in halvings:
            grad = exchange_half(grad, bit, send)
        return grad

    gw_in_share = reduce_rows(gw_in)
    gw_out_share = reduce_rows(gw_out)
    gw_in_all = gather_doubling(gw_in_share, doublings)
    gw_out_all = gather_doubling(gw_out_share, doublings)
    gw_in_came, gw_out_came = swap_core(gw_in_all), swap_core(gw_out_all)

    att, grad_pieces, qkv_weights, gain_sums = [], [], [], 0.0
    for head in range(PER_Z):
        out_t, dq_t, dkv_t = attention(
            head, q_slots, do_slots, kv_sources, query_images, key_images
        )
        att.append(out_t)
        parts = {mask: dkv_t[i] for i, mask in enumerate(source_masks)}
        for bit in range(rest_bits):
            for mask in sorted(m for m in parts if m >> bit & 1):
                came = flip(1 << bit)(parts.pop(mask))
                if bit < rest_bits - 1:
                    kept = parts[mask ^ (1 << bit)]
                    parts[mask ^ (1 << bit)] = (kept.astype(F32) + came.astype(F32)).astype(BF)
        grads, weight, gain_sum = post(
            head, dq_t, parts[0], came, raw_slots, normed_slots, q_col, k_col
        )
        qkv_weights.append(weight)
        gain_sums = gain_sums + gain_sum[:, :, 0]
        grad_pieces += [grads[0]] + [z_shift(grads[d], -d) for d in range(1, Z_COUNT)]

    att_t = jnp.concatenate(att, axis=0)
    att_slots = [att_t[:, :rows]]
    for d in range(1, Z_COUNT):
        att_slots.append(z_shift(att_t[:, d * rows : (d + 1) * rows], -d))
    result, gw_attn = block_output(
        z_scalar, att_slots, x, dy, mlp_out[:rows], out_came, b_out.reshape(1, width), w_attn_out
    )

    grad_tokens, gg = token_gradient(
        z_scalar, grad_pieces, x, dy, ln_row, mlp_ngrad[:rows], ngrad_came, w_all
    )

    gw_attn = exchange_half(gw_attn.reshape(width, width), grp, swap_packs)
    gw_attn = exchange_half(gw_attn, core, swap_core)
    for bit, send in halvings:
        gw_attn = exchange_half(gw_attn, bit, send)
    gw_attn = gather_doubling(gw_attn, doublings + [swap_core])

    gw_qkv = jnp.concatenate(qkv_weights, axis=1)
    half_width = width // 2
    gone = lax.dynamic_index_in_dim(gw_qkv, 1 - grp, 0, keepdims=False)
    kept = lax.dynamic_index_in_dim(gw_qkv, grp, 0, keepdims=False)
    gw_qkv = (kept.astype(F32) + swap_packs(gone).astype(F32)).astype(BF)
    for bit in range(rest_bits):
        gw_qkv = exchange_half(gw_qkv, (r_index >> bit) & 1, flip(1 << bit))
    gw_qkv = gather_doubling(
        gw_qkv, [flip(rest), flip(2 * rest)] + [flip(1 << bit) for bit in reversed(range(rest_bits))]
    )

    gb_in_full = lax.dynamic_update_slice(
        jnp.zeros((2, 2, hidden // 4), F32), gb_in.reshape(2, 1, hidden // 4), (0, core, 0)
    ).reshape(hidden)
    small = jnp.concatenate(
        [gg[0], gain_sums[0], gain_sums[1], gb_in_full, gb_out[0]]
    )
    small = lax.psum(small, ("seq", "grp"))

    def share(start, size):
        return lax.dynamic_slice_in_dim(small, start + grp * (size // 2), size // 2, 0)

    in_pieces = jnp.concatenate([gw_in_all, gw_in_came], axis=0)
    out_pieces = jnp.concatenate([gw_out_all, gw_out_came], axis=0)
    count = gw_in_all.shape[0]
    full_index = core * count + share_index
    grad_w_in = place(in_pieces, full_index)
    grad_w_in = (
        grad_w_in.reshape(2, half_width, hidden // 4 * 2)
    )
    grad_w_in = (
        grad_w_in.reshape(2, half_width, 2, hidden // 4).transpose(1, 2, 0, 3).reshape(half_width, hidden)
    )
    grad_w_mlp_out = place(out_pieces, full_index).reshape(hidden // 2, width)
    grad_w_attn_out = place(gw_attn, full_index).reshape(half_width, width)

    index = z_index
    for position, bit in enumerate(range(rest_bits)):
        index = index + (((r_index >> bit) & 1) << (rest_bits - 1 - position)) * Z_COUNT
    qkv_all = place(gw_qkv, index).reshape(rest, Z_COUNT, 3 * PER_Z * HD // rest, half_width)
    grad_w_qkv = (
        qkv_all.transpose(1, 0, 2, 3)
        .reshape(Z_COUNT, PER_Z, 3, HD, half_width)
        .transpose(4, 2, 0, 1, 3)
        .reshape(half_width, 3 * width)
    )
    return (
        result[None],
        grad_tokens[None],
        share(0, width),
        grad_w_qkv,
        share(width, HD),
        share(width + HD, HD),
        grad_w_attn_out,
        grad_w_in,
        share(width + 2 * HD, hidden),
        grad_w_mlp_out,
        share(width + 2 * HD + hidden, width),
    )


def solution(mesh):
    placed = (
        P("grp", "seq", None), P("grp", None), P("grp", None),
        P(), P(), P(), P(), P(), P(), P(), P(), P(), P("grp", "seq", None),
    )
    return jax.shard_map(
        per_device,
        mesh=mesh,
        in_specs=placed,
        out_specs=(
            P("grp", "seq", None), P("grp", "seq", None), P("grp"), P("grp", None), P("grp"),
            P("grp"), P("grp", None), P("grp", None), P("grp"), P("grp", None), P("grp"),
        ),
        check_vma=False,
    )
```

```python
import functools

import jax
import jax.numpy as jnp
from jax import lax
from jax.experimental import pallas as pl
from jax.experimental.pallas import tpu as pltpu
from jax.sharding import PartitionSpec as P

H = 12
HD = 64
Z_COUNT = 4
PER_Z = H // Z_COUNT
EPSILON = 1e-06
BF = jnp.bfloat16
F32 = jnp.float32
VMEM_BYTES = 58 * 1024 * 1024
FLOPS_PER_US = 1_150_000_000


def params():
    return pltpu.CompilerParams(vmem_limit_bytes=VMEM_BYTES)


def dot_nn(left, right):
    return lax.dot_general(left, right, (((1,), (0,)), ((), ())), preferred_element_type=F32)


def dot_nt(left, right):
    return lax.dot_general(left, right, (((1,), (1,)), ((), ())), preferred_element_type=F32)


def dot_tn(left, right):
    return lax.dot_general(left, right, (((0,), (0,)), ((), ())), preferred_element_type=F32)


def whole(shape):
    return pl.BlockSpec(shape, lambda *_: (0,) * len(shape))


def normalized(values, axis):
    mean = jnp.mean(values, axis=axis, keepdims=True)
    centred = values - mean
    spread = jnp.mean(centred * centred, axis=axis, keepdims=True)
    scale = lax.rsqrt(spread + EPSILON)
    return centred * scale, scale


GRP, CORE, TOP, Z_LOW, Z_HIGH = range(5)
SHARDS = 8


COST_US = {
    "prep": 4, "mlp": 18, "qkv": 6, "attention": 18, "post": 5, "post_pair": 9, "block_output": 5, "token_gradient": 6, "stage": 3,
    "first_stage": 4, "place_mlp": 9, "place_heads": 8,
}


def cost(name):
    return pl.CostEstimate(flops=COST_US[name] * FLOPS_PER_US, bytes_accessed=0, transcendentals=0)


def call(body, scalars, inputs, in_specs, out_shapes, out_specs, scratch=(), grid=(1,), name=None):
    return pl.pallas_call(
        body,
        grid_spec=pltpu.PrefetchScalarGridSpec(
            num_scalar_prefetch=1,
            grid=grid,
            in_specs=in_specs,
            out_specs=out_specs,
            scratch_shapes=list(scratch),
        ),
        out_shape=out_shapes,
        compiler_params=params(),
        cost_estimate=cost(name),
        name=name,
    )(scalars, *inputs)


def struct(shape, dtype):
    return jax.ShapeDtypeStruct(shape, dtype)


def prep_kernel(shifts, coords, dy_ref, w_ref, sum_ref, *refs):
    out_refs, grad_s = refs[:-1], refs[-1]
    dy = dy_ref[...]
    sum_ref[...] = jnp.sum(dy.astype(F32), axis=0, keepdims=True)
    grad_s[...] = dot_nt(w_ref[...], dy).astype(BF)
    z_index = coords[Z_LOW] + 2 * coords[Z_HIGH]
    depth = PER_Z * HD
    for shift, out_ref in zip(shifts, out_refs, strict=True):
        row = pl.multiple_of(lax.rem(z_index + shift, Z_COUNT) * depth, depth)
        out_ref[...] = grad_s[pl.ds(row, depth), :]


def prep(coords, shifts, dy, w_attn_out):
    rows, width = dy.shape
    piece = (PER_Z * HD, rows)
    return call(
        functools.partial(prep_kernel, shifts),
        coords,
        [dy, w_attn_out],
        [whole((rows, width)), whole((width, width))],
        [struct((1, width), F32)] + [struct(piece, BF)] * len(shifts),
        [whole((1, width))] + [whole(piece)] * len(shifts),
        [pltpu.VMEM((width, rows), BF)],
        name="prep",
    )


def mlp_kernel(coords, *refs):
    x_refs, dy_refs, refs = refs[:4], refs[4:8], refs[8:]
    (gain_ref, w_in_ref, b_in_ref, w_out_ref, near_ref, mid_ref, far_ref, keep_ref, send_ref,
     gb_in_ref, normed_s, dy_s, out_s, ngrad_s, g_in_s, g_out_s) = refs
    step = pl.program_id(0)
    rows = x_refs[0].shape[0]
    tile = w_in_ref.shape[1]

    @pl.when(step == 0)
    def _():
        for i in range(4):
            span = slice(i * rows, (i + 1) * rows)
            hat, _unused = normalized(x_refs[i][...].astype(F32), 1)
            normed_s[span, :] = (hat * gain_ref[...]).astype(BF)
            dy_s[span, :] = dy_refs[i][...]
        out_s[...] = jnp.zeros_like(out_s)
        ngrad_s[...] = jnp.zeros_like(ngrad_s)

    pre = dot_nn(normed_s[...], w_in_ref[...]) + b_in_ref[...]
    square = pre * pre
    tanh = jnp.tanh(pre * (0.7978845608028654 + 0.03567740813630193 * square))
    half = 0.5 + 0.5 * tanh
    hidden = (pre * half).astype(BF)
    slope = half + pre * (0.5 - 0.5 * tanh * tanh) * (
        0.7978845608028654 + 0.10703222440890579 * square
    )
    out_s[...] += dot_nn(hidden, w_out_ref[...])
    grad_pre_f = slope * dot_nt(dy_s[...], w_out_ref[...])
    grad_pre = grad_pre_f.astype(BF)
    gb_in_ref[...] = jnp.sum(grad_pre.astype(F32), axis=0, keepdims=True)
    ngrad_s[...] += dot_nt(grad_pre, w_in_ref[...])
    span = pl.ds(pl.multiple_of(step * tile, tile), tile)
    g_in_s[span, :] = dot_nn(jnp.transpose(grad_pre), normed_s[...]).astype(BF)
    g_out_s[span, :] = dot_nn(jnp.transpose(hidden), dy_s[...]).astype(BF)

    @pl.when(step == pl.num_programs(0) - 1)
    def _():
        for which, total in enumerate((out_s, ngrad_s)):
            near_ref[which] = total[:rows, :]
            mid_ref[which] = total[2 * rows : 3 * rows, :].astype(BF)
            far_ref[0, which] = total[rows : 2 * rows, :].astype(BF)
            far_ref[1, which] = total[3 * rows :, :].astype(BF)

    part = g_out_s.shape[0] // SHARDS
    for value in (0, 1):

        @pl.when((step == pl.num_programs(0) - 1) & (coords[TOP] == value))
        def _():
            for shard in range(SHARDS):
                target = keep_ref if shard // Z_COUNT == value else send_ref
                start = shard % Z_COUNT * 2 * part
                span = slice(shard * part, (shard + 1) * part)
                target[start : start + part, :] = g_out_s[span, :]
                target[start + part : start + 2 * part, :] = g_in_s[span, :]


def mlp(coords, xs, dys, ln_gain, w_in, b_in, w_out):
    rows, width = xs[0].shape
    own = w_in.shape[1] // 4
    tile = 256
    steps = own // tile
    place = lambda s, c: (c[GRP] * 2 + c[CORE]) * steps + s
    share = (own, width)
    return call(
        mlp_kernel,
        coords,
        [*xs, *dys, ln_gain, w_in, b_in, w_out],
        [whole((rows, width))] * 8
        + [
            whole((1, width)),
            pl.BlockSpec((width, tile), lambda s, c: (0, place(s, c))),
            pl.BlockSpec((1, tile), lambda s, c: (0, place(s, c))),
            pl.BlockSpec((tile, width), lambda s, c: (place(s, c), 0)),
        ],
        [
            struct((2, rows, width), F32),
            struct((2, rows, width), BF),
            struct((2, 2, rows, width), BF),
            struct(share, BF),
            struct(share, BF),
            struct((1, own), F32),
        ],
        [
            whole((2, rows, width)),
            whole((2, rows, width)),
            whole((2, 2, rows, width)),
            whole(share),
            whole(share),
            pl.BlockSpec((1, tile), lambda s, c: (0, s)),
        ],
        [
            pltpu.VMEM((4 * rows, width), BF),
            pltpu.VMEM((4 * rows, width), BF),
            pltpu.VMEM((4 * rows, width), F32),
            pltpu.VMEM((4 * rows, width), F32),
            pltpu.VMEM((own, width), BF),
            pltpu.VMEM((own, width), BF),
        ],
        grid=(steps,),
        name="mlp",
    )


def qkv_kernel(count, coords, *refs):
    x_refs, refs = refs[:count], refs[count:]
    w_refs, refs = refs[:6], refs[6:]
    gain_ref, q_gain_ref, k_gain_ref, normed_ref, q_ref, kv_ref, raw_ref, w_s, turn_s = refs
    rows = x_refs[0].shape[0]
    zeros = jnp.zeros((HD, rows), F32)
    for i, w_ref in enumerate(w_refs):
        w_s[:, i * 128 : (i + 1) * 128] = w_ref[...]
    for slot in range(count):
        span = slice(slot * rows, (slot + 1) * rows)
        hat, _unused = normalized(x_refs[slot][...].astype(F32), 1)
        normed = (hat * gain_ref[...]).astype(BF)
        normed_ref[span, :] = normed
        projected = dot_nn(normed, w_s[...])
        turn_s[slot] = jnp.transpose(projected)
    for slot in range(count):
        span = slice(slot * rows, (slot + 1) * rows)
        for head in range(PER_Z):
            q_raw, k_raw, v = (
                turn_s[slot, pl.ds(pl.multiple_of(part * 256 + head * HD + coords[Z_LOW] * HD, HD), HD), :]
                for part in range(3)
            )
            raw_ref[head, :HD, span] = q_raw
            raw_ref[head, HD:, span] = k_raw
            q = normalized(q_raw, 0)[0] * q_gain_ref[...] * HD ** (-0.5)
            k = normalized(k_raw, 0)[0] * k_gain_ref[...]
            q_ref[head, span, :] = jnp.transpose(jnp.concatenate([q, zeros], axis=0)).astype(BF)
            kv_ref[head, span, :] = jnp.transpose(jnp.concatenate([k, v], axis=0)).astype(BF)


def qkv(coords, blocks, ln_gain, w_qkv, q_gain, k_gain):
    rows, width = blocks[0].shape
    count = len(blocks)
    total = count * rows

    def columns(part, second):
        first = lambda c: 3 * (c[Z_LOW] + 2 * c[Z_HIGH]) // 2
        return pl.BlockSpec((width, 128), lambda i, c: (0, part * (width // 128) + first(c) + second))

    shapes = [
        struct((total, width), BF),
        struct((PER_Z, total, 2 * HD), BF),
        struct((PER_Z, total, 2 * HD), BF),
        struct((PER_Z, 2 * HD, total), F32),
    ]
    return call(
        functools.partial(qkv_kernel, count),
        coords,
        [*blocks, *[w_qkv] * 6, ln_gain, q_gain, k_gain],
        [whole((rows, width))] * count
        + [columns(part, second) for part in range(3) for second in range(2)]
        + [whole((1, width)), whole((HD, 1)), whole((HD, 1))],
        shapes,
        [whole(shape.shape) for shape in shapes],
        [pltpu.VMEM((width, 768), BF), pltpu.VMEM((count, 768, rows), F32)],
        name="qkv",
    )


def attention_kernel(groups, slots, sources, coords, *refs):
    count = len(groups)
    q_refs, refs = refs[:count], refs[count:]
    do_refs, refs = refs[:slots], refs[slots:]
    kv_refs, refs = refs[: sources * count], refs[sources * count :]
    qi_ref, ki_ref, out_ref, *refs = refs
    dq_ref, low_ref, high_ref, q_s, do_s, kv_s, one_v_s, e_s, acc_s = refs
    rows = sum(groups)
    tokens = rows // slots
    start = 0
    for group, size in enumerate(groups):
        span = slice(start, start + size)
        lane = lax.broadcasted_iota(jnp.int32, (size, 2 * HD), 1)
        q_s[span, :] = q_refs[group][0]
        for source in range(sources):
            block = kv_refs[source * count + group][0]
            kv_s[source, span, :] = block
            one_v_s[source, span, :] = jnp.where(lane < HD, jnp.ones((), BF), block)
        start += size
    for slot in range(slots):
        grad = do_refs[slot][...].astype(F32)
        do_s[slot * tokens : (slot + 1) * tokens, :] = jnp.transpose(
            jnp.concatenate([jnp.zeros_like(grad), grad], axis=0)
        )
    acc_s[...] = jnp.zeros_like(acc_s)

    def forward(source, carry):
        scores = dot_nt(q_s[...], kv_s[source])
        same = qi_ref[...] == ki_ref[source]
        weights = jnp.where(same, jnp.exp(scores), 0.0).astype(BF)
        e_s[source] = weights
        acc_s[...] += dot_nn(weights, one_v_s[source])
        return carry

    lax.fori_loop(0, sources, forward, 0)
    acc = acc_s[...]
    wide = lax.broadcasted_iota(jnp.int32, (rows, 2 * HD), 1)
    attended = jnp.where(wide >= HD, acc / pltpu.roll(acc, HD, 1), 0.0)
    inverse = 1.0 / acc[:, 0:1]
    do = do_s[...]
    out_dot = jnp.sum(do * attended, axis=1, keepdims=True) * inverse
    coarse = out_dot.astype(BF).astype(F32)
    do = do * inverse
    probe = jnp.where(wide == 0, -coarse, jnp.where(wide == 1, coarse - out_dot, do)).astype(BF)
    out_ref[...] = jnp.transpose(attended)[HD:].astype(BF)
    q_t = jnp.transpose(q_s[...].astype(F32))[:HD].astype(BF)
    do_t = jnp.transpose(do)[HD:].astype(BF)
    acc_s[...] = jnp.zeros_like(acc_s)

    def backward_into(dkv_ref, first):
        def backward(source, carry):
            weights = e_s[first + source]
            grad_weights = dot_nt(probe, one_v_s[first + source])
            grad_scores = (weights.astype(F32) * grad_weights).astype(BF)
            acc_s[...] += dot_nn(grad_scores, kv_s[first + source])
            dkv_ref[source, :HD, :] = dot_nn(q_t, grad_scores).astype(BF)
            dkv_ref[source, HD:, :] = dot_nn(do_t, weights).astype(BF)
            return carry

        lax.fori_loop(0, sources // 2, backward, 0)

    backward_into(high_ref, sources // 2)
    backward_into(low_ref, 0)
    dq_ref[...] = jnp.transpose(acc_s[...])[:HD]


def attention(head, coords, q_groups, do_slots, kv_sources, query_images, key_images):
    groups = [q.shape[1] for q in q_groups]
    slots, sources = len(do_slots), len(kv_sources)
    rows = sum(groups)
    parts = [pl.BlockSpec((1, size, 2 * HD), lambda i, c: (head, 0, 0)) for size in groups]
    do_part = pl.BlockSpec((HD, rows // slots), lambda i, c: (head, 0))
    half = (sources // 2, 2 * HD, rows)
    return call(
        functools.partial(attention_kernel, groups, slots, sources),
        coords,
        [*q_groups, *do_slots, *[kv for source in kv_sources for kv in source], query_images, key_images],
        parts
        + [do_part] * slots
        + parts * sources
        + [whole((rows, 1)), whole((sources, 1, rows))],
        [struct((HD, rows), BF), struct((HD, rows), F32), struct(half, BF), struct(half, BF)],
        [whole((HD, rows)), whole((HD, rows)), whole(half), whole(half)],
        [
            pltpu.VMEM((rows, 2 * HD), BF),
            pltpu.VMEM((rows, 2 * HD), F32),
            pltpu.VMEM((sources, rows, 2 * HD), BF),
            pltpu.VMEM((sources, rows, 2 * HD), BF),
            pltpu.VMEM((sources, rows, rows), BF),
            pltpu.VMEM((rows, 2 * HD), F32),
        ],
        name="attention",
    )


EXTRA = 16


def post_kernel(groups, slots, terms, heads, coords, *refs):
    count = len(groups)
    per_head = []
    for _head in heads:
        per_head.append((refs[0], refs[1], refs[2 : 2 + terms], refs[2 + terms : 2 + terms + count]))
        refs = refs[2 + terms + count :]
    normed_refs, dy_refs, refs = refs[:count], refs[count : count + slots], refs[count + slots :]
    (q_gain_ref, k_gain_ref, b_in_ref, b_out_ref), refs = refs[:4], refs[4:]
    piece_refs, (keep_ref, send_ref) = refs[:slots], refs[slots:]
    tokens = piece_refs[0].shape[1]
    half = keep_ref.shape[1]
    rows, attn = 3 * HD // 2, HD // 2
    block = len(heads) * rows + EXTRA
    gains = [0.0, 0.0]
    for place, (dq_ref, out_ref, term_refs, raw_refs) in enumerate(per_head):
        total = attn_total = None
        start = 0
        for group, size in enumerate(groups):
            span = slice(start, start + size)
            dkv = sum(term[0][:, span].astype(F32) for term in term_refs)
            grads = []
            for which, (grad, gain) in enumerate(
                ((dq_ref[:, span], q_gain_ref[...] * HD ** (-0.5)), (dkv[:HD], k_gain_ref[...]))
            ):
                hat, scale = normalized(raw_refs[group][0, which * HD : (which + 1) * HD, :], 0)
                factor = HD ** (-0.5) if which == 0 else 1.0
                gains[which] += jnp.sum(grad * hat, axis=1, keepdims=True) * factor
                grad = grad * gain
                grad = scale * (
                    grad
                    - jnp.mean(grad, axis=0, keepdims=True)
                    - hat * jnp.mean(grad * hat, axis=0, keepdims=True)
                )
                grads.append(grad)
            grads.append(dkv[HD:])
            projected_grad = jnp.concatenate(grads, axis=0).astype(BF)
            first = place * 4 * HD
            for slot in range(start // tokens, (start + size) // tokens):
                inner = slice(slot * tokens - start, (slot + 1) * tokens - start)
                outer = slice(slot * tokens, (slot + 1) * tokens)
                piece_refs[slot][first : first + 3 * HD, :] = projected_grad[:, inner]
                piece_refs[slot][first + 3 * HD : first + 4 * HD, :] = out_ref[:, outer]
                term = dot_nn(out_ref[:, outer], dy_refs[slot][...])
                attn_total = term if attn_total is None else attn_total + term
            term = dot_nn(projected_grad, normed_refs[group][...])
            total = term if total is None else total + term
            start += size
        total, attn_total = total.astype(BF), attn_total.astype(BF)
        for value in (0, 1):

            @pl.when(coords[CORE] == value)
            def _():
                for side in (0, 1):
                    lanes = slice(side * half, (side + 1) * half)
                    at = side * block + place * rows
                    attn_at = 2 * block + (side * len(heads) + place) * attn
                    for target, mine in ((keep_ref, value), (send_ref, 1 - value)):
                        target[at : at + rows, :] = total[mine * rows : (mine + 1) * rows, lanes]
                        target[attn_at : attn_at + attn, :] = attn_total[
                            mine * attn : (mine + 1) * attn, lanes
                        ]

    turned = jnp.transpose(
        jnp.concatenate([jnp.broadcast_to(gain, (HD, 128)) for gain in gains], axis=0)
    )
    line = lax.broadcasted_iota(jnp.int32, (EXTRA, half), 0)
    gain_row = jnp.concatenate([turned[:1], jnp.zeros((1, half - 2 * HD), F32)], axis=1)
    for pack in (0, 1):
        extra = jnp.where(line == 5, gain_row, 0.0)
        if heads[0] == 0:
            extra = jnp.where(line == 0, b_out_ref[:, pack * half : (pack + 1) * half], extra)
            for i in (0, 1):
                here = (line == 1 + 2 * coords[CORE] + i) & (coords[GRP] == pack)
                extra = jnp.where(here, b_in_ref[:, i * half : (i + 1) * half], extra)
        for target in (keep_ref, send_ref):
            target[(pack + 1) * block - EXTRA : (pack + 1) * block, :] = extra.astype(BF)


def post(heads, coords, parts, raw_groups, normed_groups, dy_slots, q_gain, k_gain, gb_in, gb_out):
    groups = [raw.shape[2] for raw in raw_groups]
    width = normed_groups[0].shape[1]
    rows = sum(groups)
    slots = len(dy_slots)
    tokens = rows // slots
    count = len(heads)
    terms = len(parts[0][2])
    piece = (count * 4 * HD, tokens)
    share = (2 * (count * 3 * HD // 2 + EXTRA) + count * HD, width // 2)
    inputs, specs = [], []
    for head, (dq, out, added) in zip(heads, parts, strict=True):
        inputs += [dq, out, *added, *raw_groups]
        specs += [whole((HD, rows))] * 2 + [whole((1, 2 * HD, rows))] * terms
        specs += [
            pl.BlockSpec((1, 2 * HD, size), functools.partial(lambda h, i, c: (h, 0, 0), head))
            for size in groups
        ]
    return call(
        functools.partial(post_kernel, groups, slots, terms, heads),
        coords,
        [*inputs, *normed_groups, *dy_slots, q_gain, k_gain, gb_in, gb_out],
        specs
        + [whole((size, width)) for size in groups]
        + [whole((tokens, width))] * slots
        + [whole((HD, 1))] * 2
        + [whole((1, width))] * 2,
        [struct(piece, BF)] * slots + [struct(share, BF)] * 2,
        [whole(piece)] * slots + [whole(share)] * 2,
        name="post" if count == 1 else "post_pair",
    )


def head_of(coords, slot_shift, head):
    z_index = coords[Z_LOW] + 2 * coords[Z_HIGH]
    return lax.rem(z_index + slot_shift, Z_COUNT) * PER_Z + head


def piece_of(pieces, slot, head, part):
    return pieces[Z_COUNT * head + slot][part * HD : (part + 1) * HD, :]


def output_kernel(shifts, coords, *refs):
    count = PER_Z * Z_COUNT
    pieces, refs = refs[:count], refs[count:]
    x_ref, near_ref, far_ref, back_ref, b_ref, w_ref, out_ref, att_s = refs
    for head in range(PER_Z):
        for slot, shift in enumerate(shifts):
            row = pl.multiple_of(head_of(coords, shift, head) * HD, HD)
            att_s[pl.ds(row, HD), :] = piece_of(pieces, slot, head, 3)
    out_ref[...] = (
        x_ref[...].astype(F32)
        + near_ref[0]
        + far_ref[0, 0].astype(F32)
        + back_ref[0].astype(F32)
        + b_ref[...]
        + dot_nn(jnp.transpose(att_s[...]), w_ref[...])
    ).astype(BF)


def block_output(coords, shifts, pieces, x, near, far, back, b_out, w_attn_out):
    rows, width = x.shape
    one = whole((1, rows, width))
    return call(
        functools.partial(output_kernel, shifts),
        coords,
        [*pieces, x, near, far, back, b_out, w_attn_out],
        [whole(piece.shape) for piece in pieces]
        + [whole((rows, width)), one, whole((1, 1, rows, width)), one]
        + [whole((1, width)), whole((width, width))],
        struct((rows, width), BF),
        whole((rows, width)),
        [pltpu.VMEM((width, rows), BF)],
        name="block_output",
    )


def tokens_kernel(shifts, coords, *refs):
    count = PER_Z * Z_COUNT
    pieces, refs = refs[:count], refs[count:]
    x_ref, dy_ref, gain_ref, near_ref, far_ref, back_ref, w_ref, out_ref, grad_s = refs
    width = x_ref.shape[1]
    for head in range(PER_Z):
        for slot, shift in enumerate(shifts):
            row = pl.multiple_of(head_of(coords, shift, head) * HD, HD)
            for part in range(3):
                grad_s[pl.ds(part * width + row, HD), :] = piece_of(pieces, slot, head, part)
    normed_grad = (
        near_ref[0]
        + far_ref[0, 0].astype(F32)
        + back_ref[0].astype(F32)
        + dot_nt(jnp.transpose(grad_s[...]), w_ref[...])
    )
    hat, scale = normalized(x_ref[...].astype(F32), 1)
    grad = normed_grad * gain_ref[...]
    out_ref[...] = dy_ref[...].astype(F32) + scale * (
        grad
        - jnp.mean(grad, axis=1, keepdims=True)
        - hat * jnp.mean(grad * hat, axis=1, keepdims=True)
    )


def token_gradient(coords, shifts, pieces, x, dy, ln_gain, near, far, back, w_qkv):
    rows, width = x.shape
    one = pl.BlockSpec((1, rows, width), lambda i, c: (1, 0, 0))
    return call(
        functools.partial(tokens_kernel, shifts),
        coords,
        [*pieces, x, dy, ln_gain, near, far, back, w_qkv],
        [whole(piece.shape) for piece in pieces]
        + [whole((rows, width))] * 2
        + [whole((1, width)), one, pl.BlockSpec((1, 1, rows, width), lambda i, c: (0, 1, 0, 0)), one]
        + [whole(w_qkv.shape)],
        struct((rows, width), F32),
        whole((rows, width)),
        [pltpu.VMEM((3 * width, rows), BF)],
        name="token_gradient",
    )


HALVE, BOTH, KEEP = range(3)


def stage_kernel(segments, bit, coords, keep_ref, came_ref, *out_refs):
    keep_at = came_at = kept = sent = 0
    for rows, came, mode in segments:
        total = keep_ref[keep_at : keep_at + rows, :]
        if came:
            total = (total.astype(F32) + came_ref[came_at : came_at + rows, :].astype(F32)).astype(BF)
            came_at += rows
        keep_at += rows
        if mode == HALVE:
            half = rows // 2
            for value in (0, 1):

                @pl.when(coords[bit] == value)
                def _():
                    out_refs[0][kept : kept + half, :] = total[value * half : (value + 1) * half]
                    out_refs[1][sent : sent + half, :] = total[(1 - value) * half : (2 - value) * half]

            kept += half
            sent += half
        else:
            out_refs[0][kept : kept + rows, :] = total
            kept += rows
            if mode == BOTH:
                out_refs[1][sent : sent + rows, :] = total
                sent += rows


def stage(coords, segments, bit, keep, came):
    width = keep.shape[1]
    kept = sum(rows // 2 if mode == HALVE else rows for rows, _came, mode in segments)
    sent = sum({HALVE: rows // 2, BOTH: rows, KEEP: 0}[mode] for rows, _came, mode in segments)
    shapes = [(kept, width)] + ([(sent, width)] if sent else [])
    return call(
        functools.partial(stage_kernel, segments, bit),
        coords,
        [keep, came],
        [whole(keep.shape), whole(came.shape)],
        [struct(shape, BF) for shape in shapes],
        [whole(shape) for shape in shapes],
        name="stage",
    )


def first_stage_kernel(counts, coords, *refs):
    (*shares, keep_ref, send_ref) = refs
    attn, rows = HD // 2, 3 * HD // 2
    blocks = [count * rows + EXTRA for count in counts]
    pairs = list(zip(blocks, counts, shares[::2], shares[1::2], strict=True))
    for value in (0, 1):

        @pl.when(coords[GRP] == value)
        def _():
            for pack, target in ((value, keep_ref), (1 - value, send_ref)):
                extra, at = 0.0, 0
                for block, count, own, came in pairs:
                    span = slice(pack * block, (pack + 1) * block)
                    total = own[span, :].astype(F32) + came[span, :].astype(F32)
                    target[at : at + count * rows, :] = total[: count * rows].astype(BF)
                    extra = extra + total[count * rows :]
                    at += count * rows
                target[PER_Z * (rows + 2 * attn) :, :] = extra.astype(BF)

    before = 0
    for block, count, own, came in pairs:
        total = (own[2 * block :, :].astype(F32) + came[2 * block :, :].astype(F32)).astype(BF)
        for side in (0, 1):
            start = PER_Z * rows + (side * PER_Z + before) * attn
            for target in (keep_ref, send_ref):
                target[start : start + count * attn, :] = total[
                    side * count * attn : (side + 1) * count * attn
                ]
        before += count


def first_stage(coords, counts, shares):
    half = shares[0].shape[1]
    shape = (PER_Z * (3 * HD // 2 + HD) + EXTRA, half)
    return call(
        functools.partial(first_stage_kernel, counts),
        coords,
        shares,
        [whole(share.shape) for share in shares],
        [struct(shape, BF)] * 2,
        [whole(shape)] * 2,
        name="first_stage",
    )


def mlp_place_kernel(coords, *refs):
    units, (w_ref, rows_ref, columns_ref, sum_ref, turn_s) = refs[:4], refs[4:]
    step = pl.program_id(0)
    part, half = units[0].shape[1] // 2, units[0].shape[2] // 2
    here = coords[Z_LOW] * 2 + coords[Z_HIGH]

    @pl.when(step == 0)
    def _():
        sum_ref[...] = jnp.zeros_like(sum_ref)

    chosen = (step // 2 ^ coords[CORE]) * 2 + (step % 2 ^ coords[TOP])
    for i, unit in enumerate(units):

        @pl.when(chosen == i)
        def _():
            for shard in range(Z_COUNT):
                rows_ref[shard * part : (shard + 1) * part, :] = unit[shard ^ here, :part, :].astype(F32)

    lanes = pl.ds(pl.multiple_of((step // 2 ^ coords[GRP]) * half, 128), half)
    chosen = (step % 2 ^ coords[CORE]) * 2 + coords[TOP]
    for i in range(4):

        @pl.when(chosen == i)
        def _():
            for top in (0, 1):
                unit = units[i ^ top]
                for shard in range(Z_COUNT):
                    row = (top * Z_COUNT + shard) * part
                    turn_s[row : row + part, :] = unit[shard ^ here, part:, lanes].astype(F32)

    total = 0.0
    for block in range(SHARDS * part // 128):
        span = slice(block * 128, (block + 1) * 128)
        turned = jnp.transpose(turn_s[span, :])
        columns_ref[:, span] = turned
        total = total + turned * w_ref[:, span].astype(F32)
    sum_ref[...] += jnp.sum(total, axis=1, keepdims=True)


def place_mlp(coords, units, w_in):
    _shards, rows, width = units[0].shape
    part, half = rows // 2, width // 2
    span = SHARDS * part
    return call(
        mlp_place_kernel,
        coords,
        [*units, w_in],
        [whole(unit.shape) for unit in units]
        + [pl.BlockSpec((half, span), lambda s, c: (c[GRP], s))],
        [
            struct((2 * span, width), F32),
            struct((half, 4 * span), F32),
            struct((half, 1), F32),
        ],
        [
            pl.BlockSpec((Z_COUNT * part, width), lambda s, c: (s, 0)),
            pl.BlockSpec((half, span), lambda s, c: (0, s)),
            whole((half, 1)),
        ],
        [pltpu.VMEM((span, half), F32)],
        grid=(4,),
        name="place_mlp",
    )


def heads_kernel(coords, *refs):
    (*unit_refs, w_ref, gain_ref, sum_ref, qkv_ref, attn_ref, ln_ref, turn_s) = refs
    half = unit_refs[0].shape[2]
    width = 2 * half
    q_rows, a_rows, unit = 3 * PER_Z * HD // 4, PER_Z * HD // 2, 16
    per_head = 3 * HD // 2 // unit
    for relative in range(8):
        block = unit_refs[relative // 2][relative % 2].astype(F32)
        core = coords[CORE] ^ (relative // 4)
        top = coords[TOP] ^ (relative // 2 % 2)
        low = coords[Z_LOW] ^ (relative % 2)
        for side in (0, 1):
            z_index = low + 2 * (coords[Z_HIGH] ^ side)
            for i in range(q_rows // unit):
                number = top * (q_rows // unit) + i
                inner = number % per_head + core * per_head
                row = (inner // (HD // unit)) * width + (inner % (HD // unit)) * unit
                row = row + (z_index * PER_Z + number // per_head) * HD
                turn_s[pl.ds(pl.multiple_of(row, unit), unit), :] = block[
                    side * q_rows + i * unit : side * q_rows + (i + 1) * unit
                ]
        lanes = pl.ds(pl.multiple_of(top * half, 128), half)
        for head in range(PER_Z):
            row = pl.multiple_of((low * PER_Z + head) * HD + core * (HD // 2), HD // 2)
            start = 2 * q_rows + head * (HD // 2)
            attn_ref[pl.ds(row, HD // 2), lanes] = block[start : start + HD // 2]
    total = 0.0
    for block in range(3 * width // 128):
        span = slice(block * 128, (block + 1) * 128)
        turned = jnp.transpose(turn_s[span, :])
        qkv_ref[:, span] = turned
        total = total + turned * w_ref[:, span].astype(F32)
    ln = (jnp.sum(total, axis=1, keepdims=True) + sum_ref[...]) / gain_ref[...]
    ln_ref[...] = jnp.transpose(jnp.broadcast_to(ln, (half, 128)))[:1]


def place_heads(coords, units, w_qkv, gain_column, in_sums):
    half = units[0].shape[2]
    width = 2 * half
    row_half = lambda columns: pl.BlockSpec((half, columns), lambda s, c: (c[GRP], 0))
    return call(
        heads_kernel,
        coords,
        [*units, w_qkv, gain_column, in_sums],
        [whole(unit.shape) for unit in units] + [row_half(3 * width), row_half(1), whole((half, 1))],
        [struct((half, 3 * width), F32), struct((half, width), F32), struct((1, half), F32)],
        [whole((half, 3 * width)), whole((half, width)), whole((1, half))],
        [pltpu.VMEM((3 * width, half), F32)],
        name="place_heads",
    )


def per_device(
    tokens, lengths, image_ids, ln_gain, w_qkv, q_gain, k_gain,
    w_attn_out, w_in, b_in, w_mlp_out, b_out, cotangent,
):
    x, dy = tokens[0], cotangent[0]
    rows, width = x.shape
    half = width // 2
    hidden = w_in.shape[1]
    seq_count = lax.axis_size("seq")
    rest = seq_count // Z_COUNT
    rest_bits = rest.bit_length() - 1
    top_bit = rest_bits - 1
    me = lax.axis_index("seq")
    z_index, r_index = me // rest, me % rest
    grp = lax.axis_index("grp")
    core, top = r_index & 1, r_index >> top_bit
    coords = jnp.stack([grp, core, top, z_index & 1, z_index >> 1]).astype(jnp.int32)

    def z_shift(block, distance):
        route = [(i, (i + distance * rest) % seq_count) for i in range(seq_count)]
        return lax.ppermute(block, "seq", route)

    def flip(mask):
        route = [(i, i ^ mask) for i in range(seq_count)]
        return lambda block: lax.ppermute(block, "seq", route)

    def swap_packs(block):
        return lax.ppermute(block, "grp", [(0, 1), (1, 0)])

    swap_core, swap_top = flip(1), flip(1 << top_bit)
    swap_low, swap_high = flip(rest), flip(2 * rest)
    others = range(1, top_bit)

    def add(*terms):
        return sum(term.astype(F32) for term in terms).astype(BF)

    def after(value, *events):
        return lax.optimization_barrier((value, *events))[0]

    def after(value, *events):
        return lax.optimization_barrier((value, *events))[0]

    turn = [coords]

    def then(results):
        turn[0] = after(turn[0], results[0] if isinstance(results, (list, tuple)) else results)
        return results

    def until(*events):
        turn[0] = after(turn[0], *events)

    shifts = [0, 1, 3, 2]
    x_slots = {0: x, **{d: z_shift(x, d) for d in (1, 3)}}
    pack_x, pack_dy = swap_packs(x), swap_packs(dy)
    core_x, core_dy = swap_core(x), swap_core(dy)
    x_slots[2] = z_shift(after(x, x_slots[1]), 2)
    gb_out, *do_pieces = then(prep(coords, shifts, dy, w_attn_out))

    order = image_ids[0]
    labels = jnp.arange(order.shape[0], dtype=jnp.int32)
    ordered = jnp.sum(jnp.where(order[:, None] == labels[None, :], lengths[0][None, :], 0), axis=1)
    ends = jnp.cumsum(ordered)
    offsets = jnp.arange(rows, dtype=jnp.int32)
    slot_z = (z_index - jnp.array(shifts, dtype=jnp.int32)) % Z_COUNT
    masks = [2 * i for i in range(rest // 2)] + [2 * i + 1 for i in range(rest // 2)]
    source_r = r_index ^ jnp.array(masks, dtype=jnp.int32)
    starts = (slot_z[None, :] * rest + source_r[:, None]) * rows
    places = (starts[:, :, None] + offsets).reshape(rest, Z_COUNT * rows)
    images = jnp.sum((places[:, :, None] >= ends).astype(jnp.int32), axis=2)
    key_images = images[:, None, :]
    query_images = images[0][:, None]

    ln_row = ln_gain.reshape(1, width)
    q_col, k_col = q_gain.reshape(HD, 1), k_gain.reshape(HD, 1)

    normed_groups, q_groups, kv_groups, raw_groups = [], [], [], []

    def project(group):
        normed, q, kv, raw = then(
            qkv(turn[0], [x_slots[d] for d in group], ln_row, w_qkv, q_col, k_col)
        )
        normed_groups.append(normed)
        q_groups.append(q)
        raw_groups.append(raw)
        kv_groups.append({0: kv})

    def spread(group, bits, event):
        for bit in bits:
            moved = {m | 1 << bit: flip(1 << bit)(after(block, event)) for m, block in group.items()}
            group.update(moved)

    high_bits = list(reversed(range(1, rest_bits)))
    project([0, 1, 3])
    spread(kv_groups[0], high_bits, coords)
    near, mid, far, mlp_keep, mlp_send, gb_in = then(
        mlp(
            turn[0], [x, core_x, pack_x, swap_core(pack_x)], [dy, core_dy, pack_dy, swap_core(pack_dy)],
            ln_row, w_in, b_in.reshape(1, hidden), w_mlp_out,
        )
    )
    spread(kv_groups[0], [0], mlp_keep)
    do_moved = {d: z_shift(piece, d) for piece, d in zip(do_pieces[1:3], shifts[1:3], strict=True)}
    until(*do_moved.values())
    do_moved[2] = z_shift(after(do_pieces[3], x_slots[2]), 2)
    do_slots = [do_pieces[0], *(do_moved[d] for d in shifts[1:])]
    project([2])
    spread(kv_groups[1], [*high_bits, 0], coords)
    kv_sources = [[gathered[m] for gathered in kv_groups] for m in masks]
    mlp_came = swap_top(after(mlp_send, kv_groups[1][1 << top_bit]))
    dy_slots = {0: dy, **{d: z_shift(after(dy, do_moved[2]), d) for d in (1, 3)}}

    pieces, shares = [], []

    def finish(heads, parts):
        results = then(
            post(
                heads, turn[0], parts, raw_groups, normed_groups,
                [dy_slots[d] for d in shifts], q_col, k_col, gb_in, gb_out,
            )
        )
        for slot, d in enumerate(shifts):
            pieces.append(z_shift(results[slot], -d) if d else results[slot])
        shares.extend([results[Z_COUNT], swap_core(results[Z_COUNT + 1])])

    waiting = []
    size = mlp_keep.shape[0]
    for head in range(PER_Z):
        out_t, dq_t, low, high = then(
            attention(head, turn[0], q_groups, do_slots, kv_sources, query_images, key_images)
        )
        if head == 0:
            high = after(high, dy_slots[1], dy_slots[3], mlp_came)
            dy_slots[2] = z_shift(after(dy, dq_t), 2)
            far = swap_core(after(far, dq_t))
        else:
            high = after(high, *waiting[-1][2][2:], mlp_came)
        if head == 1:
            high = after(high, dy_slots[2])
        if head == 2:
            high = after(high, back, *pieces)
        came = swap_core(high)
        if head < 2:
            mlp_keep, mlp_send = then(
                stage(turn[0], [(size >> head, True, HALVE)], (Z_LOW, Z_HIGH)[head], mlp_keep, mlp_came)
            )
            mlp_came = (swap_low, swap_high)[head](mlp_send)
        parts = {2 * i: [low[i : i + 1], came[i : i + 1]] for i in range(rest // 2)}
        for bit in range(1, rest_bits):
            for mask in sorted(m for m in parts if m >> bit & 1):
                total = then(add(*parts.pop(mask)))
                parts[mask ^ (1 << bit)].append(flip(1 << bit)(total))
        waiting.append((dq_t, out_t, [low, came, *parts[0][2:]]))
        if head == 1:
            back = swap_packs(after(add(mid, far[1]), turn[0]))
            finish([0], waiting[:1])
    finish([1], waiting[1:2])
    share = then(add(after(mlp_keep, turn[0]), mlp_came))
    for bit in others:
        share = add(share, flip(1 << bit)(share))
    part = share.shape[0] // 2
    side = swap_packs(lax.dynamic_slice(share, (part, (1 - grp) * half), (part, half)))
    finish([2], waiting[2:])
    mine = jnp.concatenate([lax.dynamic_slice(share, (part, grp * half), (part, half)), side], axis=1)
    mlp_units = jnp.concatenate([share[:part], mine], axis=0)[None]
    for move in (swap_high, swap_low):
        mlp_units = jnp.concatenate([mlp_units, move(mlp_units)], axis=0)

    keep, send = then(first_stage(turn[0], [1, 1, 1], shares))
    q_size, a_size = 3 * PER_Z * HD // 2, PER_Z * HD
    came = swap_packs(send)
    near_parts = (near, far, back)
    keep, send = then(
        stage(
            turn[0],
            [(q_size, True, HALVE), (a_size, True, HALVE), (EXTRA, True, BOTH)],
            TOP, keep, came,
        )
    )
    q_size, a_size = q_size // 2, a_size // 2
    came = swap_top(send)
    share = add(keep, came)
    for bit in others:
        share = add(share, flip(1 << bit)(share))
    came = swap_high(share)
    middle = q_size + a_size
    attn = jnp.where(z_index >> 1 == grp, share[q_size:middle], came[q_size:middle])
    small = add(share[middle:], came[middle:])
    unit = jnp.concatenate([share[:q_size], came[:q_size], attn, small], axis=0)
    came = swap_low(unit)
    size = unit.shape[0] - EXTRA
    small = add(unit[size:], came[size:]).astype(F32)
    units = jnp.stack([unit[:size], came[:size]])
    came = swap_top(units)
    until(units)
    result = then(
        block_output(
            turn[0], shifts, pieces, x, *near_parts, b_out.reshape(1, width), w_attn_out
        )
    )
    grad_tokens = then(
        token_gradient(turn[0], shifts, pieces, x, dy, ln_row, *near_parts, w_qkv)
    )
    mlp_came = swap_top(mlp_units)
    mlp_units = [mlp_units, mlp_came, swap_core(mlp_units), swap_core(mlp_came)]
    grad_w_mlp_out, grad_w_in, in_sums = then(place_mlp(turn[0], mlp_units, w_in))
    came = after(came, grad_w_in)
    all_units = [units, came, swap_core(units), swap_core(came)]

    grad_w_qkv, grad_w_attn_out, grad_ln_gain = place_heads(
        coords, all_units, w_qkv, ln_gain.reshape(width, 1), in_sums
    )
    return (
        result[None],
        grad_tokens[None],
        grad_ln_gain.reshape(half),
        grad_w_qkv,
        lax.dynamic_slice(small[5], (grp * (HD // 2),), (HD // 2,)),
        lax.dynamic_slice(small[5], (HD + grp * (HD // 2),), (HD // 2,)),
        grad_w_attn_out,
        grad_w_in,
        small[1:5].reshape(hidden // 2),
        grad_w_mlp_out,
        small[0],
    )


def solution(mesh):
    placed = (
        P("grp", "seq", None), P("grp", None), P("grp", None),
        P(), P(), P(), P(), P(), P(), P(), P(), P(), P("grp", "seq", None),
    )
    return jax.shard_map(
        per_device,
        mesh=mesh,
        in_specs=placed,
        out_specs=(
            P("grp", "seq", None), P("grp", "seq", None), P("grp"), P("grp", None), P("grp"),
            P("grp"), P("grp", None), P("grp", None), P("grp"), P("grp", None), P("grp"),
        ),
        check_vma=False,
    )
```

```python
import functools

import jax
import jax.numpy as jnp
from jax import lax
from jax.experimental import pallas as pl
from jax.experimental.pallas import tpu as pltpu
from jax.sharding import PartitionSpec as P

H = 12
HD = 64
Z_COUNT = 4
PER_Z = H // Z_COUNT
EPSILON = 1e-06
BF = jnp.bfloat16
F32 = jnp.float32
VMEM_BYTES = 58 * 1024 * 1024
FLOPS_PER_US = 1_150_000_000


def params():
    return pltpu.CompilerParams(vmem_limit_bytes=VMEM_BYTES)


def dot_nn(left, right):
    return lax.dot_general(left, right, (((1,), (0,)), ((), ())), preferred_element_type=F32)


def dot_nt(left, right):
    return lax.dot_general(left, right, (((1,), (1,)), ((), ())), preferred_element_type=F32)


def dot_tn(left, right):
    return lax.dot_general(left, right, (((0,), (0,)), ((), ())), preferred_element_type=F32)


def whole(shape):
    return pl.BlockSpec(shape, lambda *_: (0,) * len(shape))


def normalized(values, axis):
    mean = jnp.mean(values, axis=axis, keepdims=True)
    centred = values - mean
    spread = jnp.mean(centred * centred, axis=axis, keepdims=True)
    scale = lax.rsqrt(spread + EPSILON)
    return centred * scale, scale


GRP, CORE, TOP, Z_LOW, Z_HIGH = range(5)
SHARDS = 8


COST_US = {"prep": 4, "mlp": 9, "qkv": 10, "attention": 18, "post": 0, "block_output": 5, "token_gradient": 6, "place_mlp": 9, "place_heads": 8}


def cost(us):
    return pl.CostEstimate(flops=us * FLOPS_PER_US, bytes_accessed=0, transcendentals=0)


def call(body, scalars, inputs, in_specs, out_shapes, out_specs, scratch=(), grid=(1,), name=None, us=None):
    return pl.pallas_call(
        body,
        grid_spec=pltpu.PrefetchScalarGridSpec(
            num_scalar_prefetch=1,
            grid=grid,
            in_specs=in_specs,
            out_specs=out_specs,
            scratch_shapes=list(scratch),
        ),
        out_shape=out_shapes,
        compiler_params=params(),
        cost_estimate=cost(COST_US.get(name, 0) if us is None else us),
        name=name,
    )(scalars, *inputs)


def struct(shape, dtype):
    return jax.ShapeDtypeStruct(shape, dtype)


def column(row):
    return jnp.transpose(jnp.broadcast_to(row, (8, row.shape[1])))[:, :1]


def prep_kernel(shifts, coords, x_ref, dy_ref, w_ref, pair_ref, sum_ref, *refs):
    out_refs, grad_s = refs[:-1], refs[-1]
    pair_ref[0] = x_ref[...]
    dy = dy_ref[...]
    pair_ref[1] = dy
    sum_ref[...] = jnp.sum(dy.astype(F32), axis=0, keepdims=True)
    grad_s[...] = dot_nt(w_ref[...], dy).astype(BF)
    z_index = coords[Z_LOW] + 2 * coords[Z_HIGH]
    depth = PER_Z * HD
    for shift, out_ref in zip(shifts, out_refs, strict=True):
        row = pl.multiple_of(lax.rem(z_index + shift, Z_COUNT) * depth, depth)
        out_ref[...] = grad_s[pl.ds(row, depth), :]


def prep(coords, shifts, x, dy, w_attn_out):
    rows, width = dy.shape
    piece = (PER_Z * HD, rows)
    return call(
        functools.partial(prep_kernel, shifts),
        coords,
        [x, dy, w_attn_out],
        [whole((rows, width))] * 2 + [whole((width, width))],
        [struct((2, rows, width), BF), struct((1, width), F32)] + [struct(piece, BF)] * len(shifts),
        [whole((2, rows, width)), whole((1, width))] + [whole(piece)] * len(shifts),
        [pltpu.VMEM((width, rows), BF)],
        name="prep",
    )


def mlp_kernel(second, coords, *refs):
    pairs, refs = refs[:2], refs[2:]
    gain_ref, w_in_refs, b_in_refs, w_out_refs, refs = refs[0], refs[1:3], refs[3:5], refs[5:7], refs[7:]
    w_in = jnp.concatenate([ref[...] for ref in w_in_refs], axis=1)
    b_in = jnp.concatenate([ref[...] for ref in b_in_refs], axis=1)
    w_out = jnp.concatenate([ref[...] for ref in w_out_refs], axis=0)
    before, refs = (refs[:3], refs[3:]) if second else ((), refs)
    (near_ref, far_ref), refs = refs[:2], refs[2:]
    rows = pairs[0].shape[1]
    normed = []
    for pair in pairs:
        hat, _unused = normalized(pair[0].astype(F32), 1)
        normed.append((hat * gain_ref[...]).astype(BF))
    normed = jnp.concatenate(normed, axis=0)
    dy = jnp.concatenate([pair[1] for pair in pairs], axis=0)
    pre = dot_nn(normed, w_in) + b_in
    square = pre * pre
    tanh = jnp.tanh(pre * (0.7978845608028654 + 0.03567740813630193 * square))
    half = 0.5 + 0.5 * tanh
    hidden = (pre * half).astype(BF)
    slope = half + pre * (0.5 - 0.5 * tanh * tanh) * (
        0.7978845608028654 + 0.10703222440890579 * square
    )
    grad_pre = (slope * dot_nt(dy, w_out)).astype(BF)
    for which, total in enumerate((dot_nn(hidden, w_out), dot_nt(grad_pre, w_in))):
        near_ref[which] = total[:rows, :].astype(near_ref.dtype)
        far_ref[which] = total[rows:, :].astype(BF)
    gb_in = jnp.sum(grad_pre.astype(F32), axis=0, keepdims=True)
    g_out = dot_nn(jnp.transpose(hidden), dy)
    g_in = dot_nn(jnp.transpose(grad_pre), normed)
    if not second:
        g_out_ref, g_in_ref, gb_in_ref = refs
        g_out_ref[...] = g_out.astype(BF)
        g_in_ref[...] = g_in.astype(BF)
        gb_in_ref[...] = gb_in
        return
    g_out_before, g_in_before, gb_in_before = before
    keep_ref, send_ref, gb_in_ref = refs
    gb_in_ref[...] = gb_in + gb_in_before[...]
    g_out = (g_out + g_out_before[...].astype(F32)).astype(BF)
    g_in = (g_in + g_in_before[...].astype(F32)).astype(BF)
    part, half = g_out.shape[0] // SHARDS, g_out.shape[1] // 2
    first = Z_COUNT * part
    for value in (0, 1):

        @pl.when(coords[GRP] == value)
        def _():
            for shard in range(Z_COUNT):
                at, row = 2 * shard * part, shard * part
                for target, pack in ((keep_ref, value), (send_ref, 1 - value)):
                    start = pack * first + row
                    target[at : at + part, :] = g_out[start : start + part, :]
                    lanes = slice(pack * half, (pack + 1) * half)
                    target[at + part : at + 2 * part, :half] = g_in[row : row + part, lanes]
                    target[at + part : at + 2 * part, half:] = g_in[first + row : first + row + part, lanes]


def mlp(coords, pairs, ln_gain, w_in, b_in, w_out, before=()):
    _two, rows, width = pairs[0].shape
    own = w_in.shape[1] // 4
    second = bool(before)
    place = lambda c, side: side * 4 + c[TOP] * 2 + c[CORE]
    columns = lambda rows, side: pl.BlockSpec((rows, own // 2), lambda s, c: (0, place(c, side)))
    outs = [
        struct((2, rows, width), BF if second else F32),
        struct((2, rows, width), BF),
        struct((own, width), BF),
        struct((own, width), BF),
        struct((1, own), F32),
    ]
    return call(
        functools.partial(mlp_kernel, second),
        coords,
        [*pairs, ln_gain, w_in, w_in, b_in, b_in, w_out, w_out, *before],
        [whole((2, rows, width))] * 2
        + [
            whole((1, width)),
            columns(width, 0),
            columns(width, 1),
            columns(1, 0),
            columns(1, 1),
            pl.BlockSpec((own // 2, width), lambda s, c: (place(c, 0), 0)),
            pl.BlockSpec((own // 2, width), lambda s, c: (place(c, 1), 0)),
        ]
        + [whole(array.shape) for array in before],
        outs,
        [whole(out.shape) for out in outs],
        name="mlp",
    )


def qkv_kernel(count, coords, *refs):
    x_refs, refs = refs[:count], refs[count:]
    w_refs, refs = refs[:6], refs[6:]
    gain_ref, q_gain_ref, k_gain_ref, normed_ref, q_ref, first_ref, kv_ref, raw_ref, w_s, turn_s = refs
    rows = x_refs[0].shape[0]
    zeros = jnp.zeros((HD, rows), F32)
    q_gain, k_gain = column(q_gain_ref[...]), column(k_gain_ref[...])
    for i, w_ref in enumerate(w_refs):
        w_s[:, i * 128 : (i + 1) * 128] = w_ref[...]
    for slot in range(count):
        span = slice(slot * rows, (slot + 1) * rows)
        hat, _unused = normalized(x_refs[slot][...].astype(F32), 1)
        normed = (hat * gain_ref[...]).astype(BF)
        normed_ref[span, :] = normed
        projected = dot_nn(normed, w_s[...])
        turn_s[slot] = jnp.transpose(projected)
    for slot in range(count):
        span = slice(slot * rows, (slot + 1) * rows)
        for head in range(PER_Z):
            q_raw, k_raw, v = (
                turn_s[slot, pl.ds(pl.multiple_of(part * 256 + head * HD + coords[Z_LOW] * HD, HD), HD), :]
                for part in range(3)
            )
            raw_ref[head, :HD, span] = q_raw
            raw_ref[head, HD:, span] = k_raw
            q = normalized(q_raw, 0)[0] * q_gain * HD ** (-0.5)
            k = normalized(k_raw, 0)[0] * k_gain
            q_ref[head, span, :] = jnp.transpose(jnp.concatenate([q, zeros], axis=0)).astype(BF)
            target = kv_ref if head else first_ref
            target[max(head - 1, 0), span, :] = jnp.transpose(jnp.concatenate([k, v], axis=0)).astype(BF)


def qkv(coords, blocks, ln_gain, w_qkv, q_gain, k_gain):
    rows, width = blocks[0].shape
    count = len(blocks)
    total = count * rows

    def columns(part, second):
        first = lambda c: 3 * (c[Z_LOW] + 2 * c[Z_HIGH]) // 2
        return pl.BlockSpec((width, 128), lambda i, c: (0, part * (width // 128) + first(c) + second))

    shapes = [
        struct((total, width), BF),
        struct((PER_Z, total, 2 * HD), BF),
        struct((1, total, 2 * HD), BF),
        struct((PER_Z - 1, total, 2 * HD), BF),
        struct((PER_Z, 2 * HD, total), F32),
    ]
    return call(
        functools.partial(qkv_kernel, count),
        coords,
        [*blocks, *[w_qkv] * 6, ln_gain, q_gain, k_gain],
        [whole((rows, width))] * count
        + [columns(part, second) for part in range(3) for second in range(2)]
        + [whole((1, width)), whole((1, HD)), whole((1, HD))],
        shapes,
        [whole(shape.shape) for shape in shapes],
        [pltpu.VMEM((width, 768), BF), pltpu.VMEM((count, 768, rows), F32)],
        name="qkv",
    )


def attention_kernel(groups, slots, sources, coords, *refs):
    count = len(groups)
    q_refs, refs = refs[:count], refs[count:]
    do_refs, refs = refs[:slots], refs[slots:]
    kv_refs, refs = refs[:sources], refs[sources:]
    qi_ref, ki_ref, out_ref, *refs = refs
    dq_ref, low_ref, high_ref, q_s, do_s, kv_s, one_v_s, e_s, acc_s = refs
    rows = sum(groups)
    tokens = rows // slots
    start = 0
    for group, size in enumerate(groups):
        q_s[start : start + size, :] = q_refs[group][0]
        start += size
    lane = lax.broadcasted_iota(jnp.int32, (rows, 2 * HD), 1)
    for source in range(sources):
        block = kv_refs[source][0]
        kv_s[source] = block
        one_v_s[source] = jnp.where(lane < HD, jnp.ones((), BF), block)
    for slot in range(slots):
        grad = do_refs[slot][...].astype(F32)
        do_s[slot * tokens : (slot + 1) * tokens, :] = jnp.transpose(
            jnp.concatenate([jnp.zeros_like(grad), grad], axis=0)
        )
    acc_s[...] = jnp.zeros_like(acc_s)
    query_images = column(qi_ref[...])

    def forward(source, carry):
        scores = dot_nt(q_s[...], kv_s[source])
        same = query_images == ki_ref[source]
        weights = jnp.where(same, jnp.exp(scores), 0.0).astype(BF)
        e_s[source] = weights
        acc_s[...] += dot_nn(weights, one_v_s[source])
        return carry

    lax.fori_loop(0, sources, forward, 0)
    acc = acc_s[...]
    wide = lax.broadcasted_iota(jnp.int32, (rows, 2 * HD), 1)
    attended = jnp.where(wide >= HD, acc / pltpu.roll(acc, HD, 1), 0.0)
    inverse = 1.0 / acc[:, 0:1]
    do = do_s[...]
    out_dot = jnp.sum(do * attended, axis=1, keepdims=True) * inverse
    coarse = out_dot.astype(BF).astype(F32)
    do = do * inverse
    probe = jnp.where(wide == 0, -coarse, jnp.where(wide == 1, coarse - out_dot, do)).astype(BF)
    out_ref[...] = jnp.transpose(attended)[HD:].astype(BF)
    q_t = jnp.transpose(q_s[...].astype(F32))[:HD].astype(BF)
    do_t = jnp.transpose(do)[HD:].astype(BF)
    acc_s[...] = jnp.zeros_like(acc_s)

    def backward_into(dkv_ref, first):
        def backward(source, carry):
            weights = e_s[first + source]
            grad_weights = dot_nt(probe, one_v_s[first + source])
            grad_scores = (weights.astype(F32) * grad_weights).astype(BF)
            acc_s[...] += dot_nn(grad_scores, kv_s[first + source])
            dkv_ref[source, :HD, :] = dot_nn(q_t, grad_scores).astype(BF)
            dkv_ref[source, HD:, :] = dot_nn(do_t, weights).astype(BF)
            return carry

        lax.fori_loop(0, sources // 2, backward, 0)

    backward_into(high_ref, sources // 2)
    backward_into(low_ref, 0)
    dq_ref[...] = jnp.transpose(acc_s[...])[:HD]


def attention(head, coords, q_groups, do_slots, kv_sources, query_images, key_images):
    groups = [q.shape[1] for q in q_groups]
    slots, sources = len(do_slots), len(kv_sources)
    rows = sum(groups)
    parts = [pl.BlockSpec((1, size, 2 * HD), lambda i, c: (head, 0, 0)) for size in groups]
    place = kv_sources[0][1]
    kv_part = pl.BlockSpec((1, rows, 2 * HD), lambda i, c: (place, 0, 0))
    do_part = pl.BlockSpec((HD, rows // slots), lambda i, c: (head, 0))
    half = (sources // 2, 2 * HD, rows)
    return call(
        functools.partial(attention_kernel, groups, slots, sources),
        coords,
        [*q_groups, *do_slots, *[source[0] for source in kv_sources], query_images, key_images],
        parts
        + [do_part] * slots
        + [kv_part] * sources
        + [whole((1, rows)), whole((sources, 1, rows))],
        [struct((HD, rows), BF), struct((HD, rows), F32), struct(half, BF), struct(half, BF)],
        [whole((HD, rows)), whole((HD, rows)), whole(half), whole(half)],
        [
            pltpu.VMEM((rows, 2 * HD), BF),
            pltpu.VMEM((rows, 2 * HD), F32),
            pltpu.VMEM((sources, rows, 2 * HD), BF),
            pltpu.VMEM((sources, rows, 2 * HD), BF),
            pltpu.VMEM((sources, rows, rows), BF),
            pltpu.VMEM((rows, 2 * HD), F32),
        ],
        name="attention",
    )


EXTRA = 16


def post_kernel(groups, slots, terms, heads, coords, *refs):
    count = len(groups)
    per_head = []
    for _head in heads:
        per_head.append((refs[0], refs[1], refs[2 : 2 + terms], refs[2 + terms : 2 + terms + count]))
        refs = refs[2 + terms + count :]
    normed_refs, dy_refs, refs = refs[:count], refs[count : count + slots], refs[count + slots :]
    (q_gain_ref, k_gain_ref, b_in_ref, b_out_ref), refs = refs[:4], refs[4:]
    piece_refs, (keep_ref, send_ref) = refs[:slots], refs[slots:]
    tokens = piece_refs[0].shape[1]
    half = keep_ref.shape[1]
    rows, attn = 3 * HD // 2, HD // 2
    block = len(heads) * rows + EXTRA
    gains = [0.0, 0.0]
    q_gain, k_gain = column(q_gain_ref[...]), column(k_gain_ref[...])
    for place, (dq_ref, out_ref, term_refs, raw_refs) in enumerate(per_head):
        total = attn_total = None
        start = 0
        for group, size in enumerate(groups):
            span = slice(start, start + size)
            dkv = sum(term[0][:, span].astype(F32) for term in term_refs)
            grads = []
            for which, (grad, gain) in enumerate(
                ((dq_ref[:, span], q_gain * HD ** (-0.5)), (dkv[:HD], k_gain))
            ):
                hat, scale = normalized(raw_refs[group][0, which * HD : (which + 1) * HD, :], 0)
                factor = HD ** (-0.5) if which == 0 else 1.0
                gains[which] += jnp.sum(grad * hat, axis=1, keepdims=True) * factor
                grad = grad * gain
                grad = scale * (
                    grad
                    - jnp.mean(grad, axis=0, keepdims=True)
                    - hat * jnp.mean(grad * hat, axis=0, keepdims=True)
                )
                grads.append(grad)
            grads.append(dkv[HD:])
            projected_grad = jnp.concatenate(grads, axis=0).astype(BF)
            first = place * 4 * HD
            for slot in range(start // tokens, (start + size) // tokens):
                inner = slice(slot * tokens - start, (slot + 1) * tokens - start)
                outer = slice(slot * tokens, (slot + 1) * tokens)
                piece_refs[slot][first : first + 3 * HD, :] = projected_grad[:, inner]
                piece_refs[slot][first + 3 * HD : first + 4 * HD, :] = out_ref[:, outer]
                term = dot_nn(out_ref[:, outer], dy_refs[slot][...])
                attn_total = term if attn_total is None else attn_total + term
            term = dot_nn(projected_grad, normed_refs[group][...])
            total = term if total is None else total + term
            start += size
        total, attn_total = total.astype(BF), attn_total.astype(BF)
        for value in (0, 1):

            @pl.when(coords[CORE] == value)
            def _():
                for side in (0, 1):
                    lanes = slice(side * half, (side + 1) * half)
                    at = side * block + place * rows
                    attn_at = 2 * block + (side * len(heads) + place) * attn
                    for target, mine in ((keep_ref, value), (send_ref, 1 - value)):
                        target[at : at + rows, :] = total[mine * rows : (mine + 1) * rows, lanes]
                        target[attn_at : attn_at + attn, :] = attn_total[
                            mine * attn : (mine + 1) * attn, lanes
                        ]

    turned = jnp.transpose(
        jnp.concatenate([jnp.broadcast_to(gain, (HD, 128)) for gain in gains], axis=0)
    )
    line = lax.broadcasted_iota(jnp.int32, (EXTRA, half), 0)
    gain_row = jnp.concatenate([turned[:1], jnp.zeros((1, half - 2 * HD), F32)], axis=1)
    for pack in (0, 1):
        extra = jnp.where(line == 5, gain_row, 0.0)
        if heads[0] == 0:
            extra = jnp.where(line == 0, b_out_ref[:, pack * half : (pack + 1) * half], extra)
            here = line == 1 + 2 * coords[TOP] + coords[CORE]
            extra = jnp.where(here, b_in_ref[:, pack * half : (pack + 1) * half], extra)
        for target in (keep_ref, send_ref):
            target[(pack + 1) * block - EXTRA : (pack + 1) * block, :] = extra.astype(BF)


def post(heads, coords, parts, raw_groups, normed_groups, dy_slots, q_gain, k_gain, gb_in, gb_out):
    groups = [raw.shape[2] for raw in raw_groups]
    width = normed_groups[0].shape[1]
    rows = sum(groups)
    slots = len(dy_slots)
    tokens = rows // slots
    count = len(heads)
    terms = len(parts[0][2])
    piece = (count * 4 * HD, tokens)
    share = (2 * (count * 3 * HD // 2 + EXTRA) + count * HD, width // 2)
    inputs, specs = [], []
    for head, (dq, out, added) in zip(heads, parts, strict=True):
        inputs += [dq, out, *added, *raw_groups]
        specs += [whole((HD, rows))] * 2 + [whole((1, 2 * HD, rows))] * terms
        specs += [
            pl.BlockSpec((1, 2 * HD, size), functools.partial(lambda h, i, c: (h, 0, 0), head))
            for size in groups
        ]
    return call(
        functools.partial(post_kernel, groups, slots, terms, heads),
        coords,
        [*inputs, *normed_groups, *dy_slots, q_gain, k_gain, gb_in, gb_out],
        specs
        + [whole((size, width)) for size in groups]
        + [whole((tokens, width))] * slots
        + [whole((1, HD))] * 2
        + [whole((1, width))] * 2,
        [struct(piece, BF)] * slots + [struct(share, BF)] * 2,
        [whole(piece)] * slots + [whole(share)] * 2,
        name="post",
        us=18 if heads == [1] else 0,
    )


def head_of(coords, slot_shift, head):
    z_index = coords[Z_LOW] + 2 * coords[Z_HIGH]
    return lax.rem(z_index + slot_shift, Z_COUNT) * PER_Z + head


def piece_of(pieces, slot, head, part):
    return pieces[Z_COUNT * head + slot][part * HD : (part + 1) * HD, :]


def output_kernel(shifts, coords, *refs):
    count = PER_Z * Z_COUNT
    pieces, refs = refs[:count], refs[count:]
    x_ref, near_ref, far_ref, back_ref, b_ref, w_ref, out_ref, att_s = refs
    for head in range(PER_Z):
        for slot, shift in enumerate(shifts):
            row = pl.multiple_of(head_of(coords, shift, head) * HD, HD)
            att_s[pl.ds(row, HD), :] = piece_of(pieces, slot, head, 3)
    out_ref[...] = (
        x_ref[...].astype(F32)
        + near_ref[0]
        + far_ref[0].astype(F32)
        + back_ref[0].astype(F32)
        + b_ref[...]
        + dot_nn(jnp.transpose(att_s[...]), w_ref[...])
    ).astype(BF)


def block_output(coords, shifts, pieces, x, near, far, back, b_out, w_attn_out):
    rows, width = x.shape
    one = whole((1, rows, width))
    return call(
        functools.partial(output_kernel, shifts),
        coords,
        [*pieces, x, near, far, back, b_out, w_attn_out],
        [whole(piece.shape) for piece in pieces]
        + [whole((rows, width)), one, one, one]
        + [whole((1, width)), whole((width, width))],
        struct((rows, width), BF),
        whole((rows, width)),
        [pltpu.VMEM((width, rows), BF)],
        name="block_output",
    )


def tokens_kernel(shifts, coords, *refs):
    count = PER_Z * Z_COUNT
    pieces, refs = refs[:count], refs[count:]
    x_ref, dy_ref, gain_ref, near_ref, far_ref, back_ref, w_ref, out_ref, grad_s = refs
    width = x_ref.shape[1]
    for head in range(PER_Z):
        for slot, shift in enumerate(shifts):
            row = pl.multiple_of(head_of(coords, shift, head) * HD, HD)
            for part in range(3):
                grad_s[pl.ds(part * width + row, HD), :] = piece_of(pieces, slot, head, part)
    normed_grad = (
        near_ref[0]
        + far_ref[0].astype(F32)
        + back_ref[0].astype(F32)
        + dot_nt(jnp.transpose(grad_s[...]), w_ref[...])
    )
    hat, scale = normalized(x_ref[...].astype(F32), 1)
    grad = normed_grad * gain_ref[...]
    out_ref[...] = dy_ref[...].astype(F32) + scale * (
        grad
        - jnp.mean(grad, axis=1, keepdims=True)
        - hat * jnp.mean(grad * hat, axis=1, keepdims=True)
    )


def token_gradient(coords, shifts, pieces, x, dy, ln_gain, near, far, back, w_qkv):
    rows, width = x.shape
    one = pl.BlockSpec((1, rows, width), lambda i, c: (1, 0, 0))
    return call(
        functools.partial(tokens_kernel, shifts),
        coords,
        [*pieces, x, dy, ln_gain, near, far, back, w_qkv],
        [whole(piece.shape) for piece in pieces]
        + [whole((rows, width))] * 2
        + [whole((1, width)), one, one, one]
        + [whole(w_qkv.shape)],
        struct((rows, width), F32),
        whole((rows, width)),
        [pltpu.VMEM((3 * width, rows), BF)],
        name="token_gradient",
    )


HALVE, BOTH, KEEP = range(3)


def stage_kernel(segments, bit, coords, keep_ref, came_ref, *out_refs):
    keep_at = came_at = kept = sent = 0
    for rows, came, mode in segments:
        total = keep_ref[keep_at : keep_at + rows, :]
        if came:
            total = (total.astype(F32) + came_ref[came_at : came_at + rows, :].astype(F32)).astype(BF)
            came_at += rows
        keep_at += rows
        if mode == HALVE:
            half = rows // 2
            for value in (0, 1):

                @pl.when(coords[bit] == value)
                def _():
                    out_refs[0][kept : kept + half, :] = total[value * half : (value + 1) * half]
                    out_refs[1][sent : sent + half, :] = total[(1 - value) * half : (2 - value) * half]

            kept += half
            sent += half
        else:
            out_refs[0][kept : kept + rows, :] = total
            kept += rows
            if mode == BOTH:
                out_refs[1][sent : sent + rows, :] = total
                sent += rows


def stage(coords, segments, bit, keep, came):
    width = keep.shape[1]
    kept = sum(rows // 2 if mode == HALVE else rows for rows, _came, mode in segments)
    sent = sum({HALVE: rows // 2, BOTH: rows, KEEP: 0}[mode] for rows, _came, mode in segments)
    shapes = [(kept, width)] + ([(sent, width)] if sent else [])
    return call(
        functools.partial(stage_kernel, segments, bit),
        coords,
        [keep, came],
        [whole(keep.shape), whole(came.shape)],
        [struct(shape, BF) for shape in shapes],
        [whole(shape) for shape in shapes],
        name="stage",
    )


def first_stage_kernel(counts, coords, *refs):
    (*shares, keep_ref, send_ref) = refs
    attn, rows = HD // 2, 3 * HD // 2
    blocks = [count * rows + EXTRA for count in counts]
    pairs = list(zip(blocks, counts, shares[::2], shares[1::2], strict=True))
    for value in (0, 1):

        @pl.when(coords[GRP] == value)
        def _():
            for pack, target in ((value, keep_ref), (1 - value, send_ref)):
                extra, at = 0.0, 0
                for block, count, own, came in pairs:
                    span = slice(pack * block, (pack + 1) * block)
                    total = own[span, :].astype(F32) + came[span, :].astype(F32)
                    target[at : at + count * rows, :] = total[: count * rows].astype(BF)
                    extra = extra + total[count * rows :]
                    at += count * rows
                target[PER_Z * (rows + 2 * attn) :, :] = extra.astype(BF)

    before = 0
    for block, count, own, came in pairs:
        total = (own[2 * block :, :].astype(F32) + came[2 * block :, :].astype(F32)).astype(BF)
        for side in (0, 1):
            start = PER_Z * rows + (side * PER_Z + before) * attn
            for target in (keep_ref, send_ref):
                target[start : start + count * attn, :] = total[
                    side * count * attn : (side + 1) * count * attn
                ]
        before += count


def first_stage(coords, counts, shares):
    half = shares[0].shape[1]
    shape = (PER_Z * (3 * HD // 2 + HD) + EXTRA, half)
    return call(
        functools.partial(first_stage_kernel, counts),
        coords,
        shares,
        [whole(share.shape) for share in shares],
        [struct(shape, BF)] * 2,
        [whole(shape)] * 2,
        name="first_stage",
    )


def mlp_place_kernel(coords, *refs):
    units, (w_ref, rows_ref, columns_ref, sum_ref, turn_s) = refs[:4], refs[4:]
    step = pl.program_id(0)
    part, half = units[0].shape[1] // 2, units[0].shape[2] // 2
    here = coords[Z_LOW] * 2 + coords[Z_HIGH]

    @pl.when(step == 0)
    def _():
        sum_ref[...] = jnp.zeros_like(sum_ref)

    chosen = (step % 2 ^ coords[CORE]) * 2 + (step // 2 ^ coords[TOP])
    for i, unit in enumerate(units):

        @pl.when(chosen == i)
        def _():
            for shard in range(Z_COUNT):
                rows_ref[shard * part : (shard + 1) * part, :] = unit[shard ^ here, :part, :].astype(F32)

    lanes = pl.ds(pl.multiple_of((step // 2) * half, 128), half)
    chosen = coords[CORE] * 2 + (step % 2 ^ coords[TOP])
    for i in range(4):

        @pl.when(chosen == i)
        def _():
            for core in (0, 1):
                unit = units[i ^ (2 * core)]
                for shard in range(Z_COUNT):
                    row = (core * Z_COUNT + shard) * part
                    turn_s[row : row + part, :] = unit[shard ^ here, part:, lanes].astype(F32)

    total = 0.0
    for block in range(SHARDS * part // 128):
        span = slice(block * 128, (block + 1) * 128)
        turned = jnp.transpose(turn_s[span, :])
        columns_ref[:, span] = turned
        total = total + turned * w_ref[:, span].astype(F32)
    sum_ref[...] += jnp.sum(total, axis=1, keepdims=True)


def place_mlp(coords, units, w_in):
    _shards, rows, width = units[0].shape
    part, half = rows // 2, width // 2
    span = SHARDS * part
    return call(
        mlp_place_kernel,
        coords,
        [*units, w_in],
        [whole(unit.shape) for unit in units]
        + [pl.BlockSpec((half, span), lambda s, c: (c[GRP], s))],
        [
            struct((2 * span, width), F32),
            struct((half, 4 * span), F32),
            struct((half, 1), F32),
        ],
        [
            pl.BlockSpec((Z_COUNT * part, width), lambda s, c: (s, 0)),
            pl.BlockSpec((half, span), lambda s, c: (0, s)),
            whole((half, 1)),
        ],
        [pltpu.VMEM((span, half), F32)],
        grid=(4,),
        name="place_mlp",
    )


def heads_kernel(coords, *refs):
    (*unit_refs, w_ref, gain_ref, sum_ref, qkv_ref, attn_ref, ln_ref, turn_s) = refs
    half = unit_refs[0].shape[2]
    width = 2 * half
    q_rows, a_rows, unit = 3 * PER_Z * HD // 4, PER_Z * HD // 2, 16
    per_head = 3 * HD // 2 // unit
    for relative in range(8):
        block = unit_refs[relative // 2][relative % 2].astype(F32)
        core = coords[CORE] ^ (relative // 4)
        top = coords[TOP] ^ (relative // 2 % 2)
        low = coords[Z_LOW] ^ (relative % 2)
        for side in (0, 1):
            z_index = low + 2 * (coords[Z_HIGH] ^ side)
            for i in range(q_rows // unit):
                number = top * (q_rows // unit) + i
                inner = number % per_head + core * per_head
                row = (inner // (HD // unit)) * width + (inner % (HD // unit)) * unit
                row = row + (z_index * PER_Z + number // per_head) * HD
                turn_s[pl.ds(pl.multiple_of(row, unit), unit), :] = block[
                    side * q_rows + i * unit : side * q_rows + (i + 1) * unit
                ]
        lanes = pl.ds(pl.multiple_of(top * half, 128), half)
        for head in range(PER_Z):
            row = pl.multiple_of((low * PER_Z + head) * HD + core * (HD // 2), HD // 2)
            start = 2 * q_rows + head * (HD // 2)
            attn_ref[pl.ds(row, HD // 2), lanes] = block[start : start + HD // 2]
    total = 0.0
    for block in range(3 * width // 128):
        span = slice(block * 128, (block + 1) * 128)
        turned = jnp.transpose(turn_s[span, :])
        qkv_ref[:, span] = turned
        total = total + turned * w_ref[:, span].astype(F32)
    ln = (jnp.sum(total, axis=1, keepdims=True) + sum_ref[...]) / gain_ref[...]
    ln_ref[...] = jnp.transpose(jnp.broadcast_to(ln, (half, 128)))[0]


def place_heads(coords, units, w_qkv, gain_column, in_sums):
    half = units[0].shape[2]
    width = 2 * half
    row_half = lambda columns: pl.BlockSpec((half, columns), lambda s, c: (c[GRP], 0))
    return call(
        heads_kernel,
        coords,
        [*units, w_qkv, gain_column, in_sums],
        [whole(unit.shape) for unit in units] + [row_half(3 * width), row_half(1), whole((half, 1))],
        [struct((half, 3 * width), F32), struct((half, width), F32), struct((half,), F32)],
        [whole((half, 3 * width)), whole((half, width)), whole((half,))],
        [pltpu.VMEM((3 * width, half), F32)],
        name="place_heads",
    )


def per_device(
    tokens, lengths, image_ids, ln_gain, w_qkv, q_gain, k_gain,
    w_attn_out, w_in, b_in, w_mlp_out, b_out, cotangent,
):
    x, dy = tokens[0], cotangent[0]
    rows, width = x.shape
    half = width // 2
    hidden = w_in.shape[1]
    seq_count = lax.axis_size("seq")
    rest = seq_count // Z_COUNT
    rest_bits = rest.bit_length() - 1
    top_bit = rest_bits - 1
    me = lax.axis_index("seq")
    z_index, r_index = me // rest, me % rest
    grp = lax.axis_index("grp")
    core, top = r_index & 1, r_index >> top_bit
    coords = jnp.stack([grp, core, top, z_index & 1, z_index >> 1]).astype(jnp.int32)

    def z_shift(block, distance):
        route = [(i, (i + distance * rest) % seq_count) for i in range(seq_count)]
        return lax.ppermute(block, "seq", route)

    def flip(mask):
        route = [(i, i ^ mask) for i in range(seq_count)]
        return lambda block: lax.ppermute(block, "seq", route)

    def swap_packs(block):
        return lax.ppermute(block, "grp", [(0, 1), (1, 0)])

    swap_core, swap_top = flip(1), flip(1 << top_bit)
    swap_low, swap_high = flip(rest), flip(2 * rest)
    others = range(1, top_bit)

    def add(*terms):
        return sum(term.astype(F32) for term in terms).astype(BF)

    def after(value, *events):
        return lax.optimization_barrier((value, *events))[0]

    def after(value, *events):
        return lax.optimization_barrier((value, *events))[0]

    turn = [coords]

    def then(results):
        if isinstance(results, (list, tuple)):
            return [then(results[0]), *results[1:]]
        turn[0], results = lax.optimization_barrier((turn[0], results))
        return results

    def until(*events):
        turn[0] = after(turn[0], *events)

    shifts = [0, 1, 3, 2]
    x_slots = {0: x, **{d: z_shift(x, d) for d in (1, 3, 2)}}
    mine, gb_out, *do_pieces = then(prep(coords, shifts, x, dy, w_attn_out))
    across, other = swap_top(mine), swap_core(mine)
    mlp_weights = (ln_gain.reshape(1, width), w_in, b_in.reshape(1, hidden), w_mlp_out)
    near, near_far, *before = then(mlp(turn[0], [mine, other], *mlp_weights))
    near_far = swap_core(near_far)

    order = image_ids[0]
    labels = jnp.arange(order.shape[0], dtype=jnp.int32)
    ordered = jnp.sum(jnp.where(order[:, None] == labels[None, :], lengths[0][None, :], 0), axis=1)
    ends = jnp.cumsum(ordered)
    offsets = jnp.arange(rows, dtype=jnp.int32)
    slot_z = (z_index - jnp.array(shifts, dtype=jnp.int32)) % Z_COUNT
    masks = [2 * i for i in range(rest // 2)] + [2 * i + 1 for i in range(rest // 2)]
    source_r = r_index ^ jnp.array(masks, dtype=jnp.int32)
    starts = (slot_z[None, :] * rest + source_r[:, None]) * rows
    places = (starts[:, :, None] + offsets).reshape(rest, Z_COUNT * rows)
    images = jnp.sum((places[:, :, None] >= ends).astype(jnp.int32), axis=2).astype(F32)
    key_images = images[:, None, :]
    query_images = images[:1]

    ln_row = ln_gain.reshape(1, width)
    q_col, k_col = q_gain.reshape(1, HD), k_gain.reshape(1, HD)

    until(across)
    normed, q, kv_first, kv_rest, raw = then(
        qkv(turn[0], [x_slots[d] for d in shifts], ln_row, w_qkv, q_col, k_col)
    )
    normed_groups, q_groups, raw_groups = [normed], [q], [raw]

    def spread(group, bits):
        for bit in bits:
            group = {**group, **{m | 1 << bit: flip(1 << bit)(block) for m, block in group.items()}}
        return group

    upper = list(reversed(range(1, rest_bits)))
    kv_first = spread({0: kv_first}, upper)
    do_slots = [
        z_shift(after(piece, normed), d) if d else piece
        for piece, d in zip(do_pieces, shifts, strict=True)
    ]
    mid, far, mlp_keep, mlp_send, gb_in = then(
        mlp(turn[0], [across, swap_core(after(across, near))], *mlp_weights, before)
    )
    mlp_came = swap_packs(mlp_send)
    kv_first = spread({m: after(block, mlp_keep, *do_slots[1:]) for m, block in kv_first.items()}, [0])
    kv_rest = spread({0: after(kv_rest, kv_first[1 << top_bit])}, upper)
    dy_slots = {0: dy, **{d: z_shift(after(dy, mlp_keep), d) for d in (1, 3)}}

    pieces, shares = [], []

    def finish(heads, parts):
        results = then(
            post(
                heads, turn[0], parts, raw_groups, normed_groups,
                dy_list, q_col, k_col, gb_in, gb_out,
            )
        )
        for slot, d in enumerate(shifts):
            pieces.append(z_shift(results[slot], -d) if d else results[slot])
        shares.extend([results[Z_COUNT], swap_core(results[Z_COUNT + 1])])

    waiting = []

    def halve(keep, came, bit, move):
        size = keep.shape[0] // 2
        rows_of = lambda array, which: lax.dynamic_slice_in_dim(array, which * size, size, 0)
        gone = then(add(rows_of(keep, 1 - bit), rows_of(came, 1 - bit)))
        keep = then(add(rows_of(keep, bit), rows_of(came, bit)))
        return keep, move(gone)

    far = swap_core(far)
    kv_sources = [[(kv_first[m], 0) for m in masks]]
    for head in range(PER_Z):
        out_t, dq_t, low, high = then(
            attention(head, turn[0], q_groups, do_slots, kv_sources[head], query_images, key_images)
        )
        if head == 0:
            high = after(high, kv_rest[1 << top_bit])
            kv_rest = spread({m: after(block, dq_t) for m, block in kv_rest.items()}, [0])
            kv_sources += [[(kv_rest[m], place) for m in masks] for place in (0, 1)]
            high = after(high, dy_slots[1], dy_slots[3])
            dy_slots[2] = z_shift(after(dy, dq_t), 2)
        if head:
            high = after(high, mlp_came, *waiting[-1][2][2:])
        if head == 1:
            high = after(high, dy_slots[2])
            dy_list = [dy_slots[d] for d in shifts]
        if head == 2:
            high = after(high, *pieces)
            mlp_share = then(add(after(mlp_keep, turn[0]), mlp_came))
            for bit in others:
                mlp_share = add(mlp_share, flip(1 << bit)(mlp_share))
            mlp_units = mlp_share[None]
            mlp_came = swap_high(mlp_units)
        came = swap_core(high)
        if head == 1:
            mlp_keep, mlp_came = halve(after(mlp_keep, turn[0]), mlp_came, z_index >> 1, swap_high)
        parts = {2 * i: [low[i : i + 1], came[i : i + 1]] for i in range(rest // 2)}
        for bit in range(1, rest_bits):
            for mask in sorted(m for m in parts if m >> bit & 1):
                total = then(add(*parts.pop(mask)))
                parts[mask ^ (1 << bit)].append(flip(1 << bit)(total))
        if head == 0:
            mlp_keep, mlp_came = halve(after(mlp_keep, turn[0]), mlp_came, z_index & 1, swap_low)
        waiting.append((dq_t, out_t, [low, came, *parts[0][2:]]))
        if head == 1:
            finish([0], waiting[:1])
    finish([1], waiting[1:2])
    back = swap_top(add(after(mid, waiting[2][2][2]), far))
    finish([2], waiting[2:])
    until(mlp_came)

    keep, send = then(first_stage(turn[0], [1, 1, 1], shares))
    q_size, a_size = 3 * PER_Z * HD // 2, PER_Z * HD
    came = swap_packs(send)
    near_parts = (near, near_far, back)
    mlp_units = then(jnp.concatenate([mlp_units, mlp_came], axis=0))
    mlp_came = swap_low(mlp_units)
    until(*pieces[Z_COUNT + 1 : 2 * Z_COUNT])
    keep, send = then(
        stage(
            turn[0],
            [(q_size, True, HALVE), (a_size, True, HALVE), (EXTRA, True, BOTH)],
            TOP, keep, came,
        )
    )
    q_size, a_size = q_size // 2, a_size // 2
    came = swap_top(send)
    share = then(add(keep, came))
    for bit in others:
        share = add(share, flip(1 << bit)(share))
    came = swap_high(share)
    mlp_units = then(jnp.concatenate([after(mlp_units, turn[0]), mlp_came], axis=0))
    mlp_came = swap_top(mlp_units)
    result = then(
        block_output(
            turn[0], shifts, pieces, x, *near_parts, b_out.reshape(1, width), w_attn_out
        )
    )
    came = after(came, result)
    middle = q_size + a_size
    attn = jnp.where(z_index >> 1 == grp, share[q_size:middle], came[q_size:middle])
    small = add(share[middle:], came[middle:])
    unit = then(jnp.concatenate([share[:q_size], came[:q_size], attn, small], axis=0))
    came = swap_low(unit)
    grad_tokens = then(
        token_gradient(turn[0], shifts, pieces, x, dy, ln_row, *near_parts, w_qkv)
    )
    came = after(came, grad_tokens)
    size = unit.shape[0] - EXTRA
    small = add(unit[size:], came[size:]).astype(F32)
    units = then(jnp.stack([unit[:size], came[:size]]))
    came = swap_top(units)
    mlp_came = after(mlp_came, units)
    mlp_units = [mlp_units, mlp_came, swap_core(mlp_units), swap_core(mlp_came)]
    grad_w_mlp_out, grad_w_in, in_sums = then(place_mlp(turn[0], mlp_units, w_in))
    came = after(came, grad_w_in)
    all_units = [units, came, swap_core(units), swap_core(came)]

    grad_w_qkv, grad_w_attn_out, grad_ln_gain = place_heads(
        coords, all_units, w_qkv, ln_gain.reshape(width, 1), in_sums
    )
    return (
        result[None],
        grad_tokens[None],
        grad_ln_gain,
        grad_w_qkv,
        lax.dynamic_slice(small[5], (grp * (HD // 2),), (HD // 2,)),
        lax.dynamic_slice(small[5], (HD + grp * (HD // 2),), (HD // 2,)),
        grad_w_attn_out,
        grad_w_in,
        small[1:5].reshape(hidden // 2),
        grad_w_mlp_out,
        small[0],
    )


def solution(mesh):
    placed = (
        P("grp", "seq", None), P("grp", None), P("grp", None),
        P(), P(), P(), P(), P(), P(), P(), P(), P(), P("grp", "seq", None),
    )
    return jax.shard_map(
        per_device,
        mesh=mesh,
        in_specs=placed,
        out_specs=(
            P("grp", "seq", None), P("grp", "seq", None), P("grp"), P("grp", None), P("grp"),
            P("grp"), P("grp", None), P("grp", None), P("grp"), P("grp", None), P("grp"),
        ),
        check_vma=False,
    )
```

```python
import functools

import jax
import jax.numpy as jnp
from jax import lax
from jax.experimental import pallas as pl
from jax.experimental.pallas import tpu as pltpu
from jax.sharding import PartitionSpec as P

H = 12
HD = 64
Z_COUNT = 4
PER_Z = H // Z_COUNT
EPSILON = 1e-06
BF = jnp.bfloat16
F32 = jnp.float32
VMEM_BYTES = 58 * 1024 * 1024
FLOPS_PER_US = 1_150_000_000


def params():
    return pltpu.CompilerParams(vmem_limit_bytes=VMEM_BYTES)


def dot_nn(left, right):
    return lax.dot_general(left, right, (((1,), (0,)), ((), ())), preferred_element_type=F32)


def dot_nt(left, right):
    return lax.dot_general(left, right, (((1,), (1,)), ((), ())), preferred_element_type=F32)


def dot_tn(left, right):
    return lax.dot_general(left, right, (((0,), (0,)), ((), ())), preferred_element_type=F32)


def whole(shape):
    return pl.BlockSpec(shape, lambda *_: (0,) * len(shape))


def normalized(values, axis):
    mean = jnp.mean(values, axis=axis, keepdims=True)
    centred = values - mean
    spread = jnp.mean(centred * centred, axis=axis, keepdims=True)
    scale = lax.rsqrt(spread + EPSILON)
    return centred * scale, scale


GRP, CORE, TOP, Z_LOW, Z_HIGH = range(5)
SHARDS = 8


OPT = {
    "prep": 18,
    "mlp1": 0,
    "mlp2": 40,
    "qkv": 5,
    "attention0": 18,
    "attention1": 18,
    "attention2": 18,
    "post01": 18,
    "post2": 0,
    "first_stage": 0,
    "stage": 0,
    "block_output": 5,
    "token_gradient": 6,
    "place_mlp": 9,
    "place_heads": 8,
    "x2": 0,
    "across": 0,
    "order": 0,
    "do_tie": 2,
    "do_use": 1,
    "core_tie": 1,
    "dy_tie": 1,
    "near": 2,
    "back": 1,
    "mlp_early": 0,
    "mlp_first": 0,
    "zh_tie": 1,
    "far_piece": 0,
    "far_use": 0,
    "zl_use": 2,
    "topb": 1,
    "p_use": 3,
    "unit_tie": 1,
    "place_at": 1,
    "out_at": 2,
    "tokens_at": 2,
    "concat_at": 1,
    "p_tie": 3,
    "img": 1
}


def cost(us):
    return pl.CostEstimate(flops=us * FLOPS_PER_US, bytes_accessed=0, transcendentals=0)


def call(body, scalars, inputs, in_specs, out_shapes, out_specs, scratch=(), grid=(1,), name=None, us=0):
    return pl.pallas_call(
        body,
        grid_spec=pltpu.PrefetchScalarGridSpec(
            num_scalar_prefetch=1,
            grid=grid,
            in_specs=in_specs,
            out_specs=out_specs,
            scratch_shapes=list(scratch),
        ),
        out_shape=out_shapes,
        compiler_params=params(),
        cost_estimate=cost(OPT.get(name, us)),
        name=name,
    )(scalars, *inputs)


def struct(shape, dtype):
    return jax.ShapeDtypeStruct(shape, dtype)


def column(row):
    return jnp.transpose(jnp.broadcast_to(row, (8, row.shape[1])))[:, :1]


def prep_kernel(shifts, coords, x_ref, dy_ref, w_ref, pair_ref, sum_ref, *refs):
    out_refs, grad_s = refs[:-1], refs[-1]
    pair_ref[0] = x_ref[...]
    dy = dy_ref[...]
    pair_ref[1] = dy
    sum_ref[...] = jnp.sum(dy.astype(F32), axis=0, keepdims=True)
    grad_s[...] = dot_nt(w_ref[...], dy).astype(BF)
    z_index = coords[Z_LOW] + 2 * coords[Z_HIGH]
    depth = PER_Z * HD
    for shift, out_ref in zip(shifts, out_refs, strict=True):
        row = pl.multiple_of(lax.rem(z_index + shift, Z_COUNT) * depth, depth)
        out_ref[...] = grad_s[pl.ds(row, depth), :]


def prep(coords, shifts, x, dy, w_attn_out):
    rows, width = dy.shape
    piece = (PER_Z * HD, rows)
    return call(
        functools.partial(prep_kernel, shifts),
        coords,
        [x, dy, w_attn_out],
        [whole((rows, width))] * 2 + [whole((width, width))],
        [struct((2, rows, width), BF), struct((1, width), F32)] + [struct(piece, BF)] * len(shifts),
        [whole((2, rows, width)), whole((1, width))] + [whole(piece)] * len(shifts),
        [pltpu.VMEM((width, rows), BF)],
        name="prep",
    )


def mlp_kernel(second, coords, *refs):
    pairs, refs = refs[:2], refs[2:]
    gain_ref, w_in_refs, b_in_refs, w_out_refs, refs = refs[0], refs[1:3], refs[3:5], refs[5:7], refs[7:]
    w_in = jnp.concatenate([ref[...] for ref in w_in_refs], axis=1)
    b_in = jnp.concatenate([ref[...] for ref in b_in_refs], axis=1)
    w_out = jnp.concatenate([ref[...] for ref in w_out_refs], axis=0)
    before, refs = (refs[:3], refs[3:]) if second else ((), refs)
    (near_ref, far_ref), refs = refs[:2], refs[2:]
    rows = pairs[0].shape[1]
    normed = []
    for pair in pairs:
        hat, _unused = normalized(pair[0].astype(F32), 1)
        normed.append((hat * gain_ref[...]).astype(BF))
    normed = jnp.concatenate(normed, axis=0)
    dy = jnp.concatenate([pair[1] for pair in pairs], axis=0)
    pre = dot_nn(normed, w_in) + b_in
    square = pre * pre
    tanh = jnp.tanh(pre * (0.7978845608028654 + 0.03567740813630193 * square))
    half = 0.5 + 0.5 * tanh
    hidden = (pre * half).astype(BF)
    slope = half + pre * (0.5 - 0.5 * tanh * tanh) * (
        0.7978845608028654 + 0.10703222440890579 * square
    )
    grad_pre = (slope * dot_nt(dy, w_out)).astype(BF)
    for which, total in enumerate((dot_nn(hidden, w_out), dot_nt(grad_pre, w_in))):
        near_ref[which] = total[:rows, :].astype(near_ref.dtype)
        far_ref[which] = total[rows:, :].astype(BF)
    gb_in = jnp.sum(grad_pre.astype(F32), axis=0, keepdims=True)
    g_out = dot_nn(jnp.transpose(hidden), dy)
    g_in = dot_nn(jnp.transpose(grad_pre), normed)
    if not second:
        g_out_ref, g_in_ref, gb_in_ref = refs
        g_out_ref[...] = g_out.astype(BF)
        g_in_ref[...] = g_in.astype(BF)
        gb_in_ref[...] = gb_in
        return
    g_out_before, g_in_before, gb_in_before = before
    keep_ref, send_ref, gb_in_ref = refs
    gb_in_ref[...] = gb_in + gb_in_before[...]
    g_out = (g_out + g_out_before[...].astype(F32)).astype(BF)
    g_in = (g_in + g_in_before[...].astype(F32)).astype(BF)
    part, half = g_out.shape[0] // SHARDS, g_out.shape[1] // 2
    first = Z_COUNT * part
    for value in (0, 1):

        @pl.when(coords[GRP] == value)
        def _():
            for shard in range(Z_COUNT):
                at, row = 2 * shard * part, shard * part
                for target, pack in ((keep_ref, value), (send_ref, 1 - value)):
                    start = pack * first + row
                    target[at : at + part, :] = g_out[start : start + part, :]
                    lanes = slice(pack * half, (pack + 1) * half)
                    target[at + part : at + 2 * part, :half] = g_in[row : row + part, lanes]
                    target[at + part : at + 2 * part, half:] = g_in[first + row : first + row + part, lanes]


def mlp(coords, pairs, ln_gain, w_in, b_in, w_out, before=()):
    _two, rows, width = pairs[0].shape
    own = w_in.shape[1] // 4
    second = bool(before)
    place = lambda c, side: side * 4 + c[TOP] * 2 + c[CORE]
    columns = lambda rows, side: pl.BlockSpec((rows, own // 2), lambda s, c: (0, place(c, side)))
    outs = [
        struct((2, rows, width), BF if second else F32),
        struct((2, rows, width), BF),
        struct((own, width), BF),
        struct((own, width), BF),
        struct((1, own), F32),
    ]
    return call(
        functools.partial(mlp_kernel, second),
        coords,
        [*pairs, ln_gain, w_in, w_in, b_in, b_in, w_out, w_out, *before],
        [whole((2, rows, width))] * 2
        + [
            whole((1, width)),
            columns(width, 0),
            columns(width, 1),
            columns(1, 0),
            columns(1, 1),
            pl.BlockSpec((own // 2, width), lambda s, c: (place(c, 0), 0)),
            pl.BlockSpec((own // 2, width), lambda s, c: (place(c, 1), 0)),
        ]
        + [whole(array.shape) for array in before],
        outs,
        [whole(out.shape) for out in outs],
        name="mlp2" if second else "mlp1",
    )


def qkv_kernel(count, coords, *refs):
    x_refs, refs = refs[:count], refs[count:]
    w_refs, refs = refs[:6], refs[6:]
    gain_ref, q_gain_ref, k_gain_ref, normed_ref, q_ref, first_ref, kv_ref, raw_ref, w_s, turn_s = refs
    rows = x_refs[0].shape[0]
    zeros = jnp.zeros((HD, rows), F32)
    q_gain, k_gain = column(q_gain_ref[...]), column(k_gain_ref[...])
    for i, w_ref in enumerate(w_refs):
        w_s[:, i * 128 : (i + 1) * 128] = w_ref[...]
    for slot in range(count):
        span = slice(slot * rows, (slot + 1) * rows)
        hat, _unused = normalized(x_refs[slot][...].astype(F32), 1)
        normed = (hat * gain_ref[...]).astype(BF)
        normed_ref[span, :] = normed
        projected = dot_nn(normed, w_s[...])
        turn_s[slot] = jnp.transpose(projected)
    for slot in range(count):
        span = slice(slot * rows, (slot + 1) * rows)
        for head in range(PER_Z):
            q_raw, k_raw, v = (
                turn_s[slot, pl.ds(pl.multiple_of(part * 256 + head * HD + coords[Z_LOW] * HD, HD), HD), :]
                for part in range(3)
            )
            raw_ref[head, :HD, span] = q_raw
            raw_ref[head, HD:, span] = k_raw
            q = normalized(q_raw, 0)[0] * q_gain * HD ** (-0.5)
            k = normalized(k_raw, 0)[0] * k_gain
            q_ref[head, span, :] = jnp.transpose(jnp.concatenate([q, zeros], axis=0)).astype(BF)
            target = kv_ref if head else first_ref
            target[max(head - 1, 0), span, :] = jnp.transpose(jnp.concatenate([k, v], axis=0)).astype(BF)


def qkv(coords, blocks, ln_gain, w_qkv, q_gain, k_gain):
    rows, width = blocks[0].shape
    count = len(blocks)
    total = count * rows

    def columns(part, second):
        first = lambda c: 3 * (c[Z_LOW] + 2 * c[Z_HIGH]) // 2
        return pl.BlockSpec((width, 128), lambda i, c: (0, part * (width // 128) + first(c) + second))

    shapes = [
        struct((total, width), BF),
        struct((PER_Z, total, 2 * HD), BF),
        struct((1, total, 2 * HD), BF),
        struct((PER_Z - 1, total, 2 * HD), BF),
        struct((PER_Z, 2 * HD, total), F32),
    ]
    return call(
        functools.partial(qkv_kernel, count),
        coords,
        [*blocks, *[w_qkv] * 6, ln_gain, q_gain, k_gain],
        [whole((rows, width))] * count
        + [columns(part, second) for part in range(3) for second in range(2)]
        + [whole((1, width)), whole((1, HD)), whole((1, HD))],
        shapes,
        [whole(shape.shape) for shape in shapes],
        [pltpu.VMEM((width, 768), BF), pltpu.VMEM((count, 768, rows), F32)],
        name="qkv",
    )


def attention_kernel(groups, slots, sources, coords, *refs):
    count = len(groups)
    q_refs, refs = refs[:count], refs[count:]
    do_refs, refs = refs[:slots], refs[slots:]
    kv_refs, refs = refs[:sources], refs[sources:]
    qi_ref, ki_ref, out_ref, *refs = refs
    dq_ref, low_ref, high_ref, q_s, do_s, kv_s, one_v_s, e_s, acc_s = refs
    rows = sum(groups)
    tokens = rows // slots
    start = 0
    for group, size in enumerate(groups):
        q_s[start : start + size, :] = q_refs[group][0]
        start += size
    lane = lax.broadcasted_iota(jnp.int32, (rows, 2 * HD), 1)
    for source in range(sources):
        block = kv_refs[source][0]
        kv_s[source] = block
        one_v_s[source] = jnp.where(lane < HD, jnp.ones((), BF), block)
    for slot in range(slots):
        grad = do_refs[slot][...].astype(F32)
        do_s[slot * tokens : (slot + 1) * tokens, :] = jnp.transpose(
            jnp.concatenate([jnp.zeros_like(grad), grad], axis=0)
        )
    acc_s[...] = jnp.zeros_like(acc_s)
    query_images = column(qi_ref[...])

    def forward(source, carry):
        scores = dot_nt(q_s[...], kv_s[source])
        same = query_images == ki_ref[source]
        weights = jnp.where(same, jnp.exp(scores), 0.0).astype(BF)
        e_s[source] = weights
        acc_s[...] += dot_nn(weights, one_v_s[source])
        return carry

    lax.fori_loop(0, sources, forward, 0)
    acc = acc_s[...]
    wide = lax.broadcasted_iota(jnp.int32, (rows, 2 * HD), 1)
    attended = jnp.where(wide >= HD, acc / pltpu.roll(acc, HD, 1), 0.0)
    inverse = 1.0 / acc[:, 0:1]
    do = do_s[...]
    out_dot = jnp.sum(do * attended, axis=1, keepdims=True) * inverse
    coarse = out_dot.astype(BF).astype(F32)
    do = do * inverse
    probe = jnp.where(wide == 0, -coarse, jnp.where(wide == 1, coarse - out_dot, do)).astype(BF)
    out_ref[...] = jnp.transpose(attended)[HD:].astype(BF)
    q_t = jnp.transpose(q_s[...].astype(F32))[:HD].astype(BF)
    do_t = jnp.transpose(do)[HD:].astype(BF)
    acc_s[...] = jnp.zeros_like(acc_s)

    def backward_into(dkv_ref, first):
        def backward(source, carry):
            weights = e_s[first + source]
            grad_weights = dot_nt(probe, one_v_s[first + source])
            grad_scores = (weights.astype(F32) * grad_weights).astype(BF)
            acc_s[...] += dot_nn(grad_scores, kv_s[first + source])
            dkv_ref[source, :HD, :] = dot_nn(q_t, grad_scores).astype(BF)
            dkv_ref[source, HD:, :] = dot_nn(do_t, weights).astype(BF)
            return carry

        lax.fori_loop(0, sources // 2, backward, 0)

    backward_into(high_ref, sources // 2)
    backward_into(low_ref, 0)
    dq_ref[...] = jnp.transpose(acc_s[...])[:HD]


def attention(head, coords, q_groups, do_slots, kv_sources, query_images, key_images):
    groups = [q.shape[1] for q in q_groups]
    slots, sources = len(do_slots), len(kv_sources)
    rows = sum(groups)
    parts = [pl.BlockSpec((1, size, 2 * HD), lambda i, c: (head, 0, 0)) for size in groups]
    place = kv_sources[0][1]
    kv_part = pl.BlockSpec((1, rows, 2 * HD), lambda i, c: (place, 0, 0))
    do_part = pl.BlockSpec((HD, rows // slots), lambda i, c: (head, 0))
    half = (sources // 2, 2 * HD, rows)
    return call(
        functools.partial(attention_kernel, groups, slots, sources),
        coords,
        [*q_groups, *do_slots, *[source[0] for source in kv_sources], query_images, key_images],
        parts
        + [do_part] * slots
        + [kv_part] * sources
        + [whole((1, rows)), whole((sources, 1, rows))],
        [struct((HD, rows), BF), struct((HD, rows), F32), struct(half, BF), struct(half, BF)],
        [whole((HD, rows)), whole((HD, rows)), whole(half), whole(half)],
        [
            pltpu.VMEM((rows, 2 * HD), BF),
            pltpu.VMEM((rows, 2 * HD), F32),
            pltpu.VMEM((sources, rows, 2 * HD), BF),
            pltpu.VMEM((sources, rows, 2 * HD), BF),
            pltpu.VMEM((sources, rows, rows), BF),
            pltpu.VMEM((rows, 2 * HD), F32),
        ],
        name=f"attention{head}",
    )


EXTRA = 16


def post_kernel(groups, slots, terms, heads, earlier, coords, *refs):
    count = len(groups)
    per_head = []
    for _head in heads:
        per_head.append((refs[0], refs[1], refs[2 : 2 + terms], refs[2 + terms : 2 + terms + count]))
        refs = refs[2 + terms + count :]
    normed_refs, dy_refs, refs = refs[:count], refs[count : count + slots], refs[count + slots :]
    (q_gain_ref, k_gain_ref, b_in_ref, b_out_ref), refs = refs[:4], refs[4:]
    before, refs = refs[:earlier], refs[earlier:]
    piece_refs, (keep_ref, send_ref) = refs[:slots], refs[slots:]
    tokens = piece_refs[0].shape[1]
    for ref, piece_ref in zip(before, piece_refs):
        piece_ref[: ref.shape[0], :] = ref[...]
    half = keep_ref.shape[1]
    rows, attn = 3 * HD // 2, HD // 2
    block = len(heads) * rows + EXTRA
    gains = [0.0, 0.0]
    q_gain, k_gain = column(q_gain_ref[...]), column(k_gain_ref[...])
    for place, (dq_ref, out_ref, term_refs, raw_refs) in enumerate(per_head):
        total = attn_total = None
        start = 0
        for group, size in enumerate(groups):
            span = slice(start, start + size)
            dkv = sum(term[0][:, span].astype(F32) for term in term_refs)
            grads = []
            for which, (grad, gain) in enumerate(
                ((dq_ref[:, span], q_gain * HD ** (-0.5)), (dkv[:HD], k_gain))
            ):
                hat, scale = normalized(raw_refs[group][0, which * HD : (which + 1) * HD, :], 0)
                factor = HD ** (-0.5) if which == 0 else 1.0
                gains[which] += jnp.sum(grad * hat, axis=1, keepdims=True) * factor
                grad = grad * gain
                grad = scale * (
                    grad
                    - jnp.mean(grad, axis=0, keepdims=True)
                    - hat * jnp.mean(grad * hat, axis=0, keepdims=True)
                )
                grads.append(grad)
            grads.append(dkv[HD:])
            projected_grad = jnp.concatenate(grads, axis=0).astype(BF)
            first = (place + (heads[0] if before else 0)) * 4 * HD
            for slot in range(start // tokens, (start + size) // tokens):
                inner = slice(slot * tokens - start, (slot + 1) * tokens - start)
                outer = slice(slot * tokens, (slot + 1) * tokens)
                piece_refs[slot][first : first + 3 * HD, :] = projected_grad[:, inner]
                piece_refs[slot][first + 3 * HD : first + 4 * HD, :] = out_ref[:, outer]
                term = dot_nn(out_ref[:, outer], dy_refs[slot][...])
                attn_total = term if attn_total is None else attn_total + term
            term = dot_nn(projected_grad, normed_refs[group][...])
            total = term if total is None else total + term
            start += size
        total, attn_total = total.astype(BF), attn_total.astype(BF)
        for value in (0, 1):

            @pl.when(coords[CORE] == value)
            def _():
                for side in (0, 1):
                    lanes = slice(side * half, (side + 1) * half)
                    at = side * block + place * rows
                    attn_at = 2 * block + (side * len(heads) + place) * attn
                    for target, mine in ((keep_ref, value), (send_ref, 1 - value)):
                        target[at : at + rows, :] = total[mine * rows : (mine + 1) * rows, lanes]
                        target[attn_at : attn_at + attn, :] = attn_total[
                            mine * attn : (mine + 1) * attn, lanes
                        ]

    turned = jnp.transpose(
        jnp.concatenate([jnp.broadcast_to(gain, (HD, 128)) for gain in gains], axis=0)
    )
    line = lax.broadcasted_iota(jnp.int32, (EXTRA, half), 0)
    gain_row = jnp.concatenate([turned[:1], jnp.zeros((1, half - 2 * HD), F32)], axis=1)
    for pack in (0, 1):
        extra = jnp.where(line == 5, gain_row, 0.0)
        if heads[0] == 0:
            extra = jnp.where(line == 0, b_out_ref[:, pack * half : (pack + 1) * half], extra)
            here = line == 1 + 2 * coords[TOP] + coords[CORE]
            extra = jnp.where(here, b_in_ref[:, pack * half : (pack + 1) * half], extra)
        for target in (keep_ref, send_ref):
            target[(pack + 1) * block - EXTRA : (pack + 1) * block, :] = extra.astype(BF)


def post(heads, coords, parts, raw_groups, normed_groups, dy_slots, q_gain, k_gain, gb_in, gb_out, before=()):
    groups = [raw.shape[2] for raw in raw_groups]
    width = normed_groups[0].shape[1]
    rows = sum(groups)
    slots = len(dy_slots)
    tokens = rows // slots
    count = len(heads)
    terms = len(parts[0][2])
    piece = (count * 4 * HD + (before[0].shape[0] if before else 0), tokens)
    share = (2 * (count * 3 * HD // 2 + EXTRA) + count * HD, width // 2)
    inputs, specs = [], []
    for head, (dq, out, added) in zip(heads, parts, strict=True):
        inputs += [dq, out, *added, *raw_groups]
        specs += [whole((HD, rows))] * 2 + [whole((1, 2 * HD, rows))] * terms
        specs += [
            pl.BlockSpec((1, 2 * HD, size), functools.partial(lambda h, i, c: (h, 0, 0), head))
            for size in groups
        ]
    return call(
        functools.partial(post_kernel, groups, slots, terms, heads, len(before)),
        coords,
        [*inputs, *normed_groups, *dy_slots, q_gain, k_gain, gb_in, gb_out, *before],
        specs
        + [whole((size, width)) for size in groups]
        + [whole((tokens, width))] * slots
        + [whole((1, HD))] * 2
        + [whole((1, width))] * 2
        + [whole(array.shape) for array in before],
        [struct(piece, BF)] * slots + [struct(share, BF)] * 2,
        [whole(piece)] * slots + [whole(share)] * 2,
        name="post" + "".join(map(str, heads)),
    )


def head_of(coords, slot_shift, head):
    z_index = coords[Z_LOW] + 2 * coords[Z_HIGH]
    return lax.rem(z_index + slot_shift, Z_COUNT) * PER_Z + head


def piece_of(pieces, slot, head, part):
    start = (head * 4 + part) * HD
    return pieces[slot][start : start + HD, :]


def output_kernel(shifts, coords, *refs):
    pieces, refs = refs[:Z_COUNT], refs[Z_COUNT:]
    x_ref, near_ref, far_ref, back_ref, b_ref, w_ref, out_ref, att_s = refs
    for head in range(PER_Z):
        for slot, shift in enumerate(shifts):
            row = pl.multiple_of(head_of(coords, shift, head) * HD, HD)
            att_s[pl.ds(row, HD), :] = piece_of(pieces, slot, head, 3)
    out_ref[...] = (
        x_ref[...].astype(F32)
        + near_ref[0]
        + far_ref[0].astype(F32)
        + back_ref[0].astype(F32)
        + b_ref[...]
        + dot_nn(jnp.transpose(att_s[...]), w_ref[...])
    ).astype(BF)


def block_output(coords, shifts, pieces, x, near, far, back, b_out, w_attn_out):
    rows, width = x.shape
    one = whole((1, rows, width))
    return call(
        functools.partial(output_kernel, shifts),
        coords,
        [*pieces, x, near, far, back, b_out, w_attn_out],
        [whole(piece.shape) for piece in pieces]
        + [whole((rows, width)), one, one, one]
        + [whole((1, width)), whole((width, width))],
        struct((rows, width), BF),
        whole((rows, width)),
        [pltpu.VMEM((width, rows), BF)],
        name="block_output",
    )


def tokens_kernel(shifts, coords, *refs):
    pieces, refs = refs[:Z_COUNT], refs[Z_COUNT:]
    x_ref, dy_ref, gain_ref, near_ref, far_ref, back_ref, w_ref, out_ref, grad_s = refs
    width = x_ref.shape[1]
    for head in range(PER_Z):
        for slot, shift in enumerate(shifts):
            row = pl.multiple_of(head_of(coords, shift, head) * HD, HD)
            for part in range(3):
                grad_s[pl.ds(part * width + row, HD), :] = piece_of(pieces, slot, head, part)
    normed_grad = (
        near_ref[0]
        + far_ref[0].astype(F32)
        + back_ref[0].astype(F32)
        + dot_nt(jnp.transpose(grad_s[...]), w_ref[...])
    )
    hat, scale = normalized(x_ref[...].astype(F32), 1)
    grad = normed_grad * gain_ref[...]
    out_ref[...] = dy_ref[...].astype(F32) + scale * (
        grad
        - jnp.mean(grad, axis=1, keepdims=True)
        - hat * jnp.mean(grad * hat, axis=1, keepdims=True)
    )


def token_gradient(coords, shifts, pieces, x, dy, ln_gain, near, far, back, w_qkv):
    rows, width = x.shape
    one = pl.BlockSpec((1, rows, width), lambda i, c: (1, 0, 0))
    return call(
        functools.partial(tokens_kernel, shifts),
        coords,
        [*pieces, x, dy, ln_gain, near, far, back, w_qkv],
        [whole(piece.shape) for piece in pieces]
        + [whole((rows, width))] * 2
        + [whole((1, width)), one, one, one]
        + [whole(w_qkv.shape)],
        struct((rows, width), F32),
        whole((rows, width)),
        [pltpu.VMEM((3 * width, rows), BF)],
        name="token_gradient",
    )


HALVE, BOTH, KEEP = range(3)


def stage_kernel(segments, bit, coords, keep_ref, came_ref, *out_refs):
    keep_at = came_at = kept = sent = 0
    for rows, came, mode in segments:
        total = keep_ref[keep_at : keep_at + rows, :]
        if came:
            total = (total.astype(F32) + came_ref[came_at : came_at + rows, :].astype(F32)).astype(BF)
            came_at += rows
        keep_at += rows
        if mode == HALVE:
            half = rows // 2
            for value in (0, 1):

                @pl.when(coords[bit] == value)
                def _():
                    out_refs[0][kept : kept + half, :] = total[value * half : (value + 1) * half]
                    out_refs[1][sent : sent + half, :] = total[(1 - value) * half : (2 - value) * half]

            kept += half
            sent += half
        else:
            out_refs[0][kept : kept + rows, :] = total
            kept += rows
            if mode == BOTH:
                out_refs[1][sent : sent + rows, :] = total
                sent += rows


def stage(coords, segments, bit, keep, came):
    width = keep.shape[1]
    kept = sum(rows // 2 if mode == HALVE else rows for rows, _came, mode in segments)
    sent = sum({HALVE: rows // 2, BOTH: rows, KEEP: 0}[mode] for rows, _came, mode in segments)
    shapes = [(kept, width)] + ([(sent, width)] if sent else [])
    return call(
        functools.partial(stage_kernel, segments, bit),
        coords,
        [keep, came],
        [whole(keep.shape), whole(came.shape)],
        [struct(shape, BF) for shape in shapes],
        [whole(shape) for shape in shapes],
        name="stage",
    )


def first_stage_kernel(counts, coords, *refs):
    (*shares, keep_ref, send_ref) = refs
    attn, rows = HD // 2, 3 * HD // 2
    blocks = [count * rows + EXTRA for count in counts]
    pairs = list(zip(blocks, counts, shares[::2], shares[1::2], strict=True))
    for value in (0, 1):

        @pl.when(coords[GRP] == value)
        def _():
            for pack, target in ((value, keep_ref), (1 - value, send_ref)):
                extra, at = 0.0, 0
                for block, count, own, came in pairs:
                    span = slice(pack * block, (pack + 1) * block)
                    total = own[span, :].astype(F32) + came[span, :].astype(F32)
                    target[at : at + count * rows, :] = total[: count * rows].astype(BF)
                    extra = extra + total[count * rows :]
                    at += count * rows
                target[PER_Z * (rows + 2 * attn) :, :] = extra.astype(BF)

    before = 0
    for block, count, own, came in pairs:
        total = (own[2 * block :, :].astype(F32) + came[2 * block :, :].astype(F32)).astype(BF)
        for side in (0, 1):
            start = PER_Z * rows + (side * PER_Z + before) * attn
            for target in (keep_ref, send_ref):
                target[start : start + count * attn, :] = total[
                    side * count * attn : (side + 1) * count * attn
                ]
        before += count


def first_stage(coords, counts, shares):
    half = shares[0].shape[1]
    shape = (PER_Z * (3 * HD // 2 + HD) + EXTRA, half)
    return call(
        functools.partial(first_stage_kernel, counts),
        coords,
        shares,
        [whole(share.shape) for share in shares],
        [struct(shape, BF)] * 2,
        [whole(shape)] * 2,
        name="first_stage",
    )


def mlp_place_kernel(coords, *refs):
    units, (w_ref, rows_ref, columns_ref, sum_ref, turn_s) = refs[:8], refs[8:]
    step = pl.program_id(0)
    part, half = units[0].shape[1] // 2, units[0].shape[2] // 2
    low, high = coords[Z_LOW], coords[Z_HIGH]

    @pl.when(step == 0)
    def _():
        sum_ref[...] = jnp.zeros_like(sum_ref)

    chosen = (step % 2 ^ coords[CORE]) * 4 + (step // 2 ^ coords[TOP]) * 2 + low
    for i in range(8):

        @pl.when(chosen == i)
        def _():
            for shard in range(Z_COUNT):
                rows_ref[shard * part : (shard + 1) * part, :] = units[i ^ (shard // 2)][
                    shard % 2 ^ high, :part, :
                ].astype(F32)

    lanes = pl.ds(pl.multiple_of((step // 2) * half, 128), half)
    chosen = coords[CORE] * 4 + (step % 2 ^ coords[TOP]) * 2 + low
    for i in range(8):

        @pl.when(chosen == i)
        def _():
            for core in (0, 1):
                for shard in range(Z_COUNT):
                    row = (core * Z_COUNT + shard) * part
                    unit = units[i ^ (4 * core) ^ (shard // 2)]
                    turn_s[row : row + part, :] = unit[shard % 2 ^ high, part:, lanes].astype(F32)

    total = 0.0
    for block in range(SHARDS * part // 128):
        span = slice(block * 128, (block + 1) * 128)
        turned = jnp.transpose(turn_s[span, :])
        columns_ref[:, span] = turned
        total = total + turned * w_ref[:, span].astype(F32)
    sum_ref[...] += jnp.sum(total, axis=1, keepdims=True)


def place_mlp(coords, units, w_in):
    _shards, rows, width = units[0].shape
    part, half = rows // 2, width // 2
    span = SHARDS * part
    return call(
        mlp_place_kernel,
        coords,
        [*units, w_in],
        [whole(unit.shape) for unit in units]
        + [pl.BlockSpec((half, span), lambda s, c: (c[GRP], s))],
        [
            struct((2 * span, width), F32),
            struct((half, 4 * span), F32),
            struct((half, 1), F32),
        ],
        [
            pl.BlockSpec((Z_COUNT * part, width), lambda s, c: (s, 0)),
            pl.BlockSpec((half, span), lambda s, c: (0, s)),
            whole((half, 1)),
        ],
        [pltpu.VMEM((span, half), F32)],
        grid=(4,),
        name="place_mlp",
    )


def heads_kernel(coords, *refs):
    (*unit_refs, w_ref, gain_ref, sum_ref, qkv_ref, attn_ref, ln_ref, turn_s) = refs
    half = unit_refs[0].shape[2]
    width = 2 * half
    q_rows, a_rows, unit = 3 * PER_Z * HD // 4, PER_Z * HD // 2, 16
    per_head = 3 * HD // 2 // unit
    for relative in range(8):
        block = unit_refs[relative // 2][relative % 2].astype(F32)
        core = coords[CORE] ^ (relative // 4)
        top = coords[TOP] ^ (relative // 2 % 2)
        low = coords[Z_LOW] ^ (relative % 2)
        for side in (0, 1):
            z_index = low + 2 * (coords[Z_HIGH] ^ side)
            for i in range(q_rows // unit):
                number = top * (q_rows // unit) + i
                inner = number % per_head + core * per_head
                row = (inner // (HD // unit)) * width + (inner % (HD // unit)) * unit
                row = row + (z_index * PER_Z + number // per_head) * HD
                turn_s[pl.ds(pl.multiple_of(row, unit), unit), :] = block[
                    side * q_rows + i * unit : side * q_rows + (i + 1) * unit
                ]
        lanes = pl.ds(pl.multiple_of(top * half, 128), half)
        for head in range(PER_Z):
            row = pl.multiple_of((low * PER_Z + head) * HD + core * (HD // 2), HD // 2)
            start = 2 * q_rows + head * (HD // 2)
            attn_ref[pl.ds(row, HD // 2), lanes] = block[start : start + HD // 2]
    total = 0.0
    for block in range(3 * width // 128):
        span = slice(block * 128, (block + 1) * 128)
        turned = jnp.transpose(turn_s[span, :])
        qkv_ref[:, span] = turned
        total = total + turned * w_ref[:, span].astype(F32)
    ln = (jnp.sum(total, axis=1, keepdims=True) + sum_ref[...]) / gain_ref[...]
    ln_ref[...] = jnp.transpose(jnp.broadcast_to(ln, (half, 128)))[0]


def place_heads(coords, units, w_qkv, gain_column, in_sums):
    half = units[0].shape[2]
    width = 2 * half
    row_half = lambda columns: pl.BlockSpec((half, columns), lambda s, c: (c[GRP], 0))
    return call(
        heads_kernel,
        coords,
        [*units, w_qkv, gain_column, in_sums],
        [whole(unit.shape) for unit in units] + [row_half(3 * width), row_half(1), whole((half, 1))],
        [struct((half, 3 * width), F32), struct((half, width), F32), struct((half,), F32)],
        [whole((half, 3 * width)), whole((half, width)), whole((half,))],
        [pltpu.VMEM((3 * width, half), F32)],
        name="place_heads",
    )


def per_device(
    tokens, lengths, image_ids, ln_gain, w_qkv, q_gain, k_gain,
    w_attn_out, w_in, b_in, w_mlp_out, b_out, cotangent,
):
    x, dy = tokens[0], cotangent[0]
    rows, width = x.shape
    half = width // 2
    hidden = w_in.shape[1]
    seq_count = lax.axis_size("seq")
    rest = seq_count // Z_COUNT
    rest_bits = rest.bit_length() - 1
    top_bit = rest_bits - 1
    me = lax.axis_index("seq")
    z_index, r_index = me // rest, me % rest
    grp = lax.axis_index("grp")
    core, top = r_index & 1, r_index >> top_bit
    coords = jnp.stack([grp, core, top, z_index & 1, z_index >> 1]).astype(jnp.int32)

    def z_shift(block, distance):
        route = [(i, (i + distance * rest) % seq_count) for i in range(seq_count)]
        return lax.ppermute(block, "seq", route)

    def flip(mask):
        route = [(i, i ^ mask) for i in range(seq_count)]
        return lambda block: lax.ppermute(block, "seq", route)

    def swap_packs(block):
        return lax.ppermute(block, "grp", [(0, 1), (1, 0)])

    swap_core, swap_top = flip(1), flip(1 << top_bit)
    swap_low, swap_high = flip(rest), flip(2 * rest)
    others = range(1, top_bit)

    def add(*terms):
        return sum(term.astype(F32) for term in terms).astype(BF)

    def after(value, *events):
        return lax.optimization_barrier((value, *events))[0]

    def after(value, *events):
        return lax.optimization_barrier((value, *events))[0]

    turn = [coords]

    def then(results):
        if isinstance(results, (list, tuple)):
            return [then(results[0]), *results[1:]]
        turn[0], results = lax.optimization_barrier((turn[0], results))
        return results

    def until(*events):
        turn[0] = after(turn[0], *events)

    shifts = [0, 1, 3, 2]
    x_slots = {0: x, **{d: z_shift(x, d) for d in ((1, 3) if OPT['x2'] else (1, 3, 2))}}
    if OPT['x2']:
        x_slots[2] = z_shift(after(x, x_slots[1]), 2)
    mine, gb_out, *do_pieces = then(prep(coords, shifts, x, dy, w_attn_out))
    across, other = swap_top(mine), swap_core(mine)
    mlp_weights = (ln_gain.reshape(1, width), w_in, b_in.reshape(1, hidden), w_mlp_out)
    near, near_far, *before = then(mlp(turn[0], [mine, other], *mlp_weights))
    near_far = swap_core(near_far)

    order = image_ids[0]
    labels = jnp.arange(order.shape[0], dtype=jnp.int32)
    ordered = jnp.sum(jnp.where(order[:, None] == labels[None, :], lengths[0][None, :], 0), axis=1)
    ends = jnp.cumsum(ordered)
    offsets = jnp.arange(rows, dtype=jnp.int32)
    slot_z = (z_index - jnp.array(shifts, dtype=jnp.int32)) % Z_COUNT
    masks = [2 * i for i in range(rest // 2)] + [2 * i + 1 for i in range(rest // 2)]
    source_r = r_index ^ jnp.array(masks, dtype=jnp.int32)
    starts = (slot_z[None, :] * rest + source_r[:, None]) * rows
    places = (starts[:, :, None] + offsets).reshape(rest, Z_COUNT * rows)
    images = jnp.sum((places[:, :, None] >= ends).astype(jnp.int32), axis=2).astype(F32)
    key_images = images[:, None, :]
    query_images = images[:1]

    ln_row = ln_gain.reshape(1, width)
    q_col, k_col = q_gain.reshape(1, HD), k_gain.reshape(1, HD)

    def second_mlp(event):
        results = then(
            mlp(turn[0], [across, swap_core(after(across, event))], *mlp_weights, before)
        )
        return results

    if OPT["order"]:
        mid, far, mlp_keep, mlp_send, gb_in = second_mlp(near)
    if OPT["across"]:
        until(across)
    if OPT["img"]:
        until(query_images, key_images)
    normed, q, kv_first, kv_rest, raw = then(
        qkv(turn[0], [x_slots[d] for d in shifts], ln_row, w_qkv, q_col, k_col)
    )
    normed_groups, q_groups, raw_groups = [normed], [q], [raw]

    def spread(group, bits):
        for bit in bits:
            group = {**group, **{m | 1 << bit: flip(1 << bit)(block) for m, block in group.items()}}
        return group

    upper = list(reversed(range(1, rest_bits)))
    events = [(), (near, x_slots[1], x_slots[2], x_slots[3]), (normed,), (near,)][OPT["do_tie"]]
    do_slots = [
        z_shift(after(piece, *events) if events else piece, d) if d else piece
        for piece, d in zip(do_pieces, shifts, strict=True)
    ]
    if OPT["do_use"] == 0:
        kv_first = after(kv_first, *do_slots[1:])
    kv_first = spread({0: kv_first}, upper)
    if not OPT["order"]:
        mid, far, mlp_keep, mlp_send, gb_in = second_mlp(near)
    mlp_came = swap_packs(mlp_send)
    if OPT["do_use"] == 1:
        kv_first = {m: after(block, mlp_keep, *do_slots[1:]) for m, block in kv_first.items()}
    elif OPT["core_tie"]:
        kv_first = {m: after(block, mlp_keep) for m, block in kv_first.items()}
    kv_here = after(kv_rest, kv_first[1 << top_bit])
    kv_first = spread(kv_first, [0])
    kv_rest = spread({0: kv_here}, upper)
    if OPT["dy_tie"]:
        dy_slots = {0: dy, **{d: z_shift(after(dy, kv_first[1]), d) for d in (1, 3)}}
    else:
        dy_slots = {0: dy, **{d: z_shift(after(dy, mlp_keep), d) for d in (1, 3)}}

    pieces, shares = [], []

    def finish(heads, parts, before=()):
        results = then(
            post(
                heads, turn[0], parts, raw_groups, normed_groups, dy_list, q_col, k_col, gb_in, gb_out, before
            )
        )
        shares.extend([results[Z_COUNT], swap_core(results[Z_COUNT + 1])])
        return results[:Z_COUNT]

    waiting = []

    def halve(keep, came, bit, move):
        size = keep.shape[0] // 2
        rows_of = lambda array, which: lax.dynamic_slice_in_dim(array, which * size, size, 0)
        gone = then(add(rows_of(keep, 1 - bit), rows_of(came, 1 - bit)))
        keep = then(add(rows_of(keep, bit), rows_of(came, bit)))
        return keep, move(gone)

    far = swap_core(far)
    if OPT["near"] == 0:
        until(near_far, far)
    back_sum = add(mid, far)
    if OPT["back"] == 0:
        back = swap_top(back_sum)
    if OPT["mlp_early"]:
        until(mlp_came)
        mlp_keep, mlp_came = halve(mlp_keep, mlp_came, z_index & 1, swap_low)
    kv_sources = [[(kv_first[m], 0) for m in masks]]
    for head in range(PER_Z):
        out_t, dq_t, low, high = then(
            attention(head, turn[0], q_groups, do_slots, kv_sources[head], query_images, key_images)
        )
        if head == 0:
            high = after(high, kv_rest[1 << top_bit])
            kv_rest = spread({m: after(block, dq_t) for m, block in kv_rest.items()}, [0])
            kv_sources += [[(kv_rest[m], place) for m in masks] for place in (0, 1)]
            high = after(high, dy_slots[1], dy_slots[3])
            if OPT["back"] == 0:
                high = after(high, back)
            if OPT["near"] == 1:
                high = after(high, near_far)
            dy_slots[2] = z_shift(after(dy, dq_t), 2)
            if OPT["back"] == 1:
                back = swap_top(after(back_sum, dq_t))
        else:
            high = after(high, *waiting[-1][2][2:])
        if head or OPT["mlp_early"]:
            high = after(high, mlp_came)
        if head == 1:
            high = after(high, dy_slots[2])
            dy_list = [dy_slots[d] for d in shifts]
            if OPT["back"] == 1:
                high = after(high, back)
            if OPT["back"] == 2:
                back = swap_top(after(back_sum, dq_t))
        if head == 2 and OPT["back"] == 2:
            high = after(high, back)
        came = swap_core(high)
        step = head + OPT["mlp_early"]

        def mlp_step():
            if step < 2:
                bit, move = ((z_index & 1, swap_low), (z_index >> 1, swap_high))[step]
                return halve(after(mlp_keep, turn[0]), mlp_came, bit, move)
            if step == 2:
                share = then(add(after(mlp_keep, turn[0]), mlp_came))
                for bit in others:
                    share = add(share, flip(1 << bit)(share))
                return share[None], swap_high(share[None])
            here = then(jnp.concatenate([after(mlp_keep, turn[0]), mlp_came], axis=0))
            return here, (swap_low(here), swap_top(here))

        if head or OPT["mlp_first"]:
            mlp_keep, mlp_came = mlp_step()
        parts = {2 * i: [low[i : i + 1], came[i : i + 1]] for i in range(rest // 2)}
        for bit in range(1, rest_bits):
            for mask in sorted(m for m in parts if m >> bit & 1):
                total = then(add(*parts.pop(mask)))
                parts[mask ^ (1 << bit)].append(flip(1 << bit)(total))
        if not (head or OPT["mlp_first"]):
            mlp_keep, mlp_came = mlp_step()
        waiting.append((dq_t, out_t, [low, came, *parts[0][2:]]))
    x_last = waiting[2][2][2]
    some = finish([0, 1], waiting[:2])
    if OPT["back"] == 3:
        back = swap_top(after(back_sum, x_last))
    if OPT["concat_at"]:
        late = finish([2], waiting[2:], some)
    if not OPT["mlp_early"]:
        tie = (turn[0], x_last) if OPT["zh_tie"] else (turn[0],)
        mlp_keep = then(jnp.concatenate([after(mlp_keep, *tie), mlp_came], axis=0))
        mlp_came = (swap_low(mlp_keep), swap_top(mlp_keep))
    units_here, (units_low, units_top) = mlp_keep, mlp_came
    if not OPT["concat_at"]:
        late = finish([2], waiting[2:], some)
    pieces = [None, None, None, None]
    pieces[0] = late[0]
    if OPT["p_tie"] == 0:
        for i in (1, 2):
            pieces[i] = z_shift(late[i], -shifts[i])
    if OPT["far_piece"] == 0:
        pieces[3] = z_shift(late[3], -shifts[3])
    if OPT["zl_use"] == 1:
        until(units_low, units_top)
    if OPT["topb"] == 0:
        units_both = swap_top(units_low)

    keep, send = then(first_stage(turn[0], [2, 1], shares))
    q_size, a_size = 3 * PER_Z * HD // 2, PER_Z * HD
    came = swap_packs(send)
    if OPT["topb"] == 1:
        units_both = swap_top(after(units_low, keep))
    if OPT["zl_use"] == 2:
        until(units_low, units_top)
    if OPT["p_use"] == 0:
        until(*pieces[1:3])
    if OPT["p_use"] == 2:
        until(pieces[1])
    if OPT["far_piece"] == 0 and OPT["far_use"] == 0:
        until(pieces[3])
    keep, send = then(
        stage(
            turn[0],
            [(q_size, True, HALVE), (a_size, True, HALVE), (EXTRA, True, BOTH)],
            TOP, keep, came,
        )
    )
    q_size, a_size = q_size // 2, a_size // 2
    came = swap_top(send)
    if OPT["p_tie"] == 3:
        pieces[1] = z_shift(after(late[1], keep), -shifts[1])
        came = after(came, pieces[1])
    if OPT["p_use"] == 1:
        came = after(came, *pieces[1:3])
    if OPT["p_use"] == 2:
        came = after(came, pieces[2])
    if OPT["far_piece"] == 0 and OPT["far_use"] == 1:
        came = after(came, pieces[3])
    share = then(add(keep, came))
    for bit in others:
        share = add(share, flip(1 << bit)(share))
    came = swap_high(share)
    if OPT["topb"] == 2:
        units_both = swap_top(after(units_low, share))
    if OPT["back"] == 4:
        back = swap_top(after(back_sum, share))
    if OPT["far_piece"] == 1:
        pieces[3] = z_shift(after(late[3], share), -shifts[3])
    if OPT["far_piece"] == 2:
        pieces[3] = z_shift(after(late[3], came), -shifts[3])
    if OPT["p_tie"]:
        for i in (1, 2):
            if pieces[i] is None:
                pieces[i] = z_shift(after(late[i], (None, share, came, came)[OPT["p_tie"]]), -shifts[i])
    near_parts = (near, near_far, back)
    mlp_units = [units_here, units_low, units_top, units_both]
    core_event = [(), (share,), (came,)][OPT["unit_tie"]]
    mlp_units += [swap_core(after(unit, *core_event) if core_event else unit) for unit in mlp_units]
    done = {}

    def place():
        done["mlp"] = then(place_mlp(turn[0], mlp_units, w_in))
        return done["mlp"][1]

    def out():
        done["out"] = then(
            block_output(
                turn[0], shifts, pieces, x, *near_parts, b_out.reshape(1, width), w_attn_out
            )
        )
        return done["out"]

    def tokens_out():
        done["tokens"] = then(
            token_gradient(turn[0], shifts, pieces, x, dy, ln_row, *near_parts, w_qkv)
        )
        return done["tokens"]

    def during(place_in, came):
        for name, run in (("place_at", place), ("out_at", out), ("tokens_at", tokens_out)):
            if OPT[name] == place_in:
                came = after(came, run())
        return came

    came = during(0, came)
    middle = q_size + a_size
    attn = jnp.where(z_index >> 1 == grp, share[q_size:middle], came[q_size:middle])
    small = add(share[middle:], came[middle:])
    unit = then(jnp.concatenate([share[:q_size], came[:q_size], attn, small], axis=0))
    came = during(1, swap_low(unit))
    size = unit.shape[0] - EXTRA
    small = add(unit[size:], came[size:]).astype(F32)
    units = then(jnp.stack([unit[:size], came[:size]]))
    came = during(2, swap_top(units))
    all_units = [units, came, swap_core(units), swap_core(came)]
    grad_w_mlp_out, grad_w_in, in_sums = done["mlp"]
    result, grad_tokens = done["out"], done["tokens"]

    grad_w_qkv, grad_w_attn_out, grad_ln_gain = place_heads(
        coords, all_units, w_qkv, ln_gain.reshape(width, 1), in_sums
    )
    return (
        result[None],
        grad_tokens[None],
        grad_ln_gain,
        grad_w_qkv,
        lax.dynamic_slice(small[5], (grp * (HD // 2),), (HD // 2,)),
        lax.dynamic_slice(small[5], (HD + grp * (HD // 2),), (HD // 2,)),
        grad_w_attn_out,
        grad_w_in,
        small[1:5].reshape(hidden // 2),
        grad_w_mlp_out,
        small[0],
    )


def solution(mesh):
    placed = (
        P("grp", "seq", None), P("grp", None), P("grp", None),
        P(), P(), P(), P(), P(), P(), P(), P(), P(), P("grp", "seq", None),
    )
    return jax.shard_map(
        per_device,
        mesh=mesh,
        in_specs=placed,
        out_specs=(
            P("grp", "seq", None), P("grp", "seq", None), P("grp"), P("grp", None), P("grp"),
            P("grp"), P("grp", None), P("grp", None), P("grp"), P("grp", None), P("grp"),
        ),
        check_vma=False,
    )
```

```python
import functools

import jax
import jax.numpy as jnp
from jax import lax
from jax.experimental import pallas as pl
from jax.experimental.pallas import tpu as pltpu
from jax.sharding import PartitionSpec as P

H = 12
HD = 64
Z_COUNT = 4
PER_Z = H // Z_COUNT
EPSILON = 1e-06
BF = jnp.bfloat16
F32 = jnp.float32
VMEM_BYTES = 58 * 1024 * 1024
FLOPS_PER_US = 1_150_000_000


def params():
    return pltpu.CompilerParams(vmem_limit_bytes=VMEM_BYTES)


def dot_nn(left, right):
    return lax.dot_general(left, right, (((1,), (0,)), ((), ())), preferred_element_type=F32)


def dot_nt(left, right):
    return lax.dot_general(left, right, (((1,), (1,)), ((), ())), preferred_element_type=F32)


def dot_tn(left, right):
    return lax.dot_general(left, right, (((0,), (0,)), ((), ())), preferred_element_type=F32)


def whole(shape):
    return pl.BlockSpec(shape, lambda *_: (0,) * len(shape))


def normalized(values, axis):
    mean = jnp.mean(values, axis=axis, keepdims=True)
    centred = values - mean
    spread = jnp.mean(centred * centred, axis=axis, keepdims=True)
    scale = lax.rsqrt(spread + EPSILON)
    return centred * scale, scale


GRP, CORE, TOP, Z_LOW, Z_HIGH = range(5)
SHARDS = 8


COST_US = {
    "prep": 18,
    "mlp1": 0,
    "mlp2": 40,
    "qkv": 5,
    "attention0": 18,
    "attention1": 18,
    "attention2": 18,
    "post01": 18,
    "post2": 0,
    "first_stage": 0,
    "stage": 0,
    "block_output": 5,
    "token_gradient": 6,
    "place_mlp": 9,
    "place_heads": 8,
}


def cost(us):
    return pl.CostEstimate(flops=us * FLOPS_PER_US, bytes_accessed=0, transcendentals=0)


def call(body, scalars, inputs, in_specs, out_shapes, out_specs, scratch=(), grid=(1,), name=None):
    return pl.pallas_call(
        body,
        grid_spec=pltpu.PrefetchScalarGridSpec(
            num_scalar_prefetch=1,
            grid=grid,
            in_specs=in_specs,
            out_specs=out_specs,
            scratch_shapes=list(scratch),
        ),
        out_shape=out_shapes,
        compiler_params=params(),
        cost_estimate=cost(COST_US[name]),
        name=name,
    )(scalars, *inputs)


def struct(shape, dtype):
    return jax.ShapeDtypeStruct(shape, dtype)


def column(row):
    return jnp.transpose(jnp.broadcast_to(row, (8, row.shape[1])))[:, :1]


def prep_kernel(shifts, coords, x_ref, dy_ref, w_ref, pair_ref, sum_ref, *refs):
    out_refs, grad_s = refs[:-1], refs[-1]
    pair_ref[0] = x_ref[...]
    dy = dy_ref[...]
    pair_ref[1] = dy
    sum_ref[...] = jnp.sum(dy.astype(F32), axis=0, keepdims=True)
    grad_s[...] = dot_nt(w_ref[...], dy).astype(BF)
    z_index = coords[Z_LOW] + 2 * coords[Z_HIGH]
    depth = PER_Z * HD
    for shift, out_ref in zip(shifts, out_refs, strict=True):
        row = pl.multiple_of(lax.rem(z_index + shift, Z_COUNT) * depth, depth)
        out_ref[...] = grad_s[pl.ds(row, depth), :]


def prep(coords, shifts, x, dy, w_attn_out):
    rows, width = dy.shape
    piece = (PER_Z * HD, rows)
    return call(
        functools.partial(prep_kernel, shifts),
        coords,
        [x, dy, w_attn_out],
        [whole((rows, width))] * 2 + [whole((width, width))],
        [struct((2, rows, width), BF), struct((1, width), F32)] + [struct(piece, BF)] * len(shifts),
        [whole((2, rows, width)), whole((1, width))] + [whole(piece)] * len(shifts),
        [pltpu.VMEM((width, rows), BF)],
        name="prep",
    )


def mlp_kernel(second, coords, *refs):
    pairs, refs = refs[:2], refs[2:]
    gain_ref, w_in_refs, b_in_refs, w_out_refs, refs = refs[0], refs[1:3], refs[3:5], refs[5:7], refs[7:]
    w_in = jnp.concatenate([ref[...] for ref in w_in_refs], axis=1)
    b_in = jnp.concatenate([ref[...] for ref in b_in_refs], axis=1)
    w_out = jnp.concatenate([ref[...] for ref in w_out_refs], axis=0)
    before, refs = (refs[:3], refs[3:]) if second else ((), refs)
    (near_ref, far_ref), refs = refs[:2], refs[2:]
    rows = pairs[0].shape[1]
    normed = []
    for pair in pairs:
        hat, _unused = normalized(pair[0].astype(F32), 1)
        normed.append((hat * gain_ref[...]).astype(BF))
    normed = jnp.concatenate(normed, axis=0)
    dy = jnp.concatenate([pair[1] for pair in pairs], axis=0)
    pre = dot_nn(normed, w_in) + b_in
    square = pre * pre
    tanh = jnp.tanh(pre * (0.7978845608028654 + 0.03567740813630193 * square))
    half = 0.5 + 0.5 * tanh
    hidden = (pre * half).astype(BF)
    slope = half + pre * (0.5 - 0.5 * tanh * tanh) * (
        0.7978845608028654 + 0.10703222440890579 * square
    )
    grad_pre = (slope * dot_nt(dy, w_out)).astype(BF)
    for which, total in enumerate((dot_nn(hidden, w_out), dot_nt(grad_pre, w_in))):
        near_ref[which] = total[:rows, :].astype(near_ref.dtype)
        far_ref[which] = total[rows:, :].astype(BF)
    gb_in = jnp.sum(grad_pre.astype(F32), axis=0, keepdims=True)
    g_out = dot_nn(jnp.transpose(hidden), dy)
    g_in = dot_nn(jnp.transpose(grad_pre), normed)
    if not second:
        g_out_ref, g_in_ref, gb_in_ref = refs
        g_out_ref[...] = g_out.astype(BF)
        g_in_ref[...] = g_in.astype(BF)
        gb_in_ref[...] = gb_in
        return
    g_out_before, g_in_before, gb_in_before = before
    keep_ref, send_ref, gb_in_ref = refs
    gb_in_ref[...] = gb_in + gb_in_before[...]
    g_out = (g_out + g_out_before[...].astype(F32)).astype(BF)
    g_in = (g_in + g_in_before[...].astype(F32)).astype(BF)
    part, half = g_out.shape[0] // SHARDS, g_out.shape[1] // 2
    first = Z_COUNT * part
    for value in (0, 1):

        @pl.when(coords[GRP] == value)
        def _():
            for shard in range(Z_COUNT):
                at, row = 2 * shard * part, shard * part
                for target, pack in ((keep_ref, value), (send_ref, 1 - value)):
                    start = pack * first + row
                    target[at : at + part, :] = g_out[start : start + part, :]
                    lanes = slice(pack * half, (pack + 1) * half)
                    target[at + part : at + 2 * part, :half] = g_in[row : row + part, lanes]
                    target[at + part : at + 2 * part, half:] = g_in[first + row : first + row + part, lanes]


def mlp(coords, pairs, ln_gain, w_in, b_in, w_out, before=()):
    _two, rows, width = pairs[0].shape
    own = w_in.shape[1] // 4
    second = bool(before)
    place = lambda c, side: side * 4 + c[TOP] * 2 + c[CORE]
    columns = lambda rows, side: pl.BlockSpec((rows, own // 2), lambda s, c: (0, place(c, side)))
    outs = [
        struct((2, rows, width), BF if second else F32),
        struct((2, rows, width), BF),
        struct((own, width), BF),
        struct((own, width), BF),
        struct((1, own), F32),
    ]
    return call(
        functools.partial(mlp_kernel, second),
        coords,
        [*pairs, ln_gain, w_in, w_in, b_in, b_in, w_out, w_out, *before],
        [whole((2, rows, width))] * 2
        + [
            whole((1, width)),
            columns(width, 0),
            columns(width, 1),
            columns(1, 0),
            columns(1, 1),
            pl.BlockSpec((own // 2, width), lambda s, c: (place(c, 0), 0)),
            pl.BlockSpec((own // 2, width), lambda s, c: (place(c, 1), 0)),
        ]
        + [whole(array.shape) for array in before],
        outs,
        [whole(out.shape) for out in outs],
        name="mlp2" if second else "mlp1",
    )


def qkv_kernel(count, coords, *refs):
    x_refs, refs = refs[:count], refs[count:]
    w_refs, refs = refs[:6], refs[6:]
    gain_ref, q_gain_ref, k_gain_ref, normed_ref, q_ref, first_ref, kv_ref, raw_ref, w_s, turn_s = refs
    rows = x_refs[0].shape[0]
    zeros = jnp.zeros((HD, rows), F32)
    q_gain, k_gain = column(q_gain_ref[...]), column(k_gain_ref[...])
    for i, w_ref in enumerate(w_refs):
        w_s[:, i * 128 : (i + 1) * 128] = w_ref[...]
    for slot in range(count):
        span = slice(slot * rows, (slot + 1) * rows)
        hat, _unused = normalized(x_refs[slot][...].astype(F32), 1)
        normed = (hat * gain_ref[...]).astype(BF)
        normed_ref[span, :] = normed
        projected = dot_nn(normed, w_s[...])
        turn_s[slot] = jnp.transpose(projected)
    for slot in range(count):
        span = slice(slot * rows, (slot + 1) * rows)
        for head in range(PER_Z):
            q_raw, k_raw, v = (
                turn_s[slot, pl.ds(pl.multiple_of(part * 256 + head * HD + coords[Z_LOW] * HD, HD), HD), :]
                for part in range(3)
            )
            raw_ref[head, :HD, span] = q_raw
            raw_ref[head, HD:, span] = k_raw
            q = normalized(q_raw, 0)[0] * q_gain * HD ** (-0.5)
            k = normalized(k_raw, 0)[0] * k_gain
            q_ref[head, span, :] = jnp.transpose(jnp.concatenate([q, zeros], axis=0)).astype(BF)
            target = kv_ref if head else first_ref
            target[max(head - 1, 0), span, :] = jnp.transpose(jnp.concatenate([k, v], axis=0)).astype(BF)


def qkv(coords, blocks, ln_gain, w_qkv, q_gain, k_gain):
    rows, width = blocks[0].shape
    count = len(blocks)
    total = count * rows

    def columns(part, second):
        first = lambda c: 3 * (c[Z_LOW] + 2 * c[Z_HIGH]) // 2
        return pl.BlockSpec((width, 128), lambda i, c: (0, part * (width // 128) + first(c) + second))

    shapes = [
        struct((total, width), BF),
        struct((PER_Z, total, 2 * HD), BF),
        struct((1, total, 2 * HD), BF),
        struct((PER_Z - 1, total, 2 * HD), BF),
        struct((PER_Z, 2 * HD, total), F32),
    ]
    return call(
        functools.partial(qkv_kernel, count),
        coords,
        [*blocks, *[w_qkv] * 6, ln_gain, q_gain, k_gain],
        [whole((rows, width))] * count
        + [columns(part, second) for part in range(3) for second in range(2)]
        + [whole((1, width)), whole((1, HD)), whole((1, HD))],
        shapes,
        [whole(shape.shape) for shape in shapes],
        [pltpu.VMEM((width, 768), BF), pltpu.VMEM((count, 768, rows), F32)],
        name="qkv",
    )


def attention_kernel(groups, slots, sources, coords, *refs):
    count = len(groups)
    q_refs, refs = refs[:count], refs[count:]
    do_refs, refs = refs[:slots], refs[slots:]
    kv_refs, refs = refs[:sources], refs[sources:]
    qi_ref, ki_ref, out_ref, *refs = refs
    dq_ref, low_ref, high_ref, q_s, do_s, kv_s, one_v_s, e_s, acc_s = refs
    rows = sum(groups)
    tokens = rows // slots
    start = 0
    for group, size in enumerate(groups):
        q_s[start : start + size, :] = q_refs[group][0]
        start += size
    lane = lax.broadcasted_iota(jnp.int32, (rows, 2 * HD), 1)
    for source in range(sources):
        block = kv_refs[source][0]
        kv_s[source] = block
        one_v_s[source] = jnp.where(lane < HD, jnp.ones((), BF), block)
    for slot in range(slots):
        grad = do_refs[slot][...].astype(F32)
        do_s[slot * tokens : (slot + 1) * tokens, :] = jnp.transpose(
            jnp.concatenate([jnp.zeros_like(grad), grad], axis=0)
        )
    acc_s[...] = jnp.zeros_like(acc_s)
    query_images = column(qi_ref[...])

    def forward(source, carry):
        scores = dot_nt(q_s[...], kv_s[source])
        same = query_images == ki_ref[source]
        weights = jnp.where(same, jnp.exp(scores), 0.0).astype(BF)
        e_s[source] = weights
        acc_s[...] += dot_nn(weights, one_v_s[source])
        return carry

    lax.fori_loop(0, sources, forward, 0)
    acc = acc_s[...]
    wide = lax.broadcasted_iota(jnp.int32, (rows, 2 * HD), 1)
    attended = jnp.where(wide >= HD, acc / pltpu.roll(acc, HD, 1), 0.0)
    inverse = 1.0 / acc[:, 0:1]
    do = do_s[...]
    out_dot = jnp.sum(do * attended, axis=1, keepdims=True) * inverse
    coarse = out_dot.astype(BF).astype(F32)
    do = do * inverse
    probe = jnp.where(wide == 0, -coarse, jnp.where(wide == 1, coarse - out_dot, do)).astype(BF)
    out_ref[...] = jnp.transpose(attended)[HD:].astype(BF)
    q_t = jnp.transpose(q_s[...].astype(F32))[:HD].astype(BF)
    do_t = jnp.transpose(do)[HD:].astype(BF)
    acc_s[...] = jnp.zeros_like(acc_s)

    def backward_into(dkv_ref, first):
        def backward(source, carry):
            weights = e_s[first + source]
            grad_weights = dot_nt(probe, one_v_s[first + source])
            grad_scores = (weights.astype(F32) * grad_weights).astype(BF)
            acc_s[...] += dot_nn(grad_scores, kv_s[first + source])
            dkv_ref[source, :HD, :] = dot_nn(q_t, grad_scores).astype(BF)
            dkv_ref[source, HD:, :] = dot_nn(do_t, weights).astype(BF)
            return carry

        lax.fori_loop(0, sources // 2, backward, 0)

    backward_into(high_ref, sources // 2)
    backward_into(low_ref, 0)
    dq_ref[...] = jnp.transpose(acc_s[...])[:HD]


def attention(head, coords, q_groups, do_slots, kv_sources, query_images, key_images):
    groups = [q.shape[1] for q in q_groups]
    slots, sources = len(do_slots), len(kv_sources)
    rows = sum(groups)
    parts = [pl.BlockSpec((1, size, 2 * HD), lambda i, c: (head, 0, 0)) for size in groups]
    place = kv_sources[0][1]
    kv_part = pl.BlockSpec((1, rows, 2 * HD), lambda i, c: (place, 0, 0))
    do_part = pl.BlockSpec((HD, rows // slots), lambda i, c: (head, 0))
    half = (sources // 2, 2 * HD, rows)
    return call(
        functools.partial(attention_kernel, groups, slots, sources),
        coords,
        [*q_groups, *do_slots, *[source[0] for source in kv_sources], query_images, key_images],
        parts
        + [do_part] * slots
        + [kv_part] * sources
        + [whole((1, rows)), whole((sources, 1, rows))],
        [struct((HD, rows), BF), struct((HD, rows), F32), struct(half, BF), struct(half, BF)],
        [whole((HD, rows)), whole((HD, rows)), whole(half), whole(half)],
        [
            pltpu.VMEM((rows, 2 * HD), BF),
            pltpu.VMEM((rows, 2 * HD), F32),
            pltpu.VMEM((sources, rows, 2 * HD), BF),
            pltpu.VMEM((sources, rows, 2 * HD), BF),
            pltpu.VMEM((sources, rows, rows), BF),
            pltpu.VMEM((rows, 2 * HD), F32),
        ],
        name=f"attention{head}",
    )


EXTRA = 16


def post_kernel(groups, slots, terms, heads, earlier, coords, *refs):
    count = len(groups)
    per_head = []
    for _head in heads:
        per_head.append((refs[0], refs[1], refs[2 : 2 + terms], refs[2 + terms : 2 + terms + count]))
        refs = refs[2 + terms + count :]
    normed_refs, dy_refs, refs = refs[:count], refs[count : count + slots], refs[count + slots :]
    (q_gain_ref, k_gain_ref, b_in_ref, b_out_ref), refs = refs[:4], refs[4:]
    before, refs = refs[:earlier], refs[earlier:]
    piece_refs, (keep_ref, send_ref) = refs[:slots], refs[slots:]
    tokens = piece_refs[0].shape[1]
    for ref, piece_ref in zip(before, piece_refs):
        piece_ref[: ref.shape[0], :] = ref[...]
    half = keep_ref.shape[1]
    rows, attn = 3 * HD // 2, HD // 2
    block = len(heads) * rows + EXTRA
    gains = [0.0, 0.0]
    q_gain, k_gain = column(q_gain_ref[...]), column(k_gain_ref[...])
    for place, (dq_ref, out_ref, term_refs, raw_refs) in enumerate(per_head):
        total = attn_total = None
        start = 0
        for group, size in enumerate(groups):
            span = slice(start, start + size)
            dkv = sum(term[0][:, span].astype(F32) for term in term_refs)
            grads = []
            for which, (grad, gain) in enumerate(
                ((dq_ref[:, span], q_gain * HD ** (-0.5)), (dkv[:HD], k_gain))
            ):
                hat, scale = normalized(raw_refs[group][0, which * HD : (which + 1) * HD, :], 0)
                factor = HD ** (-0.5) if which == 0 else 1.0
                gains[which] += jnp.sum(grad * hat, axis=1, keepdims=True) * factor
                grad = grad * gain
                grad = scale * (
                    grad
                    - jnp.mean(grad, axis=0, keepdims=True)
                    - hat * jnp.mean(grad * hat, axis=0, keepdims=True)
                )
                grads.append(grad)
            grads.append(dkv[HD:])
            projected_grad = jnp.concatenate(grads, axis=0).astype(BF)
            first = (place + (heads[0] if before else 0)) * 4 * HD
            for slot in range(start // tokens, (start + size) // tokens):
                inner = slice(slot * tokens - start, (slot + 1) * tokens - start)
                outer = slice(slot * tokens, (slot + 1) * tokens)
                piece_refs[slot][first : first + 3 * HD, :] = projected_grad[:, inner]
                piece_refs[slot][first + 3 * HD : first + 4 * HD, :] = out_ref[:, outer]
                term = dot_nn(out_ref[:, outer], dy_refs[slot][...])
                attn_total = term if attn_total is None else attn_total + term
            term = dot_nn(projected_grad, normed_refs[group][...])
            total = term if total is None else total + term
            start += size
        total, attn_total = total.astype(BF), attn_total.astype(BF)
        for value in (0, 1):

            @pl.when(coords[CORE] == value)
            def _():
                for side in (0, 1):
                    lanes = slice(side * half, (side + 1) * half)
                    at = side * block + place * rows
                    attn_at = 2 * block + (side * len(heads) + place) * attn
                    for target, mine in ((keep_ref, value), (send_ref, 1 - value)):
                        target[at : at + rows, :] = total[mine * rows : (mine + 1) * rows, lanes]
                        target[attn_at : attn_at + attn, :] = attn_total[
                            mine * attn : (mine + 1) * attn, lanes
                        ]

    turned = jnp.transpose(
        jnp.concatenate([jnp.broadcast_to(gain, (HD, 128)) for gain in gains], axis=0)
    )
    line = lax.broadcasted_iota(jnp.int32, (EXTRA, half), 0)
    gain_row = jnp.concatenate([turned[:1], jnp.zeros((1, half - 2 * HD), F32)], axis=1)
    for pack in (0, 1):
        extra = jnp.where(line == 5, gain_row, 0.0)
        if heads[0] == 0:
            extra = jnp.where(line == 0, b_out_ref[:, pack * half : (pack + 1) * half], extra)
            here = line == 1 + 2 * coords[TOP] + coords[CORE]
            extra = jnp.where(here, b_in_ref[:, pack * half : (pack + 1) * half], extra)
        for target in (keep_ref, send_ref):
            target[(pack + 1) * block - EXTRA : (pack + 1) * block, :] = extra.astype(BF)


def post(heads, coords, parts, raw_groups, normed_groups, dy_slots, q_gain, k_gain, gb_in, gb_out, before=()):
    groups = [raw.shape[2] for raw in raw_groups]
    width = normed_groups[0].shape[1]
    rows = sum(groups)
    slots = len(dy_slots)
    tokens = rows // slots
    count = len(heads)
    terms = len(parts[0][2])
    piece = (count * 4 * HD + (before[0].shape[0] if before else 0), tokens)
    share = (2 * (count * 3 * HD // 2 + EXTRA) + count * HD, width // 2)
    inputs, specs = [], []
    for head, (dq, out, added) in zip(heads, parts, strict=True):
        inputs += [dq, out, *added, *raw_groups]
        specs += [whole((HD, rows))] * 2 + [whole((1, 2 * HD, rows))] * terms
        specs += [
            pl.BlockSpec((1, 2 * HD, size), functools.partial(lambda h, i, c: (h, 0, 0), head))
            for size in groups
        ]
    return call(
        functools.partial(post_kernel, groups, slots, terms, heads, len(before)),
        coords,
        [*inputs, *normed_groups, *dy_slots, q_gain, k_gain, gb_in, gb_out, *before],
        specs
        + [whole((size, width)) for size in groups]
        + [whole((tokens, width))] * slots
        + [whole((1, HD))] * 2
        + [whole((1, width))] * 2
        + [whole(array.shape) for array in before],
        [struct(piece, BF)] * slots + [struct(share, BF)] * 2,
        [whole(piece)] * slots + [whole(share)] * 2,
        name="post" + "".join(map(str, heads)),
    )


def head_of(coords, slot_shift, head):
    z_index = coords[Z_LOW] + 2 * coords[Z_HIGH]
    return lax.rem(z_index + slot_shift, Z_COUNT) * PER_Z + head


def piece_of(pieces, slot, head, part):
    start = (head * 4 + part) * HD
    return pieces[slot][start : start + HD, :]


def output_kernel(shifts, coords, *refs):
    pieces, refs = refs[:Z_COUNT], refs[Z_COUNT:]
    x_ref, near_ref, far_ref, back_ref, b_ref, w_ref, out_ref, att_s = refs
    for head in range(PER_Z):
        for slot, shift in enumerate(shifts):
            row = pl.multiple_of(head_of(coords, shift, head) * HD, HD)
            att_s[pl.ds(row, HD), :] = piece_of(pieces, slot, head, 3)
    out_ref[...] = (
        x_ref[...].astype(F32)
        + near_ref[0]
        + far_ref[0].astype(F32)
        + back_ref[0].astype(F32)
        + b_ref[...]
        + dot_nn(jnp.transpose(att_s[...]), w_ref[...])
    ).astype(BF)


def block_output(coords, shifts, pieces, x, near, far, back, b_out, w_attn_out):
    rows, width = x.shape
    one = whole((1, rows, width))
    return call(
        functools.partial(output_kernel, shifts),
        coords,
        [*pieces, x, near, far, back, b_out, w_attn_out],
        [whole(piece.shape) for piece in pieces]
        + [whole((rows, width)), one, one, one]
        + [whole((1, width)), whole((width, width))],
        struct((rows, width), BF),
        whole((rows, width)),
        [pltpu.VMEM((width, rows), BF)],
        name="block_output",
    )


def tokens_kernel(shifts, coords, *refs):
    pieces, refs = refs[:Z_COUNT], refs[Z_COUNT:]
    x_ref, dy_ref, gain_ref, near_ref, far_ref, back_ref, w_ref, out_ref, grad_s = refs
    width = x_ref.shape[1]
    for head in range(PER_Z):
        for slot, shift in enumerate(shifts):
            row = pl.multiple_of(head_of(coords, shift, head) * HD, HD)
            for part in range(3):
                grad_s[pl.ds(part * width + row, HD), :] = piece_of(pieces, slot, head, part)
    normed_grad = (
        near_ref[0]
        + far_ref[0].astype(F32)
        + back_ref[0].astype(F32)
        + dot_nt(jnp.transpose(grad_s[...]), w_ref[...])
    )
    hat, scale = normalized(x_ref[...].astype(F32), 1)
    grad = normed_grad * gain_ref[...]
    out_ref[...] = dy_ref[...].astype(F32) + scale * (
        grad
        - jnp.mean(grad, axis=1, keepdims=True)
        - hat * jnp.mean(grad * hat, axis=1, keepdims=True)
    )


def token_gradient(coords, shifts, pieces, x, dy, ln_gain, near, far, back, w_qkv):
    rows, width = x.shape
    one = pl.BlockSpec((1, rows, width), lambda i, c: (1, 0, 0))
    return call(
        functools.partial(tokens_kernel, shifts),
        coords,
        [*pieces, x, dy, ln_gain, near, far, back, w_qkv],
        [whole(piece.shape) for piece in pieces]
        + [whole((rows, width))] * 2
        + [whole((1, width)), one, one, one]
        + [whole(w_qkv.shape)],
        struct((rows, width), F32),
        whole((rows, width)),
        [pltpu.VMEM((3 * width, rows), BF)],
        name="token_gradient",
    )


HALVE, BOTH, KEEP = range(3)


def stage_kernel(segments, bit, coords, keep_ref, came_ref, *out_refs):
    keep_at = came_at = kept = sent = 0
    for rows, came, mode in segments:
        total = keep_ref[keep_at : keep_at + rows, :]
        if came:
            total = (total.astype(F32) + came_ref[came_at : came_at + rows, :].astype(F32)).astype(BF)
            came_at += rows
        keep_at += rows
        if mode == HALVE:
            half = rows // 2
            for value in (0, 1):

                @pl.when(coords[bit] == value)
                def _():
                    out_refs[0][kept : kept + half, :] = total[value * half : (value + 1) * half]
                    out_refs[1][sent : sent + half, :] = total[(1 - value) * half : (2 - value) * half]

            kept += half
            sent += half
        else:
            out_refs[0][kept : kept + rows, :] = total
            kept += rows
            if mode == BOTH:
                out_refs[1][sent : sent + rows, :] = total
                sent += rows


def stage(coords, segments, bit, keep, came):
    width = keep.shape[1]
    kept = sum(rows // 2 if mode == HALVE else rows for rows, _came, mode in segments)
    sent = sum({HALVE: rows // 2, BOTH: rows, KEEP: 0}[mode] for rows, _came, mode in segments)
    shapes = [(kept, width)] + ([(sent, width)] if sent else [])
    return call(
        functools.partial(stage_kernel, segments, bit),
        coords,
        [keep, came],
        [whole(keep.shape), whole(came.shape)],
        [struct(shape, BF) for shape in shapes],
        [whole(shape) for shape in shapes],
        name="stage",
    )


def first_stage_kernel(counts, coords, *refs):
    (*shares, keep_ref, send_ref) = refs
    attn, rows = HD // 2, 3 * HD // 2
    blocks = [count * rows + EXTRA for count in counts]
    pairs = list(zip(blocks, counts, shares[::2], shares[1::2], strict=True))
    for value in (0, 1):

        @pl.when(coords[GRP] == value)
        def _():
            for pack, target in ((value, keep_ref), (1 - value, send_ref)):
                extra, at = 0.0, 0
                for block, count, own, came in pairs:
                    span = slice(pack * block, (pack + 1) * block)
                    total = own[span, :].astype(F32) + came[span, :].astype(F32)
                    target[at : at + count * rows, :] = total[: count * rows].astype(BF)
                    extra = extra + total[count * rows :]
                    at += count * rows
                target[PER_Z * (rows + 2 * attn) :, :] = extra.astype(BF)

    before = 0
    for block, count, own, came in pairs:
        total = (own[2 * block :, :].astype(F32) + came[2 * block :, :].astype(F32)).astype(BF)
        for side in (0, 1):
            start = PER_Z * rows + (side * PER_Z + before) * attn
            for target in (keep_ref, send_ref):
                target[start : start + count * attn, :] = total[
                    side * count * attn : (side + 1) * count * attn
                ]
        before += count


def first_stage(coords, counts, shares):
    half = shares[0].shape[1]
    shape = (PER_Z * (3 * HD // 2 + HD) + EXTRA, half)
    return call(
        functools.partial(first_stage_kernel, counts),
        coords,
        shares,
        [whole(share.shape) for share in shares],
        [struct(shape, BF)] * 2,
        [whole(shape)] * 2,
        name="first_stage",
    )


def mlp_place_kernel(coords, *refs):
    units, (w_ref, rows_ref, columns_ref, sum_ref, turn_s) = refs[:8], refs[8:]
    step = pl.program_id(0)
    part, half = units[0].shape[1] // 2, units[0].shape[2] // 2
    low, high = coords[Z_LOW], coords[Z_HIGH]

    @pl.when(step == 0)
    def _():
        sum_ref[...] = jnp.zeros_like(sum_ref)

    chosen = (step % 2 ^ coords[CORE]) * 4 + (step // 2 ^ coords[TOP]) * 2 + low
    for i in range(8):

        @pl.when(chosen == i)
        def _():
            for shard in range(Z_COUNT):
                rows_ref[shard * part : (shard + 1) * part, :] = units[i ^ (shard // 2)][
                    shard % 2 ^ high, :part, :
                ].astype(F32)

    lanes = pl.ds(pl.multiple_of((step // 2) * half, 128), half)
    chosen = coords[CORE] * 4 + (step % 2 ^ coords[TOP]) * 2 + low
    for i in range(8):

        @pl.when(chosen == i)
        def _():
            for core in (0, 1):
                for shard in range(Z_COUNT):
                    row = (core * Z_COUNT + shard) * part
                    unit = units[i ^ (4 * core) ^ (shard // 2)]
                    turn_s[row : row + part, :] = unit[shard % 2 ^ high, part:, lanes].astype(F32)

    total = 0.0
    for block in range(SHARDS * part // 128):
        span = slice(block * 128, (block + 1) * 128)
        turned = jnp.transpose(turn_s[span, :])
        columns_ref[:, span] = turned
        total = total + turned * w_ref[:, span].astype(F32)
    sum_ref[...] += jnp.sum(total, axis=1, keepdims=True)


def place_mlp(coords, units, w_in):
    _shards, rows, width = units[0].shape
    part, half = rows // 2, width // 2
    span = SHARDS * part
    return call(
        mlp_place_kernel,
        coords,
        [*units, w_in],
        [whole(unit.shape) for unit in units]
        + [pl.BlockSpec((half, span), lambda s, c: (c[GRP], s))],
        [
            struct((2 * span, width), F32),
            struct((half, 4 * span), F32),
            struct((half, 1), F32),
        ],
        [
            pl.BlockSpec((Z_COUNT * part, width), lambda s, c: (s, 0)),
            pl.BlockSpec((half, span), lambda s, c: (0, s)),
            whole((half, 1)),
        ],
        [pltpu.VMEM((span, half), F32)],
        grid=(4,),
        name="place_mlp",
    )


def heads_kernel(coords, *refs):
    (*unit_refs, w_ref, gain_ref, sum_ref, qkv_ref, attn_ref, ln_ref, turn_s) = refs
    half = unit_refs[0].shape[2]
    width = 2 * half
    q_rows, a_rows, unit = 3 * PER_Z * HD // 4, PER_Z * HD // 2, 16
    per_head = 3 * HD // 2 // unit
    for relative in range(8):
        block = unit_refs[relative // 2][relative % 2].astype(F32)
        core = coords[CORE] ^ (relative // 4)
        top = coords[TOP] ^ (relative // 2 % 2)
        low = coords[Z_LOW] ^ (relative % 2)
        for side in (0, 1):
            z_index = low + 2 * (coords[Z_HIGH] ^ side)
            for i in range(q_rows // unit):
                number = top * (q_rows // unit) + i
                inner = number % per_head + core * per_head
                row = (inner // (HD // unit)) * width + (inner % (HD // unit)) * unit
                row = row + (z_index * PER_Z + number // per_head) * HD
                turn_s[pl.ds(pl.multiple_of(row, unit), unit), :] = block[
                    side * q_rows + i * unit : side * q_rows + (i + 1) * unit
                ]
        lanes = pl.ds(pl.multiple_of(top * half, 128), half)
        for head in range(PER_Z):
            row = pl.multiple_of((low * PER_Z + head) * HD + core * (HD // 2), HD // 2)
            start = 2 * q_rows + head * (HD // 2)
            attn_ref[pl.ds(row, HD // 2), lanes] = block[start : start + HD // 2]
    total = 0.0
    for block in range(3 * width // 128):
        span = slice(block * 128, (block + 1) * 128)
        turned = jnp.transpose(turn_s[span, :])
        qkv_ref[:, span] = turned
        total = total + turned * w_ref[:, span].astype(F32)
    ln = (jnp.sum(total, axis=1, keepdims=True) + sum_ref[...]) / gain_ref[...]
    ln_ref[...] = jnp.transpose(jnp.broadcast_to(ln, (half, 128)))[0]


def place_heads(coords, units, w_qkv, gain_column, in_sums):
    half = units[0].shape[2]
    width = 2 * half
    row_half = lambda columns: pl.BlockSpec((half, columns), lambda s, c: (c[GRP], 0))
    return call(
        heads_kernel,
        coords,
        [*units, w_qkv, gain_column, in_sums],
        [whole(unit.shape) for unit in units] + [row_half(3 * width), row_half(1), whole((half, 1))],
        [struct((half, 3 * width), F32), struct((half, width), F32), struct((half,), F32)],
        [whole((half, 3 * width)), whole((half, width)), whole((half,))],
        [pltpu.VMEM((3 * width, half), F32)],
        name="place_heads",
    )


def per_device(
    tokens, lengths, image_ids, ln_gain, w_qkv, q_gain, k_gain,
    w_attn_out, w_in, b_in, w_mlp_out, b_out, cotangent,
):
    x, dy = tokens[0], cotangent[0]
    rows, width = x.shape
    half = width // 2
    hidden = w_in.shape[1]
    seq_count = lax.axis_size("seq")
    rest = seq_count // Z_COUNT
    rest_bits = rest.bit_length() - 1
    top_bit = rest_bits - 1
    me = lax.axis_index("seq")
    z_index, r_index = me // rest, me % rest
    grp = lax.axis_index("grp")
    core, top = r_index & 1, r_index >> top_bit
    coords = jnp.stack([grp, core, top, z_index & 1, z_index >> 1]).astype(jnp.int32)

    def z_shift(block, distance):
        route = [(i, (i + distance * rest) % seq_count) for i in range(seq_count)]
        return lax.ppermute(block, "seq", route)

    def flip(mask):
        route = [(i, i ^ mask) for i in range(seq_count)]
        return lambda block: lax.ppermute(block, "seq", route)

    def swap_packs(block):
        return lax.ppermute(block, "grp", [(0, 1), (1, 0)])

    swap_core, swap_top = flip(1), flip(1 << top_bit)
    swap_low, swap_high = flip(rest), flip(2 * rest)
    others = range(1, top_bit)

    def add(*terms):
        return sum(term.astype(F32) for term in terms).astype(BF)

    def after(value, *events):
        return lax.optimization_barrier((value, *events))[0]

    def after(value, *events):
        return lax.optimization_barrier((value, *events))[0]

    turn = [coords]

    def then(results):
        if isinstance(results, (list, tuple)):
            return [then(results[0]), *results[1:]]
        turn[0], results = lax.optimization_barrier((turn[0], results))
        return results

    def until(*events):
        turn[0] = after(turn[0], *events)

    shifts = [0, 1, 3, 2]
    x_slots = {0: x, **{d: z_shift(x, d) for d in (1, 3, 2)}}
    mine, gb_out, *do_pieces = then(prep(coords, shifts, x, dy, w_attn_out))
    across, other = swap_top(mine), swap_core(mine)
    mlp_weights = (ln_gain.reshape(1, width), w_in, b_in.reshape(1, hidden), w_mlp_out)
    near, near_far, *before = then(mlp(turn[0], [mine, other], *mlp_weights))
    near_far = swap_core(near_far)

    order = image_ids[0]
    labels = jnp.arange(order.shape[0], dtype=jnp.int32)
    ordered = jnp.sum(jnp.where(order[:, None] == labels[None, :], lengths[0][None, :], 0), axis=1)
    ends = jnp.cumsum(ordered)
    offsets = jnp.arange(rows, dtype=jnp.int32)
    slot_z = (z_index - jnp.array(shifts, dtype=jnp.int32)) % Z_COUNT
    masks = [2 * i for i in range(rest // 2)] + [2 * i + 1 for i in range(rest // 2)]
    source_r = r_index ^ jnp.array(masks, dtype=jnp.int32)
    starts = (slot_z[None, :] * rest + source_r[:, None]) * rows
    places = (starts[:, :, None] + offsets).reshape(rest, Z_COUNT * rows)
    images = jnp.sum((places[:, :, None] >= ends).astype(jnp.int32), axis=2).astype(F32)
    key_images = images[:, None, :]
    query_images = images[:1]

    ln_row = ln_gain.reshape(1, width)
    q_col, k_col = q_gain.reshape(1, HD), k_gain.reshape(1, HD)

    until(query_images, key_images)
    normed, q, kv_first, kv_rest, raw = then(
        qkv(turn[0], [x_slots[d] for d in shifts], ln_row, w_qkv, q_col, k_col)
    )
    normed_groups, q_groups, raw_groups = [normed], [q], [raw]

    def spread(group, bits):
        for bit in bits:
            group = {**group, **{m | 1 << bit: flip(1 << bit)(block) for m, block in group.items()}}
        return group

    upper = list(reversed(range(1, rest_bits)))
    do_slots = [
        z_shift(after(piece, normed), d) if d else piece
        for piece, d in zip(do_pieces, shifts, strict=True)
    ]
    kv_first = spread({0: kv_first}, upper)
    mid, far, mlp_keep, mlp_send, gb_in = then(
        mlp(turn[0], [across, swap_core(after(across, near))], *mlp_weights, before)
    )
    mlp_came = swap_packs(mlp_send)
    kv_first = {m: after(block, mlp_keep, *do_slots[1:]) for m, block in kv_first.items()}
    kv_here = after(kv_rest, kv_first[1 << top_bit])
    kv_first = spread(kv_first, [0])
    kv_rest = spread({0: kv_here}, upper)
    dy_slots = {0: dy, **{d: z_shift(after(dy, kv_first[1]), d) for d in (1, 3)}}

    shares = []

    def finish(heads, parts, before=()):
        results = then(
            post(
                heads, turn[0], parts, raw_groups, normed_groups, dy_list, q_col, k_col, gb_in, gb_out, before
            )
        )
        shares.extend([results[Z_COUNT], swap_core(results[Z_COUNT + 1])])
        return results[:Z_COUNT]

    waiting = []

    def halve(keep, came, bit, move):
        size = keep.shape[0] // 2
        rows_of = lambda array, which: lax.dynamic_slice_in_dim(array, which * size, size, 0)
        gone = then(add(rows_of(keep, 1 - bit), rows_of(came, 1 - bit)))
        keep = then(add(rows_of(keep, bit), rows_of(came, bit)))
        return keep, move(gone)

    far = swap_core(far)
    back_sum = add(mid, far)
    kv_sources = [[(kv_first[m], 0) for m in masks]]
    for head in range(PER_Z):
        out_t, dq_t, low, high = then(
            attention(head, turn[0], q_groups, do_slots, kv_sources[head], query_images, key_images)
        )
        if head == 0:
            high = after(high, kv_rest[1 << top_bit])
            kv_rest = spread({m: after(block, dq_t) for m, block in kv_rest.items()}, [0])
            kv_sources += [[(kv_rest[m], place) for m in masks] for place in (0, 1)]
            high = after(high, dy_slots[1], dy_slots[3])
            dy_slots[2] = z_shift(after(dy, dq_t), 2)
            back = swap_top(after(back_sum, dq_t))
        elif head > 1:
            high = after(high, *waiting[-1][2][2:])
        if head == 2:
            high = after(high, *waiting[0][2][2:])
        if head:
            high = after(high, mlp_came)
        if head == 1:
            high = after(high, dy_slots[2])
            dy_list = [dy_slots[d] for d in shifts]
            high = after(high, back)
        came = swap_core(high)

        def mlp_step():
            if head < 2:
                bit, move = ((z_index & 1, swap_low), (z_index >> 1, swap_high))[head]
                return halve(after(mlp_keep, turn[0]), mlp_came, bit, move)
            share = then(add(after(mlp_keep, turn[0]), mlp_came))
            for bit in others:
                share = add(share, flip(1 << bit)(share))
            return share[None], swap_high(share[None])

        if head:
            mlp_keep, mlp_came = mlp_step()
        parts = {2 * i: [low[i : i + 1], came[i : i + 1]] for i in range(rest // 2)}
        for bit in range(1, rest_bits):
            for mask in sorted(m for m in parts if m >> bit & 1):
                total = then(add(*parts.pop(mask)))
                parts[mask ^ (1 << bit)].append(flip(1 << bit)(total))
        if not head:
            mlp_keep, mlp_came = mlp_step()
        waiting.append((dq_t, out_t, [low, came, *parts[0][2:]]))
    some = finish([0, 1], waiting[:2])
    late = finish([2], waiting[2:], some)
    units_here = then(jnp.concatenate([after(mlp_keep, turn[0]), mlp_came], axis=0))
    units_low, units_top = swap_low(units_here), swap_top(units_here)
    send_piece = lambda slot, *events: z_shift(after(late[slot], *events), -shifts[slot])
    pieces = [late[0], None, None, z_shift(late[3], -shifts[3])]

    keep, send = then(first_stage(turn[0], [2, 1], shares))
    q_size, a_size = 3 * PER_Z * HD // 2, PER_Z * HD
    came = swap_packs(send)
    units_both = swap_top(after(units_low, keep))
    until(units_low, units_top)
    until(pieces[3])
    keep, send = then(
        stage(
            turn[0],
            [(q_size, True, HALVE), (a_size, True, HALVE), (EXTRA, True, BOTH)],
            TOP, keep, came,
        )
    )
    q_size, a_size = q_size // 2, a_size // 2
    came = swap_top(send)
    pieces[1] = send_piece(1, keep)
    came = after(came, pieces[1])
    share = then(add(keep, came))
    for bit in others:
        share = add(share, flip(1 << bit)(share))
    came = swap_high(share)
    pieces[2] = send_piece(2, came)
    near_parts = (near, near_far, back)
    mlp_units = [units_here, units_low, units_top, units_both]
    mlp_units += [swap_core(after(unit, share)) for unit in mlp_units]
    middle = q_size + a_size
    attn = jnp.where(z_index >> 1 == grp, share[q_size:middle], came[q_size:middle])
    small = add(share[middle:], came[middle:])
    unit = then(jnp.concatenate([share[:q_size], came[:q_size], attn, small], axis=0))
    came = swap_low(unit)
    grad_w_mlp_out, grad_w_in, in_sums = then(place_mlp(turn[0], mlp_units, w_in))
    came = after(came, grad_w_in)
    size = unit.shape[0] - EXTRA
    small = add(unit[size:], came[size:]).astype(F32)
    units = then(jnp.stack([unit[:size], came[:size]]))
    came = swap_top(units)
    result = then(
        block_output(
            turn[0], shifts, pieces, x, *near_parts, b_out.reshape(1, width), w_attn_out
        )
    )
    came = after(came, result)
    grad_tokens = then(
        token_gradient(turn[0], shifts, pieces, x, dy, ln_row, *near_parts, w_qkv)
    )
    came = after(came, grad_tokens)
    all_units = [units, came, swap_core(units), swap_core(came)]

    grad_w_qkv, grad_w_attn_out, grad_ln_gain = place_heads(
        coords, all_units, w_qkv, ln_gain.reshape(width, 1), in_sums
    )
    return (
        result[None],
        grad_tokens[None],
        grad_ln_gain,
        grad_w_qkv,
        lax.dynamic_slice(small[5], (grp * (HD // 2),), (HD // 2,)),
        lax.dynamic_slice(small[5], (HD + grp * (HD // 2),), (HD // 2,)),
        grad_w_attn_out,
        grad_w_in,
        small[1:5].reshape(hidden // 2),
        grad_w_mlp_out,
        small[0],
    )


def solution(mesh):
    placed = (
        P("grp", "seq", None), P("grp", None), P("grp", None),
        P(), P(), P(), P(), P(), P(), P(), P(), P(), P("grp", "seq", None),
    )
    return jax.shard_map(
        per_device,
        mesh=mesh,
        in_specs=placed,
        out_specs=(
            P("grp", "seq", None), P("grp", "seq", None), P("grp"), P("grp", None), P("grp"),
            P("grp"), P("grp", None), P("grp", None), P("grp"), P("grp", None), P("grp"),
        ),
        check_vma=False,
    )
```

```python
import functools

import jax
import jax.numpy as jnp
from jax import lax
from jax.experimental import pallas as pl
from jax.experimental.pallas import tpu as pltpu
from jax.sharding import PartitionSpec as P

H = 12
HD = 64
Z_COUNT = 4
PER_Z = H // Z_COUNT
EPSILON = 1e-06
BF = jnp.bfloat16
F32 = jnp.float32
VMEM_BYTES = 58 * 1024 * 1024
FLOPS_PER_US = 1_150_000_000


def params():
    return pltpu.CompilerParams(vmem_limit_bytes=VMEM_BYTES)


def dot_nn(left, right):
    return lax.dot_general(left, right, (((1,), (0,)), ((), ())), preferred_element_type=F32)


def dot_nt(left, right):
    return lax.dot_general(left, right, (((1,), (1,)), ((), ())), preferred_element_type=F32)


def dot_tn(left, right):
    return lax.dot_general(left, right, (((0,), (0,)), ((), ())), preferred_element_type=F32)


def whole(shape):
    return pl.BlockSpec(shape, lambda *_: (0,) * len(shape))


def normalized(values, axis):
    mean = jnp.mean(values, axis=axis, keepdims=True)
    centred = values - mean
    spread = jnp.mean(centred * centred, axis=axis, keepdims=True)
    scale = lax.rsqrt(spread + EPSILON)
    return centred * scale, scale


GRP, CORE, TOP, Z_LOW, Z_HIGH = range(5)
SHARDS = 8


COST_US = {
    "prep": 18,
    "mlp1": 0,
    "mlp2": 40,
    "qkv": 5,
    "attention0": 18,
    "attention1": 18,
    "attention2": 18,
    "post01": 18,
    "post2": 0,
    "first_stage": 0,
    "stage": 0,
    "token_results": 11,
    "place_mlp": 9,
    "place_heads": 8,
}


def cost(us):
    return pl.CostEstimate(flops=us * FLOPS_PER_US, bytes_accessed=0, transcendentals=0)


def call(body, scalars, inputs, in_specs, out_shapes, out_specs, scratch=(), grid=(1,), name=None):
    return pl.pallas_call(
        body,
        grid_spec=pltpu.PrefetchScalarGridSpec(
            num_scalar_prefetch=1,
            grid=grid,
            in_specs=in_specs,
            out_specs=out_specs,
            scratch_shapes=list(scratch),
        ),
        out_shape=out_shapes,
        compiler_params=params(),
        cost_estimate=cost(COST_US[name]),
        name=name,
    )(scalars, *inputs)


def struct(shape, dtype):
    return jax.ShapeDtypeStruct(shape, dtype)


def column(row):
    return jnp.transpose(jnp.broadcast_to(row, (8, row.shape[1])))[:, :1]


def prep_kernel(shifts, coords, x_ref, dy_ref, w_ref, pair_ref, sum_ref, *refs):
    out_refs, grad_s = refs[:-1], refs[-1]
    pair_ref[0] = x_ref[...]
    dy = dy_ref[...]
    pair_ref[1] = dy
    sum_ref[...] = jnp.sum(dy.astype(F32), axis=0, keepdims=True)
    grad_s[...] = dot_nt(w_ref[...], dy).astype(BF)
    z_index = coords[Z_LOW] + 2 * coords[Z_HIGH]
    depth = PER_Z * HD
    for shift, out_ref in zip(shifts, out_refs, strict=True):
        row = pl.multiple_of(lax.rem(z_index + shift, Z_COUNT) * depth, depth)
        out_ref[...] = grad_s[pl.ds(row, depth), :]


def prep(coords, shifts, x, dy, w_attn_out):
    rows, width = dy.shape
    piece = (PER_Z * HD, rows)
    return call(
        functools.partial(prep_kernel, shifts),
        coords,
        [x, dy, w_attn_out],
        [whole((rows, width))] * 2 + [whole((width, width))],
        [struct((2, rows, width), BF), struct((1, width), F32)] + [struct(piece, BF)] * len(shifts),
        [whole((2, rows, width)), whole((1, width))] + [whole(piece)] * len(shifts),
        [pltpu.VMEM((width, rows), BF)],
        name="prep",
    )


def mlp_kernel(second, coords, *refs):
    pairs, refs = refs[:2], refs[2:]
    gain_ref, w_in_refs, b_in_refs, w_out_refs, refs = refs[0], refs[1:3], refs[3:5], refs[5:7], refs[7:]
    w_in = jnp.concatenate([ref[...] for ref in w_in_refs], axis=1)
    b_in = jnp.concatenate([ref[...] for ref in b_in_refs], axis=1)
    w_out = jnp.concatenate([ref[...] for ref in w_out_refs], axis=0)
    before, refs = (refs[:3], refs[3:]) if second else ((), refs)
    (near_ref, far_ref), refs = refs[:2], refs[2:]
    rows = pairs[0].shape[1]
    normed = []
    for pair in pairs:
        hat, _unused = normalized(pair[0].astype(F32), 1)
        normed.append((hat * gain_ref[...]).astype(BF))
    normed = jnp.concatenate(normed, axis=0)
    dy = jnp.concatenate([pair[1] for pair in pairs], axis=0)
    pre = dot_nn(normed, w_in) + b_in
    square = pre * pre
    tanh = jnp.tanh(pre * (0.7978845608028654 + 0.03567740813630193 * square))
    half = 0.5 + 0.5 * tanh
    hidden = (pre * half).astype(BF)
    slope = half + pre * (0.5 - 0.5 * tanh * tanh) * (
        0.7978845608028654 + 0.10703222440890579 * square
    )
    grad_pre = (slope * dot_nt(dy, w_out)).astype(BF)
    for which, total in enumerate((dot_nn(hidden, w_out), dot_nt(grad_pre, w_in))):
        near_ref[which] = total[:rows, :].astype(near_ref.dtype)
        far_ref[which] = total[rows:, :].astype(BF)
    gb_in = jnp.sum(grad_pre.astype(F32), axis=0, keepdims=True)
    g_out = dot_nn(jnp.transpose(hidden), dy)
    g_in = dot_nn(jnp.transpose(grad_pre), normed)
    if not second:
        g_out_ref, g_in_ref, gb_in_ref = refs
        g_out_ref[...] = g_out.astype(BF)
        g_in_ref[...] = g_in.astype(BF)
        gb_in_ref[...] = gb_in
        return
    g_out_before, g_in_before, gb_in_before = before
    keep_ref, send_ref, gb_in_ref = refs
    gb_in_ref[...] = gb_in + gb_in_before[...]
    g_out = (g_out + g_out_before[...].astype(F32)).astype(BF)
    g_in = (g_in + g_in_before[...].astype(F32)).astype(BF)
    part, half = g_out.shape[0] // SHARDS, g_out.shape[1] // 2
    first = Z_COUNT * part
    for value in (0, 1):

        @pl.when(coords[GRP] == value)
        def _():
            for shard in range(Z_COUNT):
                at, row = 2 * shard * part, shard * part
                for target, pack in ((keep_ref, value), (send_ref, 1 - value)):
                    start = pack * first + row
                    target[at : at + part, :] = g_out[start : start + part, :]
                    lanes = slice(pack * half, (pack + 1) * half)
                    target[at + part : at + 2 * part, :half] = g_in[row : row + part, lanes]
                    target[at + part : at + 2 * part, half:] = g_in[first + row : first + row + part, lanes]


def mlp(coords, pairs, ln_gain, w_in, b_in, w_out, before=()):
    _two, rows, width = pairs[0].shape
    own = w_in.shape[1] // 4
    second = bool(before)
    place = lambda c, side: side * 4 + c[TOP] * 2 + c[CORE]
    columns = lambda rows, side: pl.BlockSpec((rows, own // 2), lambda s, c: (0, place(c, side)))
    outs = [
        struct((2, rows, width), BF if second else F32),
        struct((2, rows, width), BF),
        struct((own, width), BF),
        struct((own, width), BF),
        struct((1, own), F32),
    ]
    return call(
        functools.partial(mlp_kernel, second),
        coords,
        [*pairs, ln_gain, w_in, w_in, b_in, b_in, w_out, w_out, *before],
        [whole((2, rows, width))] * 2
        + [
            whole((1, width)),
            columns(width, 0),
            columns(width, 1),
            columns(1, 0),
            columns(1, 1),
            pl.BlockSpec((own // 2, width), lambda s, c: (place(c, 0), 0)),
            pl.BlockSpec((own // 2, width), lambda s, c: (place(c, 1), 0)),
        ]
        + [whole(array.shape) for array in before],
        outs,
        [whole(out.shape) for out in outs],
        name="mlp2" if second else "mlp1",
    )


def qkv_kernel(count, coords, *refs):
    x_refs, refs = refs[:count], refs[count:]
    w_refs, refs = refs[:6], refs[6:]
    gain_ref, q_gain_ref, k_gain_ref, normed_ref, q_ref, first_ref, kv_ref, raw_ref, w_s, turn_s = refs
    rows = x_refs[0].shape[0]
    zeros = jnp.zeros((HD, rows), F32)
    q_gain, k_gain = column(q_gain_ref[...]), column(k_gain_ref[...])
    for i, w_ref in enumerate(w_refs):
        w_s[:, i * 128 : (i + 1) * 128] = w_ref[...]
    for slot in range(count):
        span = slice(slot * rows, (slot + 1) * rows)
        hat, _unused = normalized(x_refs[slot][...].astype(F32), 1)
        normed = (hat * gain_ref[...]).astype(BF)
        normed_ref[span, :] = normed
        projected = dot_nn(normed, w_s[...])
        turn_s[slot] = jnp.transpose(projected)
    for slot in range(count):
        span = slice(slot * rows, (slot + 1) * rows)
        for head in range(PER_Z):
            q_raw, k_raw, v = (
                turn_s[slot, pl.ds(pl.multiple_of(part * 256 + head * HD + coords[Z_LOW] * HD, HD), HD), :]
                for part in range(3)
            )
            raw_ref[head, :HD, span] = q_raw
            raw_ref[head, HD:, span] = k_raw
            q = normalized(q_raw, 0)[0] * q_gain * HD ** (-0.5)
            k = normalized(k_raw, 0)[0] * k_gain
            q_ref[head, span, :] = jnp.transpose(jnp.concatenate([q, zeros], axis=0)).astype(BF)
            target = kv_ref if head else first_ref
            target[max(head - 1, 0), span, :] = jnp.transpose(jnp.concatenate([k, v], axis=0)).astype(BF)


def qkv(coords, blocks, ln_gain, w_qkv, q_gain, k_gain):
    rows, width = blocks[0].shape
    count = len(blocks)
    total = count * rows

    def columns(part, second):
        first = lambda c: 3 * (c[Z_LOW] + 2 * c[Z_HIGH]) // 2
        return pl.BlockSpec((width, 128), lambda i, c: (0, part * (width // 128) + first(c) + second))

    shapes = [
        struct((total, width), BF),
        struct((PER_Z, total, 2 * HD), BF),
        struct((1, total, 2 * HD), BF),
        struct((PER_Z - 1, total, 2 * HD), BF),
        struct((PER_Z, 2 * HD, total), F32),
    ]
    return call(
        functools.partial(qkv_kernel, count),
        coords,
        [*blocks, *[w_qkv] * 6, ln_gain, q_gain, k_gain],
        [whole((rows, width))] * count
        + [columns(part, second) for part in range(3) for second in range(2)]
        + [whole((1, width)), whole((1, HD)), whole((1, HD))],
        shapes,
        [whole(shape.shape) for shape in shapes],
        [pltpu.VMEM((width, 768), BF), pltpu.VMEM((count, 768, rows), F32)],
        name="qkv",
    )


def attention_kernel(groups, slots, sources, coords, *refs):
    count = len(groups)
    q_refs, refs = refs[:count], refs[count:]
    do_refs, refs = refs[:slots], refs[slots:]
    kv_refs, refs = refs[:sources], refs[sources:]
    qi_ref, ki_ref, out_ref, *refs = refs
    dq_ref, low_ref, high_ref, q_s, do_s, kv_s, one_v_s, e_s, acc_s = refs
    rows = sum(groups)
    tokens = rows // slots
    start = 0
    for group, size in enumerate(groups):
        q_s[start : start + size, :] = q_refs[group][0]
        start += size
    lane = lax.broadcasted_iota(jnp.int32, (rows, 2 * HD), 1)
    for source in range(sources):
        block = kv_refs[source][0]
        kv_s[source] = block
        one_v_s[source] = jnp.where(lane < HD, jnp.ones((), BF), block)
    for slot in range(slots):
        grad = do_refs[slot][...].astype(F32)
        do_s[slot * tokens : (slot + 1) * tokens, :] = jnp.transpose(
            jnp.concatenate([jnp.zeros_like(grad), grad], axis=0)
        )
    acc_s[...] = jnp.zeros_like(acc_s)
    query_images = column(qi_ref[...])

    def forward(source, carry):
        scores = dot_nt(q_s[...], kv_s[source])
        same = query_images == ki_ref[source]
        weights = jnp.where(same, jnp.exp(scores), 0.0).astype(BF)
        e_s[source] = weights
        acc_s[...] += dot_nn(weights, one_v_s[source])
        return carry

    lax.fori_loop(0, sources, forward, 0)
    acc = acc_s[...]
    wide = lax.broadcasted_iota(jnp.int32, (rows, 2 * HD), 1)
    attended = jnp.where(wide >= HD, acc / pltpu.roll(acc, HD, 1), 0.0)
    inverse = 1.0 / acc[:, 0:1]
    do = do_s[...]
    out_dot = jnp.sum(do * attended, axis=1, keepdims=True) * inverse
    coarse = out_dot.astype(BF).astype(F32)
    do = do * inverse
    probe = jnp.where(wide == 0, -coarse, jnp.where(wide == 1, coarse - out_dot, do)).astype(BF)
    out_ref[...] = jnp.transpose(attended)[HD:].astype(BF)
    q_t = jnp.transpose(q_s[...].astype(F32))[:HD].astype(BF)
    do_t = jnp.transpose(do)[HD:].astype(BF)
    acc_s[...] = jnp.zeros_like(acc_s)

    def backward_into(dkv_ref, first):
        def backward(source, carry):
            weights = e_s[first + source]
            grad_weights = dot_nt(probe, one_v_s[first + source])
            grad_scores = (weights.astype(F32) * grad_weights).astype(BF)
            acc_s[...] += dot_nn(grad_scores, kv_s[first + source])
            dkv_ref[source, :HD, :] = dot_nn(q_t, grad_scores).astype(BF)
            dkv_ref[source, HD:, :] = dot_nn(do_t, weights).astype(BF)
            return carry

        lax.fori_loop(0, sources // 2, backward, 0)

    backward_into(high_ref, sources // 2)
    backward_into(low_ref, 0)
    dq_ref[...] = jnp.transpose(acc_s[...])[:HD]


def attention(head, coords, q_groups, do_slots, kv_sources, query_images, key_images):
    groups = [q.shape[1] for q in q_groups]
    slots, sources = len(do_slots), len(kv_sources)
    rows = sum(groups)
    parts = [pl.BlockSpec((1, size, 2 * HD), lambda i, c: (head, 0, 0)) for size in groups]
    place = kv_sources[0][1]
    kv_part = pl.BlockSpec((1, rows, 2 * HD), lambda i, c: (place, 0, 0))
    do_part = pl.BlockSpec((HD, rows // slots), lambda i, c: (head, 0))
    half = (sources // 2, 2 * HD, rows)
    return call(
        functools.partial(attention_kernel, groups, slots, sources),
        coords,
        [*q_groups, *do_slots, *[source[0] for source in kv_sources], query_images, key_images],
        parts
        + [do_part] * slots
        + [kv_part] * sources
        + [whole((1, rows)), whole((sources, 1, rows))],
        [struct((HD, rows), BF), struct((HD, rows), F32), struct(half, BF), struct(half, BF)],
        [whole((HD, rows)), whole((HD, rows)), whole(half), whole(half)],
        [
            pltpu.VMEM((rows, 2 * HD), BF),
            pltpu.VMEM((rows, 2 * HD), F32),
            pltpu.VMEM((sources, rows, 2 * HD), BF),
            pltpu.VMEM((sources, rows, 2 * HD), BF),
            pltpu.VMEM((sources, rows, rows), BF),
            pltpu.VMEM((rows, 2 * HD), F32),
        ],
        name=f"attention{head}",
    )


EXTRA = 16


def post_kernel(groups, slots, terms, heads, earlier, coords, *refs):
    count = len(groups)
    per_head = []
    for _head in heads:
        per_head.append((refs[0], refs[1], refs[2 : 2 + terms], refs[2 + terms : 2 + terms + count]))
        refs = refs[2 + terms + count :]
    normed_refs, dy_refs, refs = refs[:count], refs[count : count + slots], refs[count + slots :]
    (q_gain_ref, k_gain_ref, b_in_ref, b_out_ref), refs = refs[:4], refs[4:]
    before, refs = refs[:earlier], refs[earlier:]
    piece_refs, (keep_ref, send_ref) = refs[:slots], refs[slots:]
    tokens = piece_refs[0].shape[1]
    for ref, piece_ref in zip(before, piece_refs):
        piece_ref[: ref.shape[0], :] = ref[...]
    half = keep_ref.shape[1]
    rows, attn = 3 * HD // 2, HD // 2
    block = len(heads) * rows + EXTRA
    gains = [0.0, 0.0]
    q_gain, k_gain = column(q_gain_ref[...]), column(k_gain_ref[...])
    for place, (dq_ref, out_ref, term_refs, raw_refs) in enumerate(per_head):
        total = attn_total = None
        start = 0
        for group, size in enumerate(groups):
            span = slice(start, start + size)
            dkv = sum(term[0][:, span].astype(F32) for term in term_refs)
            grads = []
            for which, (grad, gain) in enumerate(
                ((dq_ref[:, span], q_gain * HD ** (-0.5)), (dkv[:HD], k_gain))
            ):
                hat, scale = normalized(raw_refs[group][0, which * HD : (which + 1) * HD, :], 0)
                factor = HD ** (-0.5) if which == 0 else 1.0
                gains[which] += jnp.sum(grad * hat, axis=1, keepdims=True) * factor
                grad = grad * gain
                grad = scale * (
                    grad
                    - jnp.mean(grad, axis=0, keepdims=True)
                    - hat * jnp.mean(grad * hat, axis=0, keepdims=True)
                )
                grads.append(grad)
            grads.append(dkv[HD:])
            projected_grad = jnp.concatenate(grads, axis=0).astype(BF)
            first = (place + (heads[0] if before else 0)) * 4 * HD
            for slot in range(start // tokens, (start + size) // tokens):
                inner = slice(slot * tokens - start, (slot + 1) * tokens - start)
                outer = slice(slot * tokens, (slot + 1) * tokens)
                piece_refs[slot][first : first + 3 * HD, :] = projected_grad[:, inner]
                piece_refs[slot][first + 3 * HD : first + 4 * HD, :] = out_ref[:, outer]
                term = dot_nn(out_ref[:, outer], dy_refs[slot][...])
                attn_total = term if attn_total is None else attn_total + term
            term = dot_nn(projected_grad, normed_refs[group][...])
            total = term if total is None else total + term
            start += size
        total, attn_total = total.astype(BF), attn_total.astype(BF)
        for value in (0, 1):

            @pl.when(coords[CORE] == value)
            def _():
                for side in (0, 1):
                    lanes = slice(side * half, (side + 1) * half)
                    at = side * block + place * rows
                    attn_at = 2 * block + (side * len(heads) + place) * attn
                    for target, mine in ((keep_ref, value), (send_ref, 1 - value)):
                        target[at : at + rows, :] = total[mine * rows : (mine + 1) * rows, lanes]
                        target[attn_at : attn_at + attn, :] = attn_total[
                            mine * attn : (mine + 1) * attn, lanes
                        ]

    turned = jnp.transpose(
        jnp.concatenate([jnp.broadcast_to(gain, (HD, 128)) for gain in gains], axis=0)
    )
    line = lax.broadcasted_iota(jnp.int32, (EXTRA, half), 0)
    gain_row = jnp.concatenate([turned[:1], jnp.zeros((1, half - 2 * HD), F32)], axis=1)
    for pack in (0, 1):
        extra = jnp.where(line == 5, gain_row, 0.0)
        if heads[0] == 0:
            extra = jnp.where(line == 0, b_out_ref[:, pack * half : (pack + 1) * half], extra)
            here = line == 1 + 2 * coords[TOP] + coords[CORE]
            extra = jnp.where(here, b_in_ref[:, pack * half : (pack + 1) * half], extra)
        for target in (keep_ref, send_ref):
            target[(pack + 1) * block - EXTRA : (pack + 1) * block, :] = extra.astype(BF)


def post(heads, coords, parts, raw_groups, normed_groups, dy_slots, q_gain, k_gain, gb_in, gb_out, before=()):
    groups = [raw.shape[2] for raw in raw_groups]
    width = normed_groups[0].shape[1]
    rows = sum(groups)
    slots = len(dy_slots)
    tokens = rows // slots
    count = len(heads)
    terms = len(parts[0][2])
    piece = (count * 4 * HD + (before[0].shape[0] if before else 0), tokens)
    share = (2 * (count * 3 * HD // 2 + EXTRA) + count * HD, width // 2)
    inputs, specs = [], []
    for head, (dq, out, added) in zip(heads, parts, strict=True):
        inputs += [dq, out, *added, *raw_groups]
        specs += [whole((HD, rows))] * 2 + [whole((1, 2 * HD, rows))] * terms
        specs += [
            pl.BlockSpec((1, 2 * HD, size), functools.partial(lambda h, i, c: (h, 0, 0), head))
            for size in groups
        ]
    return call(
        functools.partial(post_kernel, groups, slots, terms, heads, len(before)),
        coords,
        [*inputs, *normed_groups, *dy_slots, q_gain, k_gain, gb_in, gb_out, *before],
        specs
        + [whole((size, width)) for size in groups]
        + [whole((tokens, width))] * slots
        + [whole((1, HD))] * 2
        + [whole((1, width))] * 2
        + [whole(array.shape) for array in before],
        [struct(piece, BF)] * slots + [struct(share, BF)] * 2,
        [whole(piece)] * slots + [whole(share)] * 2,
        name="post" + "".join(map(str, heads)),
    )


def head_of(coords, slot_shift, head):
    z_index = coords[Z_LOW] + 2 * coords[Z_HIGH]
    return lax.rem(z_index + slot_shift, Z_COUNT) * PER_Z + head


def piece_of(pieces, slot, head, part):
    start = (head * 4 + part) * HD
    return pieces[slot][start : start + HD, :]


def tokens_kernel(shifts, coords, *refs):
    pieces, refs = refs[:Z_COUNT], refs[Z_COUNT:]
    (x_ref, dy_ref, gain_ref, near_ref, far_ref, back_ref, b_ref, w_attn_ref, w_ref,
     out_ref, grad_ref, att_s, grad_s) = refs
    width = x_ref.shape[1]
    for head in range(PER_Z):
        for slot, shift in enumerate(shifts):
            row = pl.multiple_of(head_of(coords, shift, head) * HD, HD)
            att_s[pl.ds(row, HD), :] = piece_of(pieces, slot, head, 3)
            for part in range(3):
                grad_s[pl.ds(part * width + row, HD), :] = piece_of(pieces, slot, head, part)
    x = x_ref[...].astype(F32)
    mlp_out, mlp_grad = (
        near_ref[which] + far_ref[which].astype(F32) + back_ref[which].astype(F32) for which in (0, 1)
    )
    out_ref[...] = (
        x + mlp_out + b_ref[...] + dot_nn(jnp.transpose(att_s[...]), w_attn_ref[...])
    ).astype(BF)
    normed_grad = mlp_grad + dot_nt(jnp.transpose(grad_s[...]), w_ref[...])
    hat, scale = normalized(x, 1)
    grad = normed_grad * gain_ref[...]
    grad_ref[...] = dy_ref[...].astype(F32) + scale * (
        grad
        - jnp.mean(grad, axis=1, keepdims=True)
        - hat * jnp.mean(grad * hat, axis=1, keepdims=True)
    )


def token_results(coords, shifts, pieces, x, dy, ln_gain, near, far, back, b_out, w_attn_out, w_qkv):
    rows, width = x.shape
    inputs = [*pieces, x, dy, ln_gain, near, far, back, b_out, w_attn_out, w_qkv]
    return call(
        functools.partial(tokens_kernel, shifts),
        coords,
        inputs,
        [whole(array.shape) for array in inputs],
        [struct((rows, width), BF), struct((rows, width), F32)],
        [whole((rows, width))] * 2,
        [pltpu.VMEM((width, rows), BF), pltpu.VMEM((3 * width, rows), BF)],
        name="token_results",
    )


HALVE, BOTH, KEEP = range(3)


def stage_kernel(segments, bit, coords, keep_ref, came_ref, *out_refs):
    keep_at = came_at = kept = sent = 0
    for rows, came, mode in segments:
        total = keep_ref[keep_at : keep_at + rows, :]
        if came:
            total = (total.astype(F32) + came_ref[came_at : came_at + rows, :].astype(F32)).astype(BF)
            came_at += rows
        keep_at += rows
        if mode == HALVE:
            half = rows // 2
            for value in (0, 1):

                @pl.when(coords[bit] == value)
                def _():
                    out_refs[0][kept : kept + half, :] = total[value * half : (value + 1) * half]
                    out_refs[1][sent : sent + half, :] = total[(1 - value) * half : (2 - value) * half]

            kept += half
            sent += half
        else:
            out_refs[0][kept : kept + rows, :] = total
            kept += rows
            if mode == BOTH:
                out_refs[1][sent : sent + rows, :] = total
                sent += rows


def stage(coords, segments, bit, keep, came):
    width = keep.shape[1]
    kept = sum(rows // 2 if mode == HALVE else rows for rows, _came, mode in segments)
    sent = sum({HALVE: rows // 2, BOTH: rows, KEEP: 0}[mode] for rows, _came, mode in segments)
    shapes = [(kept, width)] + ([(sent, width)] if sent else [])
    return call(
        functools.partial(stage_kernel, segments, bit),
        coords,
        [keep, came],
        [whole(keep.shape), whole(came.shape)],
        [struct(shape, BF) for shape in shapes],
        [whole(shape) for shape in shapes],
        name="stage",
    )


def first_stage_kernel(counts, coords, *refs):
    (*shares, keep_ref, send_ref) = refs
    attn, rows = HD // 2, 3 * HD // 2
    blocks = [count * rows + EXTRA for count in counts]
    pairs = list(zip(blocks, counts, shares[::2], shares[1::2], strict=True))
    for value in (0, 1):

        @pl.when(coords[GRP] == value)
        def _():
            for pack, target in ((value, keep_ref), (1 - value, send_ref)):
                extra, at = 0.0, 0
                for block, count, own, came in pairs:
                    span = slice(pack * block, (pack + 1) * block)
                    total = own[span, :].astype(F32) + came[span, :].astype(F32)
                    target[at : at + count * rows, :] = total[: count * rows].astype(BF)
                    extra = extra + total[count * rows :]
                    at += count * rows
                target[PER_Z * (rows + 2 * attn) :, :] = extra.astype(BF)

    before = 0
    for block, count, own, came in pairs:
        total = (own[2 * block :, :].astype(F32) + came[2 * block :, :].astype(F32)).astype(BF)
        for side in (0, 1):
            start = PER_Z * rows + (side * PER_Z + before) * attn
            for target in (keep_ref, send_ref):
                target[start : start + count * attn, :] = total[
                    side * count * attn : (side + 1) * count * attn
                ]
        before += count


def first_stage(coords, counts, shares):
    half = shares[0].shape[1]
    shape = (PER_Z * (3 * HD // 2 + HD) + EXTRA, half)
    return call(
        functools.partial(first_stage_kernel, counts),
        coords,
        shares,
        [whole(share.shape) for share in shares],
        [struct(shape, BF)] * 2,
        [whole(shape)] * 2,
        name="first_stage",
    )


def mlp_place_kernel(coords, *refs):
    units, (w_ref, rows_ref, columns_ref, sum_ref, turn_s) = refs[:8], refs[8:]
    step = pl.program_id(0)
    part, half = units[0].shape[1] // 2, units[0].shape[2] // 2
    low, high = coords[Z_LOW], coords[Z_HIGH]

    @pl.when(step == 0)
    def _():
        sum_ref[...] = jnp.zeros_like(sum_ref)

    chosen = (step % 2 ^ coords[CORE]) * 4 + (step // 2 ^ coords[TOP]) * 2 + low
    for i in range(8):

        @pl.when(chosen == i)
        def _():
            for shard in range(Z_COUNT):
                rows_ref[shard * part : (shard + 1) * part, :] = units[i ^ (shard // 2)][
                    shard % 2 ^ high, :part, :
                ].astype(F32)

    lanes = pl.ds(pl.multiple_of((step // 2) * half, 128), half)
    chosen = coords[CORE] * 4 + (step % 2 ^ coords[TOP]) * 2 + low
    for i in range(8):

        @pl.when(chosen == i)
        def _():
            for core in (0, 1):
                for shard in range(Z_COUNT):
                    row = (core * Z_COUNT + shard) * part
                    unit = units[i ^ (4 * core) ^ (shard // 2)]
                    turn_s[row : row + part, :] = unit[shard % 2 ^ high, part:, lanes].astype(F32)

    total = 0.0
    for block in range(SHARDS * part // 128):
        span = slice(block * 128, (block + 1) * 128)
        turned = jnp.transpose(turn_s[span, :])
        columns_ref[:, span] = turned
        total = total + turned * w_ref[:, span].astype(F32)
    sum_ref[...] += jnp.sum(total, axis=1, keepdims=True)


def place_mlp(coords, units, w_in):
    _shards, rows, width = units[0].shape
    part, half = rows // 2, width // 2
    span = SHARDS * part
    return call(
        mlp_place_kernel,
        coords,
        [*units, w_in],
        [whole(unit.shape) for unit in units]
        + [pl.BlockSpec((half, span), lambda s, c: (c[GRP], s))],
        [
            struct((2 * span, width), F32),
            struct((half, 4 * span), F32),
            struct((half, 1), F32),
        ],
        [
            pl.BlockSpec((Z_COUNT * part, width), lambda s, c: (s, 0)),
            pl.BlockSpec((half, span), lambda s, c: (0, s)),
            whole((half, 1)),
        ],
        [pltpu.VMEM((span, half), F32)],
        grid=(4,),
        name="place_mlp",
    )


def heads_kernel(coords, *refs):
    (*unit_refs, w_ref, gain_ref, sum_ref, qkv_ref, attn_ref, ln_ref, turn_s) = refs
    half = unit_refs[0].shape[2]
    width = 2 * half
    q_rows, a_rows, unit = 3 * PER_Z * HD // 4, PER_Z * HD // 2, 16
    per_head = 3 * HD // 2 // unit
    for relative in range(8):
        block = unit_refs[relative // 2][relative % 2].astype(F32)
        core = coords[CORE] ^ (relative // 4)
        top = coords[TOP] ^ (relative // 2 % 2)
        low = coords[Z_LOW] ^ (relative % 2)
        for side in (0, 1):
            z_index = low + 2 * (coords[Z_HIGH] ^ side)
            for i in range(q_rows // unit):
                number = top * (q_rows // unit) + i
                inner = number % per_head + core * per_head
                row = (inner // (HD // unit)) * width + (inner % (HD // unit)) * unit
                row = row + (z_index * PER_Z + number // per_head) * HD
                turn_s[pl.ds(pl.multiple_of(row, unit), unit), :] = block[
                    side * q_rows + i * unit : side * q_rows + (i + 1) * unit
                ]
        lanes = pl.ds(pl.multiple_of(top * half, 128), half)
        for head in range(PER_Z):
            row = pl.multiple_of((low * PER_Z + head) * HD + core * (HD // 2), HD // 2)
            start = 2 * q_rows + head * (HD // 2)
            attn_ref[pl.ds(row, HD // 2), lanes] = block[start : start + HD // 2]
    total = 0.0
    for block in range(3 * width // 128):
        span = slice(block * 128, (block + 1) * 128)
        turned = jnp.transpose(turn_s[span, :])
        qkv_ref[:, span] = turned
        total = total + turned * w_ref[:, span].astype(F32)
    ln = (jnp.sum(total, axis=1, keepdims=True) + sum_ref[...]) / gain_ref[...]
    ln_ref[...] = jnp.transpose(jnp.broadcast_to(ln, (half, 128)))[0]


def place_heads(coords, units, w_qkv, gain_column, in_sums):
    half = units[0].shape[2]
    width = 2 * half
    row_half = lambda columns: pl.BlockSpec((half, columns), lambda s, c: (c[GRP], 0))
    return call(
        heads_kernel,
        coords,
        [*units, w_qkv, gain_column, in_sums],
        [whole(unit.shape) for unit in units] + [row_half(3 * width), row_half(1), whole((half, 1))],
        [struct((half, 3 * width), F32), struct((half, width), F32), struct((half,), F32)],
        [whole((half, 3 * width)), whole((half, width)), whole((half,))],
        [pltpu.VMEM((3 * width, half), F32)],
        name="place_heads",
    )


def per_device(
    tokens, lengths, image_ids, ln_gain, w_qkv, q_gain, k_gain,
    w_attn_out, w_in, b_in, w_mlp_out, b_out, cotangent,
):
    x, dy = tokens[0], cotangent[0]
    rows, width = x.shape
    half = width // 2
    hidden = w_in.shape[1]
    seq_count = lax.axis_size("seq")
    rest = seq_count // Z_COUNT
    rest_bits = rest.bit_length() - 1
    top_bit = rest_bits - 1
    me = lax.axis_index("seq")
    z_index, r_index = me // rest, me % rest
    grp = lax.axis_index("grp")
    core, top = r_index & 1, r_index >> top_bit
    coords = jnp.stack([grp, core, top, z_index & 1, z_index >> 1]).astype(jnp.int32)

    def z_shift(block, distance):
        route = [(i, (i + distance * rest) % seq_count) for i in range(seq_count)]
        return lax.ppermute(block, "seq", route)

    def flip(mask):
        route = [(i, i ^ mask) for i in range(seq_count)]
        return lambda block: lax.ppermute(block, "seq", route)

    def swap_packs(block):
        return lax.ppermute(block, "grp", [(0, 1), (1, 0)])

    swap_core, swap_top = flip(1), flip(1 << top_bit)
    swap_low, swap_high = flip(rest), flip(2 * rest)
    others = range(1, top_bit)

    def add(*terms):
        return sum(term.astype(F32) for term in terms).astype(BF)

    def after(value, *events):
        return lax.optimization_barrier((value, *events))[0]

    def after(value, *events):
        return lax.optimization_barrier((value, *events))[0]

    turn = [coords]

    def then(results):
        if isinstance(results, (list, tuple)):
            return [then(results[0]), *results[1:]]
        turn[0], results = lax.optimization_barrier((turn[0], results))
        return results

    def until(*events):
        turn[0] = after(turn[0], *events)

    shifts = [0, 1, 3, 2]
    x_slots = {0: x, **{d: z_shift(x, d) for d in (1, 3, 2)}}
    mine, gb_out, *do_pieces = then(prep(coords, shifts, x, dy, w_attn_out))
    across, other = swap_top(mine), swap_core(mine)
    mlp_weights = (ln_gain.reshape(1, width), w_in, b_in.reshape(1, hidden), w_mlp_out)
    near, near_far, *before = then(mlp(turn[0], [mine, other], *mlp_weights))
    near_far = swap_core(near_far)

    order = image_ids[0]
    labels = jnp.arange(order.shape[0], dtype=jnp.int32)
    ordered = jnp.sum(jnp.where(order[:, None] == labels[None, :], lengths[0][None, :], 0), axis=1)
    ends = jnp.cumsum(ordered)
    offsets = jnp.arange(rows, dtype=jnp.int32)
    slot_z = (z_index - jnp.array(shifts, dtype=jnp.int32)) % Z_COUNT
    masks = [2 * i for i in range(rest // 2)] + [2 * i + 1 for i in range(rest // 2)]
    source_r = r_index ^ jnp.array(masks, dtype=jnp.int32)
    starts = (slot_z[None, :] * rest + source_r[:, None]) * rows
    places = (starts[:, :, None] + offsets).reshape(rest, Z_COUNT * rows)
    images = jnp.sum((places[:, :, None] >= ends).astype(jnp.int32), axis=2).astype(F32)
    key_images = images[:, None, :]
    query_images = images[:1]

    ln_row = ln_gain.reshape(1, width)
    q_col, k_col = q_gain.reshape(1, HD), k_gain.reshape(1, HD)

    until(query_images, key_images)
    normed, q, kv_first, kv_rest, raw = then(
        qkv(turn[0], [x_slots[d] for d in shifts], ln_row, w_qkv, q_col, k_col)
    )
    normed_groups, q_groups, raw_groups = [normed], [q], [raw]

    def spread(group, bits):
        for bit in bits:
            group = {**group, **{m | 1 << bit: flip(1 << bit)(block) for m, block in group.items()}}
        return group

    upper = list(reversed(range(1, rest_bits)))
    do_slots = [
        z_shift(after(piece, normed), d) if d else piece
        for piece, d in zip(do_pieces, shifts, strict=True)
    ]
    kv_first = spread({0: kv_first}, upper)
    mid, far, mlp_keep, mlp_send, gb_in = then(
        mlp(turn[0], [across, swap_core(after(across, near))], *mlp_weights, before)
    )
    mlp_came = swap_packs(mlp_send)
    kv_first = {m: after(block, mlp_keep, *do_slots[1:]) for m, block in kv_first.items()}
    kv_here = after(kv_rest, kv_first[1 << top_bit])
    kv_first = spread(kv_first, [0])
    kv_rest = spread({0: kv_here}, upper)
    dy_slots = {0: dy, **{d: z_shift(after(dy, kv_first[1]), d) for d in (1, 3)}}

    shares = []

    def finish(heads, parts, before=()):
        results = then(
            post(
                heads, turn[0], parts, raw_groups, normed_groups, dy_list, q_col, k_col, gb_in, gb_out, before
            )
        )
        shares.extend([results[Z_COUNT], swap_core(results[Z_COUNT + 1])])
        return results[:Z_COUNT]

    waiting = []

    def halve(keep, came, bit, move):
        size = keep.shape[0] // 2
        rows_of = lambda array, which: lax.dynamic_slice_in_dim(array, which * size, size, 0)
        gone = then(add(rows_of(keep, 1 - bit), rows_of(came, 1 - bit)))
        keep = then(add(rows_of(keep, bit), rows_of(came, bit)))
        return keep, move(gone)

    far = swap_core(far)
    back_sum = add(mid, far)
    kv_sources = [[(kv_first[m], 0) for m in masks]]
    for head in range(PER_Z):
        out_t, dq_t, low, high = then(
            attention(head, turn[0], q_groups, do_slots, kv_sources[head], query_images, key_images)
        )
        if head == 0:
            high = after(high, kv_rest[1 << top_bit])
            kv_rest = spread({m: after(block, dq_t) for m, block in kv_rest.items()}, [0])
            kv_sources += [[(kv_rest[m], place) for m in masks] for place in (0, 1)]
            high = after(high, dy_slots[1], dy_slots[3])
            dy_slots[2] = z_shift(after(dy, dq_t), 2)
            back = swap_top(after(back_sum, dq_t))
        elif head > 1:
            high = after(high, *waiting[-1][2][2:])
        if head == 2:
            high = after(high, *waiting[0][2][2:])
        if head:
            high = after(high, mlp_came)
        if head == 1:
            high = after(high, dy_slots[2])
            dy_list = [dy_slots[d] for d in shifts]
            high = after(high, back)
        came = swap_core(high)

        def mlp_step():
            if head < 2:
                bit, move = ((z_index & 1, swap_low), (z_index >> 1, swap_high))[head]
                return halve(after(mlp_keep, turn[0]), mlp_came, bit, move)
            share = then(add(after(mlp_keep, turn[0]), mlp_came))
            for bit in others:
                share = add(share, flip(1 << bit)(share))
            return share[None], swap_high(share[None])

        if head:
            mlp_keep, mlp_came = mlp_step()
        parts = {2 * i: [low[i : i + 1], came[i : i + 1]] for i in range(rest // 2)}
        for bit in range(1, rest_bits):
            for mask in sorted(m for m in parts if m >> bit & 1):
                total = then(add(*parts.pop(mask)))
                parts[mask ^ (1 << bit)].append(flip(1 << bit)(total))
        if not head:
            mlp_keep, mlp_came = mlp_step()
        waiting.append((dq_t, out_t, [low, came, *parts[0][2:]]))
    some = finish([0, 1], waiting[:2])
    late = finish([2], waiting[2:], some)
    units_here = then(jnp.concatenate([after(mlp_keep, turn[0]), mlp_came], axis=0))
    units_low, units_top = swap_low(units_here), swap_top(units_here)
    send_piece = lambda slot, *events: z_shift(after(late[slot], *events), -shifts[slot])
    pieces = [late[0], None, None, z_shift(late[3], -shifts[3])]

    keep, send = then(first_stage(turn[0], [2, 1], shares))
    q_size, a_size = 3 * PER_Z * HD // 2, PER_Z * HD
    came = swap_packs(send)
    units_both = swap_top(after(units_low, keep))
    until(units_low, units_top)
    until(pieces[3])
    keep, send = then(
        stage(
            turn[0],
            [(q_size, True, HALVE), (a_size, True, HALVE), (EXTRA, True, BOTH)],
            TOP, keep, came,
        )
    )
    q_size, a_size = q_size // 2, a_size // 2
    came = swap_top(send)
    pieces[1] = send_piece(1, keep)
    came = after(came, pieces[1])
    share = then(add(keep, came))
    for bit in others:
        share = add(share, flip(1 << bit)(share))
    came = swap_high(share)
    pieces[2] = send_piece(2, came)
    near_parts = (near, near_far, back)
    mlp_units = [units_here, units_low, units_top, units_both]
    mlp_units += [swap_core(after(unit, share)) for unit in mlp_units]
    middle = q_size + a_size
    attn = jnp.where(z_index >> 1 == grp, share[q_size:middle], came[q_size:middle])
    small = add(share[middle:], came[middle:])
    unit = then(jnp.concatenate([share[:q_size], came[:q_size], attn, small], axis=0))
    came = swap_low(unit)
    grad_w_mlp_out, grad_w_in, in_sums = then(place_mlp(turn[0], mlp_units, w_in))
    came = after(came, grad_w_in)
    size = unit.shape[0] - EXTRA
    small = add(unit[size:], came[size:]).astype(F32)
    units = then(jnp.stack([unit[:size], came[:size]]))
    came = swap_top(units)
    result, grad_tokens = then(
        token_results(
            turn[0], shifts, pieces, x, dy, ln_row, *near_parts, b_out.reshape(1, width), w_attn_out, w_qkv
        )
    )
    came = after(came, result)
    all_units = [units, came, swap_core(units), swap_core(came)]

    grad_w_qkv, grad_w_attn_out, grad_ln_gain = place_heads(
        coords, all_units, w_qkv, ln_gain.reshape(width, 1), in_sums
    )
    return (
        result[None],
        grad_tokens[None],
        grad_ln_gain,
        grad_w_qkv,
        lax.dynamic_slice(small[5], (grp * (HD // 2),), (HD // 2,)),
        lax.dynamic_slice(small[5], (HD + grp * (HD // 2),), (HD // 2,)),
        grad_w_attn_out,
        grad_w_in,
        small[1:5].reshape(hidden // 2),
        grad_w_mlp_out,
        small[0],
    )


def solution(mesh):
    placed = (
        P("grp", "seq", None), P("grp", None), P("grp", None),
        P(), P(), P(), P(), P(), P(), P(), P(), P(), P("grp", "seq", None),
    )
    return jax.shard_map(
        per_device,
        mesh=mesh,
        in_specs=placed,
        out_specs=(
            P("grp", "seq", None), P("grp", "seq", None), P("grp"), P("grp", None), P("grp"),
            P("grp"), P("grp", None), P("grp", None), P("grp"), P("grp", None), P("grp"),
        ),
        check_vma=False,
    )
```

```python
import functools

import jax
import jax.numpy as jnp
from jax import lax
from jax.experimental import pallas as pl
from jax.experimental.pallas import tpu as pltpu
from jax.sharding import PartitionSpec as P

H = 12
HD = 64
Z_COUNT = 4
PER_Z = H // Z_COUNT
EPSILON = 1e-06
BF = jnp.bfloat16
F32 = jnp.float32
VMEM_BYTES = 58 * 1024 * 1024
FLOPS_PER_US = 1_150_000_000


def params():
    return pltpu.CompilerParams(vmem_limit_bytes=VMEM_BYTES)


def dot_nn(left, right):
    return lax.dot_general(left, right, (((1,), (0,)), ((), ())), preferred_element_type=F32)


def dot_nt(left, right):
    return lax.dot_general(left, right, (((1,), (1,)), ((), ())), preferred_element_type=F32)


def dot_tn(left, right):
    return lax.dot_general(left, right, (((0,), (0,)), ((), ())), preferred_element_type=F32)


def whole(shape):
    return pl.BlockSpec(shape, lambda *_: (0,) * len(shape))


def normalized(values, axis):
    mean = jnp.mean(values, axis=axis, keepdims=True)
    centred = values - mean
    spread = jnp.mean(centred * centred, axis=axis, keepdims=True)
    scale = lax.rsqrt(spread + EPSILON)
    return centred * scale, scale


GRP, CORE, TOP, Z_LOW, Z_HIGH = range(5)
SHARDS = 8


COST_US = {
    "prep": 18,
    "mlp1": 0,
    "mlp2": 40,
    "qkv": 5,
    "attention0": 18,
    "attention1": 18,
    "attention2": 18,
    "post01": 18,
    "post2": 0,
    "first_stage": 0,
    "stage": 0,
    "token_results": 11,
    "place_mlp": 9,
    "place_heads": 8,
}


def cost(us):
    return pl.CostEstimate(flops=us * FLOPS_PER_US, bytes_accessed=0, transcendentals=0)


def call(body, scalars, inputs, in_specs, out_shapes, out_specs, scratch=(), grid=(1,), name=None):
    return pl.pallas_call(
        body,
        grid_spec=pltpu.PrefetchScalarGridSpec(
            num_scalar_prefetch=1,
            grid=grid,
            in_specs=in_specs,
            out_specs=out_specs,
            scratch_shapes=list(scratch),
        ),
        out_shape=out_shapes,
        compiler_params=params(),
        cost_estimate=cost(COST_US[name]),
        name=name,
    )(scalars, *inputs)


def struct(shape, dtype):
    return jax.ShapeDtypeStruct(shape, dtype)


def column(row):
    return jnp.transpose(jnp.broadcast_to(row, (8, row.shape[1])))[:, :1]


def prep_kernel(shifts, coords, x_ref, dy_ref, w_ref, pair_ref, sum_ref, *refs):
    out_refs, grad_s = refs[:-1], refs[-1]
    pair_ref[0] = x_ref[...]
    dy = dy_ref[...]
    pair_ref[1] = dy
    sum_ref[...] = jnp.sum(dy.astype(F32), axis=0, keepdims=True)
    grad_s[...] = dot_nt(w_ref[...], dy).astype(BF)
    z_index = coords[Z_LOW] + 2 * coords[Z_HIGH]
    depth = PER_Z * HD
    for shift, out_ref in zip(shifts, out_refs, strict=True):
        row = pl.multiple_of(lax.rem(z_index + shift, Z_COUNT) * depth, depth)
        out_ref[...] = grad_s[pl.ds(row, depth), :]


def prep(coords, shifts, x, dy, w_attn_out):
    rows, width = dy.shape
    piece = (PER_Z * HD, rows)
    return call(
        functools.partial(prep_kernel, shifts),
        coords,
        [x, dy, w_attn_out],
        [whole((rows, width))] * 2 + [whole((width, width))],
        [struct((2, rows, width), BF), struct((1, width), F32)] + [struct(piece, BF)] * len(shifts),
        [whole((2, rows, width)), whole((1, width))] + [whole(piece)] * len(shifts),
        [pltpu.VMEM((width, rows), BF)],
        name="prep",
    )


def mlp_kernel(second, coords, *refs):
    pairs, refs = refs[:2], refs[2:]
    gain_ref, w_in_refs, b_in_refs, w_out_refs, refs = refs[0], refs[1:3], refs[3:5], refs[5:7], refs[7:]
    w_in = jnp.concatenate([ref[...] for ref in w_in_refs], axis=1)
    b_in = jnp.concatenate([ref[...] for ref in b_in_refs], axis=1)
    w_out = jnp.concatenate([ref[...] for ref in w_out_refs], axis=0)
    before, refs = (refs[:3], refs[3:]) if second else ((), refs)
    (near_ref, far_ref), refs = refs[:2], refs[2:]
    rows = pairs[0].shape[1]
    normed = []
    for pair in pairs:
        hat, _unused = normalized(pair[0].astype(F32), 1)
        normed.append((hat * gain_ref[...]).astype(BF))
    normed = jnp.concatenate(normed, axis=0)
    dy = jnp.concatenate([pair[1] for pair in pairs], axis=0)
    pre = dot_nn(normed, w_in) + b_in
    square = pre * pre
    tanh = jnp.tanh(pre * (0.7978845608028654 + 0.03567740813630193 * square))
    half = 0.5 + 0.5 * tanh
    hidden = (pre * half).astype(BF)
    slope = half + pre * (0.5 - 0.5 * tanh * tanh) * (
        0.7978845608028654 + 0.10703222440890579 * square
    )
    grad_pre = (slope * dot_nt(dy, w_out)).astype(BF)
    for which, total in enumerate((dot_nn(hidden, w_out), dot_nt(grad_pre, w_in))):
        near_ref[which] = total[:rows, :].astype(near_ref.dtype)
        far_ref[which] = total[rows:, :].astype(BF)
    gb_in = jnp.sum(grad_pre.astype(F32), axis=0, keepdims=True)
    g_out = dot_nn(jnp.transpose(hidden), dy)
    g_in = dot_nn(jnp.transpose(grad_pre), normed)
    if not second:
        g_out_ref, g_in_ref, gb_in_ref = refs
        g_out_ref[...] = g_out.astype(BF)
        g_in_ref[...] = g_in.astype(BF)
        gb_in_ref[...] = gb_in
        return
    g_out_before, g_in_before, gb_in_before = before
    keep_ref, send_ref, gb_in_ref = refs
    gb_in_ref[...] = gb_in + gb_in_before[...]
    g_out = (g_out + g_out_before[...].astype(F32)).astype(BF)
    g_in = (g_in + g_in_before[...].astype(F32)).astype(BF)
    part, half = g_out.shape[0] // SHARDS, g_out.shape[1] // 2
    first = Z_COUNT * part
    for value in (0, 1):

        @pl.when(coords[GRP] == value)
        def _():
            for shard in range(Z_COUNT):
                at, row = 2 * shard * part, shard * part
                for target, pack in ((keep_ref, value), (send_ref, 1 - value)):
                    start = pack * first + row
                    target[at : at + part, :] = g_out[start : start + part, :]
                    lanes = slice(pack * half, (pack + 1) * half)
                    target[at + part : at + 2 * part, :half] = g_in[row : row + part, lanes]
                    target[at + part : at + 2 * part, half:] = g_in[first + row : first + row + part, lanes]


def mlp(coords, pairs, ln_gain, w_in, b_in, w_out, before=()):
    _two, rows, width = pairs[0].shape
    own = w_in.shape[1] // 4
    second = bool(before)
    place = lambda c, side: side * 4 + c[TOP] * 2 + c[CORE]
    columns = lambda rows, side: pl.BlockSpec((rows, own // 2), lambda s, c: (0, place(c, side)))
    outs = [
        struct((2, rows, width), BF if second else F32),
        struct((2, rows, width), BF),
        struct((own, width), BF),
        struct((own, width), BF),
        struct((1, own), F32),
    ]
    return call(
        functools.partial(mlp_kernel, second),
        coords,
        [*pairs, ln_gain, w_in, w_in, b_in, b_in, w_out, w_out, *before],
        [whole((2, rows, width))] * 2
        + [
            whole((1, width)),
            columns(width, 0),
            columns(width, 1),
            columns(1, 0),
            columns(1, 1),
            pl.BlockSpec((own // 2, width), lambda s, c: (place(c, 0), 0)),
            pl.BlockSpec((own // 2, width), lambda s, c: (place(c, 1), 0)),
        ]
        + [whole(array.shape) for array in before],
        outs,
        [whole(out.shape) for out in outs],
        name="mlp2" if second else "mlp1",
    )


def qkv_kernel(count, coords, *refs):
    x_refs, refs = refs[:count], refs[count:]
    w_refs, refs = refs[:6], refs[6:]
    gain_ref, q_gain_ref, k_gain_ref, normed_ref, q_ref, first_ref, kv_ref, raw_ref, w_s, turn_s = refs
    rows = x_refs[0].shape[0]
    zeros = jnp.zeros((HD, rows), F32)
    q_gain, k_gain = column(q_gain_ref[...]), column(k_gain_ref[...])
    for i, w_ref in enumerate(w_refs):
        w_s[:, i * 128 : (i + 1) * 128] = w_ref[...]
    for slot in range(count):
        span = slice(slot * rows, (slot + 1) * rows)
        hat, _unused = normalized(x_refs[slot][...].astype(F32), 1)
        normed = (hat * gain_ref[...]).astype(BF)
        normed_ref[span, :] = normed
        projected = dot_nn(normed, w_s[...])
        turn_s[slot] = jnp.transpose(projected)
    for slot in range(count):
        span = slice(slot * rows, (slot + 1) * rows)
        for head in range(PER_Z):
            q_raw, k_raw, v = (
                turn_s[slot, pl.ds(pl.multiple_of(part * 256 + head * HD + coords[Z_LOW] * HD, HD), HD), :]
                for part in range(3)
            )
            raw_ref[head, :HD, span] = q_raw
            raw_ref[head, HD:, span] = k_raw
            q = normalized(q_raw, 0)[0] * q_gain * HD ** (-0.5)
            k = normalized(k_raw, 0)[0] * k_gain
            q_ref[head, span, :] = jnp.transpose(jnp.concatenate([q, zeros], axis=0)).astype(BF)
            target = kv_ref if head else first_ref
            target[max(head - 1, 0), span, :] = jnp.transpose(jnp.concatenate([k, v], axis=0)).astype(BF)


def qkv(coords, blocks, ln_gain, w_qkv, q_gain, k_gain):
    rows, width = blocks[0].shape
    count = len(blocks)
    total = count * rows

    def columns(part, second):
        first = lambda c: 3 * (c[Z_LOW] + 2 * c[Z_HIGH]) // 2
        return pl.BlockSpec((width, 128), lambda i, c: (0, part * (width // 128) + first(c) + second))

    shapes = [
        struct((total, width), BF),
        struct((PER_Z, total, 2 * HD), BF),
        struct((1, total, 2 * HD), BF),
        struct((PER_Z - 1, total, 2 * HD), BF),
        struct((PER_Z, 2 * HD, total), F32),
    ]
    return call(
        functools.partial(qkv_kernel, count),
        coords,
        [*blocks, *[w_qkv] * 6, ln_gain, q_gain, k_gain],
        [whole((rows, width))] * count
        + [columns(part, second) for part in range(3) for second in range(2)]
        + [whole((1, width)), whole((1, HD)), whole((1, HD))],
        shapes,
        [whole(shape.shape) for shape in shapes],
        [pltpu.VMEM((width, 768), BF), pltpu.VMEM((count, 768, rows), F32)],
        name="qkv",
    )


def attention_kernel(groups, slots, sources, coords, *refs):
    count = len(groups)
    q_refs, refs = refs[:count], refs[count:]
    do_refs, refs = refs[:slots], refs[slots:]
    kv_refs, refs = refs[:sources], refs[sources:]
    qi_ref, ki_ref, out_ref, *refs = refs
    dq_ref, low_ref, high_ref, q_s, do_s, kv_s, one_v_s, e_s, acc_s = refs
    rows = sum(groups)
    tokens = rows // slots
    start = 0
    for group, size in enumerate(groups):
        q_s[start : start + size, :] = q_refs[group][0]
        start += size
    lane = lax.broadcasted_iota(jnp.int32, (rows, 2 * HD), 1)
    for source in range(sources):
        block = kv_refs[source][0]
        kv_s[source] = block
        one_v_s[source] = jnp.where(lane < HD, jnp.ones((), BF), block)
    for slot in range(slots):
        grad = do_refs[slot][...].astype(F32)
        do_s[slot * tokens : (slot + 1) * tokens, :] = jnp.transpose(
            jnp.concatenate([jnp.zeros_like(grad), grad], axis=0)
        )
    acc_s[...] = jnp.zeros_like(acc_s)
    query_images = column(qi_ref[...])

    def forward(source, carry):
        scores = dot_nt(q_s[...], kv_s[source])
        same = query_images == ki_ref[source]
        weights = jnp.where(same, jnp.exp(scores), 0.0).astype(BF)
        e_s[source] = weights
        acc_s[...] += dot_nn(weights, one_v_s[source])
        return carry

    lax.fori_loop(0, sources, forward, 0)
    acc = acc_s[...]
    wide = lax.broadcasted_iota(jnp.int32, (rows, 2 * HD), 1)
    attended = jnp.where(wide >= HD, acc / pltpu.roll(acc, HD, 1), 0.0)
    inverse = 1.0 / acc[:, 0:1]
    do = do_s[...]
    out_dot = jnp.sum(do * attended, axis=1, keepdims=True) * inverse
    coarse = out_dot.astype(BF).astype(F32)
    do = do * inverse
    probe = jnp.where(wide == 0, -coarse, jnp.where(wide == 1, coarse - out_dot, do)).astype(BF)
    out_ref[...] = jnp.transpose(attended)[HD:].astype(BF)
    q_t = jnp.transpose(q_s[...].astype(F32))[:HD].astype(BF)
    do_t = jnp.transpose(do)[HD:].astype(BF)
    acc_s[...] = jnp.zeros_like(acc_s)

    def backward_into(dkv_ref, first):
        def backward(source, carry):
            weights = e_s[first + source]
            grad_weights = dot_nt(probe, one_v_s[first + source])
            grad_scores = (weights.astype(F32) * grad_weights).astype(BF)
            acc_s[...] += dot_nn(grad_scores, kv_s[first + source])
            dkv_ref[source, :HD, :] = dot_nn(q_t, grad_scores).astype(BF)
            dkv_ref[source, HD:, :] = dot_nn(do_t, weights).astype(BF)
            return carry

        lax.fori_loop(0, sources // 2, backward, 0)

    backward_into(high_ref, sources // 2)
    backward_into(low_ref, 0)
    dq_ref[...] = jnp.transpose(acc_s[...])[:HD]


def attention(head, coords, q_groups, do_slots, kv_sources, query_images, key_images):
    groups = [q.shape[1] for q in q_groups]
    slots, sources = len(do_slots), len(kv_sources)
    rows = sum(groups)
    parts = [pl.BlockSpec((1, size, 2 * HD), lambda i, c: (head, 0, 0)) for size in groups]
    place = kv_sources[0][1]
    kv_part = pl.BlockSpec((1, rows, 2 * HD), lambda i, c: (place, 0, 0))
    do_part = pl.BlockSpec((HD, rows // slots), lambda i, c: (head, 0))
    half = (sources // 2, 2 * HD, rows)
    return call(
        functools.partial(attention_kernel, groups, slots, sources),
        coords,
        [*q_groups, *do_slots, *[source[0] for source in kv_sources], query_images, key_images],
        parts
        + [do_part] * slots
        + [kv_part] * sources
        + [whole((1, rows)), whole((sources, 1, rows))],
        [struct((HD, rows), BF), struct((HD, rows), F32), struct(half, BF), struct(half, BF)],
        [whole((HD, rows)), whole((HD, rows)), whole(half), whole(half)],
        [
            pltpu.VMEM((rows, 2 * HD), BF),
            pltpu.VMEM((rows, 2 * HD), F32),
            pltpu.VMEM((sources, rows, 2 * HD), BF),
            pltpu.VMEM((sources, rows, 2 * HD), BF),
            pltpu.VMEM((sources, rows, rows), BF),
            pltpu.VMEM((rows, 2 * HD), F32),
        ],
        name=f"attention{head}",
    )


EXTRA = 16


def post_kernel(groups, slots, terms, heads, earlier, coords, *refs):
    count = len(groups)
    per_head = []
    for _head in heads:
        per_head.append((refs[0], refs[1], refs[2 : 2 + terms], refs[2 + terms : 2 + terms + count]))
        refs = refs[2 + terms + count :]
    normed_refs, dy_refs, refs = refs[:count], refs[count : count + slots], refs[count + slots :]
    (q_gain_ref, k_gain_ref, b_in_ref, b_out_ref), refs = refs[:4], refs[4:]
    before, refs = refs[:earlier], refs[earlier:]
    piece_refs, (keep_ref, send_ref) = refs[:slots], refs[slots:]
    tokens = piece_refs[0].shape[1]
    for ref, piece_ref in zip(before, piece_refs):
        piece_ref[: ref.shape[0], :] = ref[...]
    half = keep_ref.shape[1]
    rows, attn = 3 * HD // 2, HD // 2
    block = len(heads) * rows + EXTRA
    gains = [0.0, 0.0]
    q_gain, k_gain = column(q_gain_ref[...]), column(k_gain_ref[...])
    for place, (dq_ref, out_ref, term_refs, raw_refs) in enumerate(per_head):
        total = attn_total = None
        start = 0
        for group, size in enumerate(groups):
            span = slice(start, start + size)
            dkv = sum(term[0][:, span].astype(F32) for term in term_refs)
            grads = []
            for which, (grad, gain) in enumerate(
                ((dq_ref[:, span], q_gain * HD ** (-0.5)), (dkv[:HD], k_gain))
            ):
                hat, scale = normalized(raw_refs[group][0, which * HD : (which + 1) * HD, :], 0)
                factor = HD ** (-0.5) if which == 0 else 1.0
                gains[which] += jnp.sum(grad * hat, axis=1, keepdims=True) * factor
                grad = grad * gain
                grad = scale * (
                    grad
                    - jnp.mean(grad, axis=0, keepdims=True)
                    - hat * jnp.mean(grad * hat, axis=0, keepdims=True)
                )
                grads.append(grad)
            grads.append(dkv[HD:])
            projected_grad = jnp.concatenate(grads, axis=0).astype(BF)
            first = (place + (heads[0] if before else 0)) * 4 * HD
            for slot in range(start // tokens, (start + size) // tokens):
                inner = slice(slot * tokens - start, (slot + 1) * tokens - start)
                outer = slice(slot * tokens, (slot + 1) * tokens)
                piece_refs[slot][first : first + 3 * HD, :] = projected_grad[:, inner]
                piece_refs[slot][first + 3 * HD : first + 4 * HD, :] = out_ref[:, outer]
                term = dot_nn(out_ref[:, outer], dy_refs[slot][...])
                attn_total = term if attn_total is None else attn_total + term
            term = dot_nn(projected_grad, normed_refs[group][...])
            total = term if total is None else total + term
            start += size
        total, attn_total = total.astype(BF), attn_total.astype(BF)
        for value in (0, 1):

            @pl.when(coords[CORE] == value)
            def _():
                for side in (0, 1):
                    lanes = slice(side * half, (side + 1) * half)
                    at = side * block + place * rows
                    attn_at = 2 * block + (side * len(heads) + place) * attn
                    for target, mine in ((keep_ref, value), (send_ref, 1 - value)):
                        target[at : at + rows, :] = total[mine * rows : (mine + 1) * rows, lanes]
                        target[attn_at : attn_at + attn, :] = attn_total[
                            mine * attn : (mine + 1) * attn, lanes
                        ]

    turned = jnp.transpose(
        jnp.concatenate([jnp.broadcast_to(gain, (HD, 128)) for gain in gains], axis=0)
    )
    line = lax.broadcasted_iota(jnp.int32, (EXTRA, half), 0)
    gain_row = jnp.concatenate([turned[:1], jnp.zeros((1, half - 2 * HD), F32)], axis=1)
    for pack in (0, 1):
        extra = jnp.where(line == 5, gain_row, 0.0)
        if heads[0] == 0:
            extra = jnp.where(line == 0, b_out_ref[:, pack * half : (pack + 1) * half], extra)
            here = line == 1 + 2 * coords[TOP] + coords[CORE]
            extra = jnp.where(here, b_in_ref[:, pack * half : (pack + 1) * half], extra)
        for target in (keep_ref, send_ref):
            target[(pack + 1) * block - EXTRA : (pack + 1) * block, :] = extra.astype(BF)


def post(heads, coords, parts, raw_groups, normed_groups, dy_slots, q_gain, k_gain, gb_in, gb_out, before=()):
    groups = [raw.shape[2] for raw in raw_groups]
    width = normed_groups[0].shape[1]
    rows = sum(groups)
    slots = len(dy_slots)
    tokens = rows // slots
    count = len(heads)
    terms = len(parts[0][2])
    piece = (count * 4 * HD + (before[0].shape[0] if before else 0), tokens)
    share = (2 * (count * 3 * HD // 2 + EXTRA) + count * HD, width // 2)
    inputs, specs = [], []
    for head, (dq, out, added) in zip(heads, parts, strict=True):
        inputs += [dq, out, *added, *raw_groups]
        specs += [whole((HD, rows))] * 2 + [whole((1, 2 * HD, rows))] * terms
        specs += [
            pl.BlockSpec((1, 2 * HD, size), functools.partial(lambda h, i, c: (h, 0, 0), head))
            for size in groups
        ]
    return call(
        functools.partial(post_kernel, groups, slots, terms, heads, len(before)),
        coords,
        [*inputs, *normed_groups, *dy_slots, q_gain, k_gain, gb_in, gb_out, *before],
        specs
        + [whole((size, width)) for size in groups]
        + [whole((tokens, width))] * slots
        + [whole((1, HD))] * 2
        + [whole((1, width))] * 2
        + [whole(array.shape) for array in before],
        [struct(piece, BF)] * slots + [struct(share, BF)] * 2,
        [whole(piece)] * slots + [whole(share)] * 2,
        name="post" + "".join(map(str, heads)),
    )


def head_of(coords, slot_shift, head):
    z_index = coords[Z_LOW] + 2 * coords[Z_HIGH]
    return lax.rem(z_index + slot_shift, Z_COUNT) * PER_Z + head


def piece_of(pieces, slot, head, part):
    start = (head * 4 + part) * HD
    return pieces[slot][start : start + HD, :]


def tokens_kernel(shifts, coords, *refs):
    pieces, refs = refs[:Z_COUNT], refs[Z_COUNT:]
    (x_ref, dy_ref, gain_ref, near_ref, far_ref, back_ref, b_ref, w_attn_ref, w_ref,
     out_ref, grad_ref, att_s, grad_s) = refs
    width = x_ref.shape[1]
    for head in range(PER_Z):
        for slot, shift in enumerate(shifts):
            row = pl.multiple_of(head_of(coords, shift, head) * HD, HD)
            att_s[pl.ds(row, HD), :] = piece_of(pieces, slot, head, 3)
            for part in range(3):
                grad_s[pl.ds(part * width + row, HD), :] = piece_of(pieces, slot, head, part)
    x = x_ref[...].astype(F32)
    mlp_out, mlp_grad = (
        near_ref[which] + far_ref[which].astype(F32) + back_ref[which].astype(F32) for which in (0, 1)
    )
    out_ref[...] = (
        x + mlp_out + b_ref[...] + dot_nn(jnp.transpose(att_s[...]), w_attn_ref[...])
    ).astype(BF)
    normed_grad = mlp_grad + dot_nt(jnp.transpose(grad_s[...]), w_ref[...])
    hat, scale = normalized(x, 1)
    grad = normed_grad * gain_ref[...]
    grad_ref[...] = dy_ref[...].astype(F32) + scale * (
        grad
        - jnp.mean(grad, axis=1, keepdims=True)
        - hat * jnp.mean(grad * hat, axis=1, keepdims=True)
    )


def token_results(coords, shifts, pieces, x, dy, ln_gain, near, far, back, b_out, w_attn_out, w_qkv):
    rows, width = x.shape
    inputs = [*pieces, x, dy, ln_gain, near, far, back, b_out, w_attn_out, w_qkv]
    return call(
        functools.partial(tokens_kernel, shifts),
        coords,
        inputs,
        [whole(array.shape) for array in inputs],
        [struct((rows, width), BF), struct((rows, width), F32)],
        [whole((rows, width))] * 2,
        [pltpu.VMEM((width, rows), BF), pltpu.VMEM((3 * width, rows), BF)],
        name="token_results",
    )


HALVE, BOTH, KEEP = range(3)


def stage_kernel(segments, bit, coords, keep_ref, came_ref, *out_refs):
    keep_at = came_at = kept = sent = 0
    for rows, came, mode in segments:
        total = keep_ref[keep_at : keep_at + rows, :]
        if came:
            total = (total.astype(F32) + came_ref[came_at : came_at + rows, :].astype(F32)).astype(BF)
            came_at += rows
        keep_at += rows
        if mode == HALVE:
            half = rows // 2
            for value in (0, 1):

                @pl.when(coords[bit] == value)
                def _():
                    out_refs[0][kept : kept + half, :] = total[value * half : (value + 1) * half]
                    out_refs[1][sent : sent + half, :] = total[(1 - value) * half : (2 - value) * half]

            kept += half
            sent += half
        else:
            out_refs[0][kept : kept + rows, :] = total
            kept += rows
            if mode == BOTH:
                out_refs[1][sent : sent + rows, :] = total
                sent += rows


def stage(coords, segments, bit, keep, came):
    width = keep.shape[1]
    kept = sum(rows // 2 if mode == HALVE else rows for rows, _came, mode in segments)
    sent = sum({HALVE: rows // 2, BOTH: rows, KEEP: 0}[mode] for rows, _came, mode in segments)
    shapes = [(kept, width)] + ([(sent, width)] if sent else [])
    return call(
        functools.partial(stage_kernel, segments, bit),
        coords,
        [keep, came],
        [whole(keep.shape), whole(came.shape)],
        [struct(shape, BF) for shape in shapes],
        [whole(shape) for shape in shapes],
        name="stage",
    )


def first_stage_kernel(counts, coords, *refs):
    (*shares, keep_ref, send_ref) = refs
    attn, rows = HD // 2, 3 * HD // 2
    blocks = [count * rows + EXTRA for count in counts]
    pairs = list(zip(blocks, counts, shares[::2], shares[1::2], strict=True))
    for value in (0, 1):

        @pl.when(coords[GRP] == value)
        def _():
            for pack, target in ((value, keep_ref), (1 - value, send_ref)):
                extra, at = 0.0, 0
                for block, count, own, came in pairs:
                    span = slice(pack * block, (pack + 1) * block)
                    total = own[span, :].astype(F32) + came[span, :].astype(F32)
                    target[at : at + count * rows, :] = total[: count * rows].astype(BF)
                    extra = extra + total[count * rows :]
                    at += count * rows
                target[PER_Z * (rows + 2 * attn) :, :] = extra.astype(BF)

    before = 0
    for block, count, own, came in pairs:
        total = (own[2 * block :, :].astype(F32) + came[2 * block :, :].astype(F32)).astype(BF)
        for side in (0, 1):
            start = PER_Z * rows + (side * PER_Z + before) * attn
            for target in (keep_ref, send_ref):
                target[start : start + count * attn, :] = total[
                    side * count * attn : (side + 1) * count * attn
                ]
        before += count


def first_stage(coords, counts, shares):
    half = shares[0].shape[1]
    shape = (PER_Z * (3 * HD // 2 + HD) + EXTRA, half)
    return call(
        functools.partial(first_stage_kernel, counts),
        coords,
        shares,
        [whole(share.shape) for share in shares],
        [struct(shape, BF)] * 2,
        [whole(shape)] * 2,
        name="first_stage",
    )


def mlp_place_kernel(coords, *refs):
    units, (w_ref, rows_ref, columns_ref, sum_ref, turn_s) = refs[:8], refs[8:]
    step = pl.program_id(0)
    part, half = units[0].shape[1] // 2, units[0].shape[2] // 2
    low, high = coords[Z_LOW], coords[Z_HIGH]

    @pl.when(step == 0)
    def _():
        sum_ref[...] = jnp.zeros_like(sum_ref)

    chosen = (step % 2 ^ coords[CORE]) * 4 + (step // 2 ^ coords[TOP]) * 2 + low
    for i in range(8):

        @pl.when(chosen == i)
        def _():
            for shard in range(Z_COUNT):
                rows_ref[shard * part : (shard + 1) * part, :] = units[i ^ (shard // 2)][
                    shard % 2 ^ high, :part, :
                ].astype(F32)

    lanes = pl.ds(pl.multiple_of((step // 2) * half, 128), half)
    chosen = coords[CORE] * 4 + (step % 2 ^ coords[TOP]) * 2 + low
    for i in range(8):

        @pl.when(chosen == i)
        def _():
            for core in (0, 1):
                for shard in range(Z_COUNT):
                    row = (core * Z_COUNT + shard) * part
                    unit = units[i ^ (4 * core) ^ (shard // 2)]
                    turn_s[row : row + part, :] = unit[shard % 2 ^ high, part:, lanes].astype(F32)

    total = 0.0
    for block in range(SHARDS * part // 128):
        span = slice(block * 128, (block + 1) * 128)
        turned = jnp.transpose(turn_s[span, :])
        columns_ref[:, span] = turned
        total = total + turned * w_ref[:, span].astype(F32)
    sum_ref[...] += jnp.sum(total, axis=1, keepdims=True)


def place_mlp(coords, units, w_in):
    _shards, rows, width = units[0].shape
    part, half = rows // 2, width // 2
    span = SHARDS * part
    return call(
        mlp_place_kernel,
        coords,
        [*units, w_in],
        [whole(unit.shape) for unit in units]
        + [pl.BlockSpec((half, span), lambda s, c: (c[GRP], s))],
        [
            struct((2 * span, width), F32),
            struct((half, 4 * span), F32),
            struct((half, 1), F32),
        ],
        [
            pl.BlockSpec((Z_COUNT * part, width), lambda s, c: (s, 0)),
            pl.BlockSpec((half, span), lambda s, c: (0, s)),
            whole((half, 1)),
        ],
        [pltpu.VMEM((span, half), F32)],
        grid=(4,),
        name="place_mlp",
    )


def heads_kernel(coords, *refs):
    (*unit_refs, w_ref, gain_ref, sum_ref, qkv_ref, attn_ref, ln_ref, turn_s) = refs
    half = unit_refs[0].shape[2]
    width = 2 * half
    q_rows, a_rows, unit = 3 * PER_Z * HD // 4, PER_Z * HD // 2, 16
    per_head = 3 * HD // 2 // unit
    for relative in range(8):
        block = unit_refs[relative // 2][relative % 2]
        core = coords[CORE] ^ (relative // 4)
        top = coords[TOP] ^ (relative // 2 % 2)
        low = coords[Z_LOW] ^ (relative % 2)
        for side in (0, 1):
            z_index = low + 2 * (coords[Z_HIGH] ^ side)
            for i in range(q_rows // unit):
                number = top * (q_rows // unit) + i
                inner = number % per_head + core * per_head
                row = (inner // (HD // unit)) * width + (inner % (HD // unit)) * unit
                row = row + (z_index * PER_Z + number // per_head) * HD
                turn_s[pl.ds(pl.multiple_of(row, unit), unit), :] = block[
                    side * q_rows + i * unit : side * q_rows + (i + 1) * unit
                ]
        lanes = pl.ds(pl.multiple_of(top * half, 128), half)
        for head in range(PER_Z):
            row = pl.multiple_of((low * PER_Z + head) * HD + core * (HD // 2), HD // 2)
            start = 2 * q_rows + head * (HD // 2)
            attn_ref[pl.ds(row, HD // 2), lanes] = block[start : start + HD // 2].astype(F32)
    total = 0.0
    for block in range(3 * width // 128):
        span = slice(block * 128, (block + 1) * 128)
        turned = jnp.transpose(turn_s[span, :]).astype(F32)
        qkv_ref[:, span] = turned
        total = total + turned * w_ref[:, span].astype(F32)
    ln = (jnp.sum(total, axis=1, keepdims=True) + sum_ref[...]) / gain_ref[...]
    ln_ref[...] = jnp.transpose(jnp.broadcast_to(ln, (half, 128)))[0]


def place_heads(coords, units, w_qkv, gain_column, in_sums):
    half = units[0].shape[2]
    width = 2 * half
    row_half = lambda columns: pl.BlockSpec((half, columns), lambda s, c: (c[GRP], 0))
    return call(
        heads_kernel,
        coords,
        [*units, w_qkv, gain_column, in_sums],
        [whole(unit.shape) for unit in units] + [row_half(3 * width), row_half(1), whole((half, 1))],
        [struct((half, 3 * width), F32), struct((half, width), F32), struct((half,), F32)],
        [whole((half, 3 * width)), whole((half, width)), whole((half,))],
        [pltpu.VMEM((3 * width, half), BF)],
        name="place_heads",
    )


def per_device(
    tokens, lengths, image_ids, ln_gain, w_qkv, q_gain, k_gain,
    w_attn_out, w_in, b_in, w_mlp_out, b_out, cotangent,
):
    x, dy = tokens[0], cotangent[0]
    rows, width = x.shape
    half = width // 2
    hidden = w_in.shape[1]
    seq_count = lax.axis_size("seq")
    rest = seq_count // Z_COUNT
    rest_bits = rest.bit_length() - 1
    top_bit = rest_bits - 1
    me = lax.axis_index("seq")
    z_index, r_index = me // rest, me % rest
    grp = lax.axis_index("grp")
    core, top = r_index & 1, r_index >> top_bit
    coords = jnp.stack([grp, core, top, z_index & 1, z_index >> 1]).astype(jnp.int32)

    def z_shift(block, distance):
        route = [(i, (i + distance * rest) % seq_count) for i in range(seq_count)]
        return lax.ppermute(block, "seq", route)

    def flip(mask):
        route = [(i, i ^ mask) for i in range(seq_count)]
        return lambda block: lax.ppermute(block, "seq", route)

    def swap_packs(block):
        return lax.ppermute(block, "grp", [(0, 1), (1, 0)])

    swap_core, swap_top = flip(1), flip(1 << top_bit)
    swap_low, swap_high = flip(rest), flip(2 * rest)
    others = range(1, top_bit)

    def add(*terms):
        return sum(term.astype(F32) for term in terms).astype(BF)

    def after(value, *events):
        return lax.optimization_barrier((value, *events))[0]

    def after(value, *events):
        return lax.optimization_barrier((value, *events))[0]

    turn = [coords]

    def then(results):
        if isinstance(results, (list, tuple)):
            return [then(results[0]), *results[1:]]
        turn[0], results = lax.optimization_barrier((turn[0], results))
        return results

    def until(*events):
        turn[0] = after(turn[0], *events)

    shifts = [0, 1, 3, 2]
    x_slots = {0: x, **{d: z_shift(x, d) for d in (1, 3, 2)}}
    mine, gb_out, *do_pieces = then(prep(coords, shifts, x, dy, w_attn_out))
    across, other = swap_top(mine), swap_core(mine)
    mlp_weights = (ln_gain.reshape(1, width), w_in, b_in.reshape(1, hidden), w_mlp_out)
    near, near_far, *before = then(mlp(turn[0], [mine, other], *mlp_weights))
    near_far = swap_core(near_far)

    order = image_ids[0]
    labels = jnp.arange(order.shape[0], dtype=jnp.int32)
    ordered = jnp.sum(jnp.where(order[:, None] == labels[None, :], lengths[0][None, :], 0), axis=1)
    ends = jnp.cumsum(ordered)
    offsets = jnp.arange(rows, dtype=jnp.int32)
    slot_z = (z_index - jnp.array(shifts, dtype=jnp.int32)) % Z_COUNT
    masks = [2 * i for i in range(rest // 2)] + [2 * i + 1 for i in range(rest // 2)]
    source_r = r_index ^ jnp.array(masks, dtype=jnp.int32)
    starts = (slot_z[None, :] * rest + source_r[:, None]) * rows
    places = (starts[:, :, None] + offsets).reshape(rest, Z_COUNT * rows)
    images = jnp.sum((places[:, :, None] >= ends).astype(jnp.int32), axis=2).astype(F32)
    key_images = images[:, None, :]
    query_images = images[:1]

    ln_row = ln_gain.reshape(1, width)
    q_col, k_col = q_gain.reshape(1, HD), k_gain.reshape(1, HD)

    until(query_images, key_images)
    normed, q, kv_first, kv_rest, raw = then(
        qkv(turn[0], [x_slots[d] for d in shifts], ln_row, w_qkv, q_col, k_col)
    )
    normed_groups, q_groups, raw_groups = [normed], [q], [raw]

    def spread(group, bits):
        for bit in bits:
            group = {**group, **{m | 1 << bit: flip(1 << bit)(block) for m, block in group.items()}}
        return group

    upper = list(reversed(range(1, rest_bits)))
    do_slots = [
        z_shift(after(piece, normed), d) if d else piece
        for piece, d in zip(do_pieces, shifts, strict=True)
    ]
    kv_first = spread({0: kv_first}, upper)
    mid, far, mlp_keep, mlp_send, gb_in = then(
        mlp(turn[0], [across, swap_core(after(across, near))], *mlp_weights, before)
    )
    mlp_came = swap_packs(mlp_send)
    kv_first = {m: after(block, mlp_keep, *do_slots[1:]) for m, block in kv_first.items()}
    kv_here = after(kv_rest, kv_first[1 << top_bit])
    kv_first = spread(kv_first, [0])
    kv_rest = spread({0: kv_here}, upper)
    dy_slots = {0: dy, **{d: z_shift(after(dy, kv_first[1]), d) for d in (1, 3)}}

    shares = []

    def finish(heads, parts, before=()):
        results = then(
            post(
                heads, turn[0], parts, raw_groups, normed_groups, dy_list, q_col, k_col, gb_in, gb_out, before
            )
        )
        shares.extend([results[Z_COUNT], swap_core(results[Z_COUNT + 1])])
        return results[:Z_COUNT]

    waiting = []

    def halve(keep, came, bit, move):
        size = keep.shape[0] // 2
        rows_of = lambda array, which: lax.dynamic_slice_in_dim(array, which * size, size, 0)
        gone = then(add(rows_of(keep, 1 - bit), rows_of(came, 1 - bit)))
        keep = then(add(rows_of(keep, bit), rows_of(came, bit)))
        return keep, move(gone)

    far = swap_core(far)
    back_sum = add(mid, far)
    kv_sources = [[(kv_first[m], 0) for m in masks]]
    for head in range(PER_Z):
        out_t, dq_t, low, high = then(
            attention(head, turn[0], q_groups, do_slots, kv_sources[head], query_images, key_images)
        )
        if head == 0:
            high = after(high, kv_rest[1 << top_bit])
            kv_rest = spread({m: after(block, dq_t) for m, block in kv_rest.items()}, [0])
            kv_sources += [[(kv_rest[m], place) for m in masks] for place in (0, 1)]
            high = after(high, dy_slots[1], dy_slots[3])
            dy_slots[2] = z_shift(after(dy, dq_t), 2)
            back = swap_top(after(back_sum, dq_t))
        elif head > 1:
            high = after(high, *waiting[-1][2][2:])
        if head == 2:
            high = after(high, *waiting[0][2][2:])
        if head:
            high = after(high, mlp_came)
        if head == 1:
            high = after(high, dy_slots[2])
            dy_list = [dy_slots[d] for d in shifts]
            high = after(high, back)
        came = swap_core(high)

        def mlp_step():
            if head < 2:
                bit, move = ((z_index & 1, swap_low), (z_index >> 1, swap_high))[head]
                return halve(after(mlp_keep, turn[0]), mlp_came, bit, move)
            share = then(add(after(mlp_keep, turn[0]), mlp_came))
            for bit in others:
                share = add(share, flip(1 << bit)(share))
            return share[None], swap_high(share[None])

        if head:
            mlp_keep, mlp_came = mlp_step()
        parts = {2 * i: [low[i : i + 1], came[i : i + 1]] for i in range(rest // 2)}
        for bit in range(1, rest_bits):
            for mask in sorted(m for m in parts if m >> bit & 1):
                total = then(add(*parts.pop(mask)))
                parts[mask ^ (1 << bit)].append(flip(1 << bit)(total))
        if not head:
            mlp_keep, mlp_came = mlp_step()
        waiting.append((dq_t, out_t, [low, came, *parts[0][2:]]))
    some = finish([0, 1], waiting[:2])
    late = finish([2], waiting[2:], some)
    units_here = then(jnp.concatenate([after(mlp_keep, turn[0]), mlp_came], axis=0))
    units_low, units_top = swap_low(units_here), swap_top(units_here)
    send_piece = lambda slot, *events: z_shift(after(late[slot], *events), -shifts[slot])
    pieces = [late[0], None, None, z_shift(late[3], -shifts[3])]

    keep, send = then(first_stage(turn[0], [2, 1], shares))
    q_size, a_size = 3 * PER_Z * HD // 2, PER_Z * HD
    came = swap_packs(send)
    units_both = swap_top(after(units_low, keep))
    until(units_low, units_top)
    until(pieces[3])
    keep, send = then(
        stage(
            turn[0],
            [(q_size, True, HALVE), (a_size, True, HALVE), (EXTRA, True, BOTH)],
            TOP, keep, came,
        )
    )
    q_size, a_size = q_size // 2, a_size // 2
    came = swap_top(send)
    pieces[1] = send_piece(1, keep)
    came = after(came, pieces[1])
    share = then(add(keep, came))
    for bit in others:
        share = add(share, flip(1 << bit)(share))
    came = swap_high(share)
    pieces[2] = send_piece(2, came)
    near_parts = (near, near_far, back)
    mlp_units = [units_here, units_low, units_top, units_both]
    mlp_units += [swap_core(after(unit, share)) for unit in mlp_units]
    middle = q_size + a_size
    attn = jnp.where(z_index >> 1 == grp, share[q_size:middle], came[q_size:middle])
    small = add(share[middle:], came[middle:])
    unit = then(jnp.concatenate([share[:q_size], came[:q_size], attn, small], axis=0))
    came = swap_low(unit)
    grad_w_mlp_out, grad_w_in, in_sums = then(place_mlp(turn[0], mlp_units, w_in))
    came = after(came, grad_w_in)
    size = unit.shape[0] - EXTRA
    small = add(unit[size:], came[size:]).astype(F32)
    units = then(jnp.stack([unit[:size], came[:size]]))
    came = swap_top(units)
    result, grad_tokens = then(
        token_results(
            turn[0], shifts, pieces, x, dy, ln_row, *near_parts, b_out.reshape(1, width), w_attn_out, w_qkv
        )
    )
    came = after(came, result)
    all_units = [units, came, swap_core(units), swap_core(came)]

    grad_w_qkv, grad_w_attn_out, grad_ln_gain = place_heads(
        coords, all_units, w_qkv, ln_gain.reshape(width, 1), in_sums
    )
    return (
        result[None],
        grad_tokens[None],
        grad_ln_gain,
        grad_w_qkv,
        lax.dynamic_slice(small[5], (grp * (HD // 2),), (HD // 2,)),
        lax.dynamic_slice(small[5], (HD + grp * (HD // 2),), (HD // 2,)),
        grad_w_attn_out,
        grad_w_in,
        small[1:5].reshape(hidden // 2),
        grad_w_mlp_out,
        small[0],
    )


def solution(mesh):
    placed = (
        P("grp", "seq", None), P("grp", None), P("grp", None),
        P(), P(), P(), P(), P(), P(), P(), P(), P(), P("grp", "seq", None),
    )
    return jax.shard_map(
        per_device,
        mesh=mesh,
        in_specs=placed,
        out_specs=(
            P("grp", "seq", None), P("grp", "seq", None), P("grp"), P("grp", None), P("grp"),
            P("grp"), P("grp", None), P("grp", None), P("grp"), P("grp", None), P("grp"),
        ),
        check_vma=False,
    )
```
